256 devices in a mesh: dp: 8 (over y, core), ctx: 32 (over z, x).
Axes of the slice: x: 4, y: 4, z: 8, core: 2. Of those that a mesh axis runs over, the one named last changes fastest.
Arguments:
- queries: bfloat16 [32768, 4096], P(('dp', 'ctx')), may hold values from -6.25 to 6.25
- keys: bfloat16 [32768, 512], P(('dp', 'ctx')), may hold values from -6.25 to 6.25
- values: bfloat16 [32768, 512], P(('dp', 'ctx')), may hold values from -6 to 6
- grad_out: bfloat16 [32768, 4096], P(('dp', 'ctx')), may hold values from -6 to 6
- inputs: bfloat16 [32768, 3072], P(('dp', 'ctx')), may hold values from -0.125 to 0.125
- span_map: int32 [8, 64], P('dp'), may hold values from 0 to 63, each once within a row
- doc_lengths: int32 [8, 32], P('dp'), may hold values from 1 to 256, 4096 in all within a row
Outputs:
- query_grads: bfloat16 [32768, 4096], P(('dp', 'ctx'))
- weight_grads: float32 [3072, 1024], P(('dp', 'ctx'))
The draws below stay inside these ranges and needn't reach their ends.
Inputs may be any that keep to these rules, and one draw needn't show every extreme that they name: `span_map`: each row lists every span of its sequence exactly once. `doc_lengths`: each row holds the lengths of consecutive documents that fill its sequence of 4096 tokens exactly, and its longest document has 256 tokens.
All inputs are finite; a program needn't handle non-finite values.
Results may differ from the reference program's by a relative error of at most 0.02.
Values may be sent and summed in bfloat16 or wider, within the bound.
A program may use at most 128 MiB of HBM per device.

```python
import math
import jax
import jax.numpy as jnp
import numpy as np
from jax import lax

H = 32
KVH = 4
HD = 128
DW = 3072
ROT = 64
G = 8
KVC = 512
CH = 64
SEQ = 4096
MOST = 256
NDOC = 32
TOKENS = 32768
N_DP = 8
N_CTX = 32


def draw_queries(key, part):
    key = jax.random.fold_in(key, 21)
    base_draw = jnp.clip(jax.random.normal(key, (TOKENS, H, HD), jnp.float32), -4.0, 4.0)
    return base_draw.reshape(TOKENS, H * HD).astype(jnp.bfloat16)


def draw_keys(key, part):
    key = jax.random.fold_in(key, 37)
    base_draw = jnp.clip(jax.random.normal(key, (TOKENS, KVH, HD), jnp.float32), -4.0, 4.0)
    return base_draw.reshape(TOKENS, KVH * HD).astype(jnp.bfloat16)


def spiked(array, key, source, target, blocks, factor):
    owner, partner = [(jnp.arange(array.shape[dim]) // (array.shape[dim] // blocks)).reshape([-1 if axis == dim else 1 for axis in range(array.ndim)]) for dim in (source, target)]
    chosen = jax.random.permutation(key, blocks)[partner]
    strong = (owner == chosen) | (owner == (partner + blocks // 2) % blocks)
    return jnp.where(strong, factor * array, array)


def steps_of(rng, extent, split, low, high):
    loudness = 1.0
    for axis_at, shards_of in split:
        steps = jax.random.uniform(jax.random.fold_in(jax.random.fold_in(rng, 6), axis_at), (shards_of,), jnp.float32, low / len(split), high / len(split))
        loudness = loudness * jnp.repeat(jnp.exp(steps), extent[axis_at] // shards_of).reshape((-1,) + (1,) * (len(extent) - 1 - axis_at))
    return loudness


def profile(amount, total, reach, skew):
    portions = [(1 << 20) // math.isqrt(grade ** skew) + 1 for grade in range(2, amount + 1)]
    rest, holding = total - reach - (amount - 1), [1] * (amount - 1)
    while rest > 0:
        movable = [i for i in range(amount - 1) if holding[i] < reach]
        pool, budget = sum([portions[i] for i in movable]), rest
        for i in movable:
            addition = min(reach - holding[i], max(1, budget * portions[i] // pool), rest)
            holding[i] = holding[i] + addition
            rest = rest - addition
    return np.array([reach] + holding)


def ragged_sizes(own_key, count, total, bound, slope):
    if count == 2:
        one = jax.random.randint(own_key, (), max(1, total - bound), min(bound, total - 1) + 1)
        return jnp.stack([one, total - one])
    tallies = jnp.asarray(profile(count, total, bound, slope), jnp.int32)
    couples = (count - 1) // 2
    giver, receiver = tallies[1:1 + 2 * couples:2], tallies[2:2 + 2 * couples:2]
    margin = jnp.minimum(giver - 1, bound - receiver)
    shifted = jax.random.randint(jax.random.fold_in(own_key, 1), (couples,), 0, 1 << 20) % (margin + 1)
    tallies = tallies.at[1:1 + 2 * couples:2].set(giver - shifted).at[2:2 + 2 * couples:2].set(receiver + shifted)
    return tallies[jax.random.permutation(jax.random.fold_in(own_key, 2), count)]


def bell_draw(own_key, extent, scale, most, shards=(), kind=jnp.bfloat16):
    array = jax.random.normal(own_key, extent, jnp.float32) * scale
    if len(shards) > 0:
        array = steps_of(own_key, extent, shards, -0.22, 0.18) * array
    return jnp.clip(array, min=-most, max=most).astype(kind)


def noise_with(stream_key, extent, spread, most, split, heavy, kind=jnp.bfloat16):
    values = spread * jax.random.normal(stream_key, extent, jnp.float32)
    if split:
        values = values * steps_of(stream_key, extent, split, -0.22, 0.18)
    return jnp.clip(spiked(values, jax.random.fold_in(stream_key, 3), *heavy), -most, most).astype(kind)


def setup_inputs(seed: int = 0) -> dict:
    key_list = jax.random.split(jax.random.key(seed), 8)
    queries = draw_queries(jax.random.fold_in(key_list[7], 71), 0)
    keys = draw_keys(jax.random.fold_in(key_list[7], 71), 0)
    values = bell_draw(key_list[2], (TOKENS, KVC), 1.0, 6.0, ((0, 256),))
    grad_out = bell_draw(key_list[3], (TOKENS, H * HD), 1.0, 6.0, ((0, 256),))
    inputs = noise_with(key_list[4], (TOKENS, DW), TOKENS ** -0.5, 0.125, ((0, 256),), (0, 1, 256, 6.0))
    span_map = jax.vmap(lambda own: jax.random.permutation(own, 2 * N_CTX))(jax.random.split(key_list[5], N_DP)).reshape((N_DP, 2 * N_CTX)).astype(jnp.int32)
    doc_lengths = jax.vmap(lambda own: ragged_sizes(own, NDOC, SEQ, MOST, 2))(jax.random.split(key_list[6], N_DP)).reshape((N_DP, NDOC)).astype(jnp.int32)
    return dict(queries=queries, keys=keys, values=values, grad_out=grad_out, inputs=inputs, span_map=span_map, doc_lengths=doc_lengths)


ROPE_BASE = 10000000.0


def doc_begin(positions, lengths):
    doc_ends = jnp.cumsum(lengths).astype(jnp.int32)
    starts = doc_ends - lengths.astype(jnp.int32)
    picked = jnp.where(starts[None, :] <= positions[:, None], starts[None, :], 0)
    return jnp.max(picked, axis=1).astype(jnp.int32)


def rotary(vectors, relative, direction_sign):
    half_rot = ROT // 2
    frequency = ROPE_BASE ** (-(jnp.arange(half_rot, dtype=jnp.float32) * 2.0 / ROT))
    angles = relative.astype(jnp.float32)[:, None] * frequency[None, :]
    cosine = jnp.cos(angles)[:, None, :]
    sine_part = direction_sign * jnp.sin(angles)[:, None, :]
    first_half = vectors[..., :half_rot]
    second = vectors[..., half_rot:ROT]
    return jnp.concatenate([first_half * cosine - second * sine_part, second * cosine + first_half * sine_part, vectors[..., ROT:]], axis=-1)


def slot_window(query_rot, dout, key_seq, value_seq, span_id, query_begin):
    scaling = HD ** -0.5
    width = MOST + CH
    seq_len = key_seq.shape[0]
    anchor = jnp.clip(span_id * CH - MOST, 0, seq_len - width).astype(jnp.int32)
    key_window = lax.dynamic_slice_in_dim(key_seq, anchor, width, 0).astype(jnp.float32)
    value_window = lax.dynamic_slice_in_dim(value_seq, anchor, width, 0).astype(jnp.float32)
    key_pos = anchor + jnp.arange(width, dtype=jnp.int32)
    query_pos = span_id * CH + jnp.arange(CH, dtype=jnp.int32)
    allowed = (key_pos[None, :] <= query_pos[:, None]) & (key_pos[None, :] >= query_begin[:, None])
    mask_full = allowed[None, None, :, :]
    query_four = query_rot.astype(jnp.float32)
    dout_four = dout.astype(jnp.float32)
    scores = jnp.einsum("qjgd,kjd->jgqk", query_four, key_window) * scaling
    log_total = jax.nn.logsumexp(jnp.where(mask_full, scores, -jnp.inf), axis=-1, keepdims=True)
    probability = jnp.where(mask_full, jnp.exp(scores - log_total), 0.0)
    dprobs = jnp.einsum("qjgd,kjd->jgqk", dout_four, value_window)
    delta_row = jnp.sum(probability * dprobs, axis=-1, keepdims=True)
    dscores = lax.optimization_barrier((probability * (dprobs - delta_row)).astype(jnp.bfloat16)).astype(jnp.float32)
    probs_low = lax.optimization_barrier(probability.astype(jnp.bfloat16)).astype(jnp.float32)
    query_part = jnp.einsum("jgqk,kjd->qjgd", dscores, key_window) * scaling
    key_part = jnp.einsum("jgqk,qjgd->kjd", dscores, query_four) * scaling
    value_part = jnp.einsum("jgqk,qjgd->kjd", probs_low, dout_four)
    both = jnp.concatenate([key_part.reshape(width, KVC), value_part.reshape(width, KVC)], axis=1)
    return query_part.reshape(CH, H * HD), both, anchor


def reference(queries, keys, values, grad_out, inputs, span_map, doc_lengths):
    seq_len = CH * 2 * N_CTX
    slot_count = 2 * N_CTX
    width = MOST + CH
    query_list = []
    weight_total = jnp.zeros((DW, 2 * KVC), jnp.float32)
    for member in range(N_DP):
        first_row = member * seq_len
        query_rows = queries[first_row:first_row + seq_len]
        key_rows = keys[first_row:first_row + seq_len]
        value_rows = values[first_row:first_row + seq_len]
        dout_rows = grad_out[first_row:first_row + seq_len]
        input_rows = inputs[first_row:first_row + seq_len]
        span_order = span_map[member].astype(jnp.int32)
        lengths = doc_lengths[member].astype(jnp.int32)
        row_ids = jnp.arange(seq_len, dtype=jnp.int32)
        positions = (span_order[row_ids // CH] * CH + row_ids % CH).astype(jnp.int32)
        begins = doc_begin(positions, lengths)
        relative = positions - begins
        query_rot = lax.optimization_barrier(rotary(query_rows.reshape(seq_len, H, HD).astype(jnp.float32), relative, 1.0).astype(jnp.bfloat16))
        key_rot = lax.optimization_barrier(rotary(key_rows.reshape(seq_len, KVH, HD).astype(jnp.float32), relative, 1.0).astype(jnp.bfloat16))
        slot_of = jnp.zeros((slot_count,), jnp.int32).at[span_order].set(jnp.arange(slot_count, dtype=jnp.int32))
        source_rows = (slot_of[row_ids // CH] * CH + row_ids % CH).astype(jnp.int32)
        key_seq = key_rot[source_rows]
        value_seq = value_rows.reshape(seq_len, KVH, HD)[source_rows]
        query_slots = query_rot.reshape(N_CTX, 2, CH, KVH, G, HD)
        dout_slots = dout_rows.reshape(N_CTX, 2, CH, KVH, G, HD)
        span_slots = span_order.reshape(N_CTX, 2)
        begin_slots = begins.reshape(N_CTX, 2, CH)

        def device_step(total, packed):
            query_pair, dout_pair, span_pair, begin_pair = packed
            partial_value = jnp.zeros((seq_len, 2 * KVC), jnp.float32)
            query_parts = []
            for side in range(2):
                query_part, both, anchor = slot_window(query_pair[side], dout_pair[side], key_seq, value_seq, span_pair[side], begin_pair[side])
                zero_index = jnp.zeros((), jnp.int32)
                current = lax.dynamic_slice(partial_value, (anchor, zero_index), (width, 2 * KVC))
                partial_value = lax.dynamic_update_slice(partial_value, current + both, (anchor, zero_index))
                query_parts.append(query_part)
            rounded = lax.optimization_barrier(partial_value.astype(jnp.bfloat16)).astype(jnp.float32)
            return total + rounded, jnp.stack(query_parts)

        start_total = jnp.zeros((seq_len, 2 * KVC), jnp.float32)
        key_total, query_stack = lax.scan(device_step, start_total, (query_slots, dout_slots, span_slots, begin_slots))
        key_grads = key_total[positions]
        grad_key = rotary(key_grads[:, :KVC].reshape(seq_len, KVH, HD), relative, -1.0).reshape(seq_len, KVC)
        grads_low = jnp.concatenate([grad_key, key_grads[:, KVC:]], axis=1).astype(jnp.bfloat16)
        weight_total = weight_total + jnp.dot(input_rows.T, grads_low, preferred_element_type=jnp.float32)
        grad_query = rotary(query_stack.reshape(seq_len, H, HD), relative, -1.0)
        query_list.append(grad_query.reshape(seq_len, H * HD).astype(jnp.bfloat16))
    return jnp.concatenate(query_list, axis=0), weight_total
```

```python
import functools

import jax
import jax.numpy as jnp
import numpy as np
from jax import lax
from jax.experimental import pallas as pl
from jax.experimental.pallas import tpu as pltpu
from jax.sharding import PartitionSpec as P

MESH = pl.DeviceIdType.MESH
BF16 = jnp.bfloat16
F32 = jnp.float32

KVH = 4
G = 8
HD = 128
ROT = 64
ROPE_BASE = 10000000.0
SPAN = 64
BACK = 4
ROWS = 2 * SPAN
N_CTX = 32
N_DP = 8
N_X = 4
N_Z = 8
SLOTS = 2 * N_CTX
NDOC = 32
KVC = KVH * HD
PIECE = 16
REACH = 2 * BACK
W_DP = 384
W_DEV = W_DP // N_CTX
W_X = W_DP // N_X
MASKED = -1e30
VMEM_LIMIT = 48 * 1024 * 1024

NT = (((1,), (1,)), ((), ()))
TN = (((0,), (0,)), ((), ()))


def rope_lanes():
    half = ROT // 2
    freq = ROPE_BASE ** (-(np.arange(half, dtype=np.float64) * 2.0 / ROT))
    row = np.zeros((1, HD), np.float32)
    row[0, :half] = freq
    row[0, half:ROT] = freq
    return row


def feature_order():
    order = np.arange(W_DP).reshape(N_Z, N_X, W_DEV).transpose(1, 0, 2).reshape(-1)
    return np.eye(W_DP, dtype=np.float32)[order]


def swap_halves(x):
    lane = lax.broadcasted_iota(jnp.int32, x.shape, 1)
    return jnp.where(lane < ROT // 2, pltpu.roll(x, HD - ROT // 2, 1), pltpu.roll(x, ROT // 2, 1))


def begin_of(pos, len_ref):
    def step(d, carry):
        start, begin = carry
        return start + len_ref[0, d], jnp.where(pos >= start, start, begin)

    _, begin = lax.fori_loop(0, NDOC, step, (jnp.int32(0), jnp.zeros_like(pos)), unroll=True)
    return begin


def prep_kernel(span_ref, len_ref, freq_ref, key_ref, val_ref, pack_ref, cos_ref, sin_ref, slot_ref):
    me = lax.axis_index("ctx")

    def place(slot, carry):
        slot_ref[0, span_ref[0, slot]] = slot
        return carry

    lax.fori_loop(0, SLOTS, place, 0, unroll=8)
    row = lax.broadcasted_iota(jnp.int32, (ROWS, HD), 0)
    lane = lax.broadcasted_iota(jnp.int32, (ROWS, HD), 1)
    second = row >= SPAN
    span = jnp.where(second, span_ref[0, 2 * me + 1], span_ref[0, 2 * me])
    pos = span * SPAN + jnp.where(second, row - SPAN, row)
    rel = (pos - begin_of(pos, len_ref)).astype(F32)
    angle = rel * freq_ref[...]
    sine = jnp.sin(angle)
    cos = jnp.where(lane < ROT, jnp.cos(angle), 1.0)
    sin = jnp.where(lane < ROT // 2, -sine, jnp.where(lane < ROT, sine, 0.0))
    cos_ref[...] = cos
    sin_ref[...] = sin
    for j in range(KVH):
        k = key_ref[:, j * HD : (j + 1) * HD].astype(F32)
        k = (k * cos + swap_halves(k) * sin).astype(BF16)
        v = val_ref[:, j * HD : (j + 1) * HD]
        for s in range(2):
            for r in range(SPAN // PIECE):
                at = s * SPAN + r * PIECE
                pack_ref[r * KVH + j, s] = k[at : at + PIECE]
                pack_ref[16 + r * KVH + j, s] = v[at : at + PIECE]


def greet(peers):
    barrier = pltpu.get_barrier_semaphore()
    count = 0
    for first, last, device in peers:

        def hello(k, carry, device=device):
            pl.semaphore_signal(barrier, inc=1, device_id=device(k), device_id_type=MESH)
            return carry

        lax.fori_loop(first, last, hello, 0)
        count += last - first
    pl.semaphore_wait(barrier, count)


def loop(first, last, body):
    def step(k, carry):
        body(k)
        return carry

    lax.fori_loop(first, last, step, 0)


def remote(src, dst, send, recv, device):
    return pltpu.make_async_remote_copy(
        src_ref=src, dst_ref=dst, send_sem=send, recv_sem=recv, device_id=device, device_id_type=MESH
    )


def gather_kernel(
    span_ref, slot_ref, pack_ref, inputs_ref, win_ref, x_ref,
    held, chosen, take, send1, recv1, send2, recv2, send3, recv3, own_sem,
):
    dp, me = lax.axis_index("dp"), lax.axis_index("ctx")
    ctx_peer = lambda k: lax.rem(me + k, N_CTX)
    dp_peer = lambda k: lax.rem(dp + k, N_DP)
    greet([(1, N_CTX, lambda k: (dp, ctx_peer(k))), (1, N_DP, lambda k: (dp_peer(k), me))])

    def first_copy(src, owner, peer):
        return remote(
            pack_ref.at[src], held.at[pl.ds(2 * owner, 2)], send1.at[src], recv1.at[owner], (dp, peer)
        )

    def input_copy(part, owner, peer):
        cols = pl.ds(pl.multiple_of(part * W_DP, W_DP), W_DP)
        return remote(inputs_ref.at[:, cols], x_ref.at[owner], send3.at[part], recv3.at[owner], (peer, me))

    def second_copy(src, owner, peer):
        return remote(chosen.at[src], win_ref.at[owner], send2.at[src], recv2.at[owner], (dp, peer))

    loop(1, N_CTX, lambda k: first_copy(ctx_peer(k), me, ctx_peer(k)).start())
    loop(1, N_DP, lambda k: input_copy(dp_peer(k), dp, dp_peer(k)).start())
    own_cols = pl.ds(pl.multiple_of(dp * W_DP, W_DP), W_DP)
    own_copy = pltpu.make_async_copy(inputs_ref.at[:, own_cols], x_ref.at[dp], own_sem)
    own_copy.start()
    held[pl.ds(2 * me, 2)] = pack_ref[me]

    def fill(slot):
        span = span_ref[0, slot]
        for w in range(BACK):
            take[slot * BACK + w] = slot_ref[0, jnp.maximum(span - BACK + w, 0)]

    loop(0, SLOTS, fill)
    loop(1, N_CTX, lambda k: first_copy(me, ctx_peer(k), ctx_peer(k)).wait_recv())

    def choose(j):
        for w in range(REACH):
            chosen[j, w] = held[take[j * REACH + w]]

    def serve(k):
        choose(ctx_peer(k))
        second_copy(ctx_peer(k), me, ctx_peer(k)).start()

    loop(1, N_CTX, serve)
    choose(me)
    win_ref[me] = chosen[me]
    loop(1, N_CTX, lambda k: first_copy(ctx_peer(k), me, ctx_peer(k)).wait_send())
    loop(1, N_DP, lambda k: input_copy(dp_peer(k), dp, dp_peer(k)).wait_send())
    own_copy.wait()
    loop(1, N_DP, lambda k: input_copy(dp, dp_peer(k), dp_peer(k)).wait_recv())
    loop(1, N_CTX, lambda k: second_copy(ctx_peer(k), me, ctx_peer(k)).wait_send())
    loop(1, N_CTX, lambda k: second_copy(me, ctx_peer(k), ctx_peer(k)).wait_recv())


def attend_kernel(
    span_ref, len_ref, q_ref, do_ref, win_ref, pack_ref, cos_ref, sin_ref,
    dq_ref, part_ref, own_ref, bias,
):
    me = lax.axis_index("ctx")
    keys_n = (BACK + 1) * SPAN

    @pl.when(pl.program_id(0) == 0)
    def _():
        for s in range(2):
            span = span_ref[0, 2 * me + s]
            lane = lax.broadcasted_iota(jnp.int32, (8, HD), 1)
            qpos = span * SPAN + jnp.where(lane >= SPAN, lane - SPAN, lane)
            qbegin = begin_of(qpos, len_ref)
            k = lax.broadcasted_iota(jnp.int32, (keys_n, HD), 0)
            r, w, t = k >> 6, (k >> 4) & 3, k & 15
            earlier = (span - BACK + w) * SPAN + r * PIECE + t
            kpos = jnp.where(k < BACK * SPAN, earlier, span * SPAN + (k - BACK * SPAN))
            allowed = (kpos <= qpos[0:1]) & (kpos >= qbegin[0:1])
            bias[s] = jnp.where(allowed, 0.0, MASKED)

    scale = HD**-0.5
    for s in range(2):
        rows = slice(s * SPAN, (s + 1) * SPAN)
        cos, sin = cos_ref[rows], sin_ref[rows]

        def window(kind):
            earlier = win_ref[kind, :, 0, s * BACK : (s + 1) * BACK].reshape(BACK * SPAN, HD)
            mine = pack_ref[kind, :, 0, s].reshape(SPAN, HD)
            return jnp.concatenate([earlier, mine], axis=0)

        def rotated(g):
            x = q_ref[rows, g * HD : (g + 1) * HD].astype(F32)
            return (x * cos + swap_halves(x) * sin).astype(BF16)

        k, v = window(0), window(1)
        q = jnp.concatenate([rotated(g) for g in range(G)], axis=0)
        do = jnp.concatenate([do_ref[rows, g * HD : (g + 1) * HD] for g in range(G)], axis=0)
        mask = jnp.concatenate([bias[s]] * (G * SPAN // HD), axis=1)
        scores = lax.dot_general(k, q, NT, preferred_element_type=F32)
        scores = scores * (scale * float(np.log2(np.e))) + mask
        weight = jnp.exp2(scores - jnp.max(scores, axis=0, keepdims=True))
        probs = weight * (1.0 / jnp.sum(weight, axis=0, keepdims=True))
        dprobs = lax.dot_general(v, do, NT, preferred_element_type=F32)
        delta = jnp.sum(probs * dprobs, axis=0, keepdims=True)
        dscores = (probs * (dprobs - delta)).astype(BF16)
        low = probs.astype(BF16)
        dk = jnp.dot(dscores, q, preferred_element_type=F32) * scale
        dv = jnp.dot(low, do, preferred_element_type=F32)
        dq = lax.dot_general(k, dscores, TN, preferred_element_type=F32).T * scale
        for kind, grad in ((0, dk), (1, dv)):
            earlier = grad[: BACK * SPAN].astype(BF16).reshape(SPAN // PIECE, BACK, PIECE, HD)
            part_ref[kind, :, 0, s * BACK : (s + 1) * BACK] = earlier
            own_ref[kind, rows] = grad[BACK * SPAN :]
        for g in range(G):
            x = dq[g * SPAN : (g + 1) * SPAN]
            dq_ref[rows, g * HD : (g + 1) * HD] = (x * cos - swap_halves(x) * sin).astype(BF16)


def reduce_kernel(
    span_ref, slot_ref, part_ref, own_ref, cos_ref, sin_ref, x_ref, perm_ref, out_ref,
    landed, give, total, back, grads, xt, wsend, xland, zsend, zland,
    send1, recv1, send2, recv2, send3, recv3, send4, recv4, send5, recv5, send6, recv6,
):
    dp, me = lax.axis_index("dp"), lax.axis_index("ctx")
    z, x = me // N_X, lax.rem(me, N_X)
    sib = dp + 1 - 2 * lax.rem(dp, 2)
    ctx_peer = lambda k: lax.rem(me + k, N_CTX)
    y_peer = lambda k: lax.rem(dp + 2 * k, N_DP)
    sib_peer = lambda k: lax.rem(sib + 2 * k, N_DP)
    x_peer = lambda k: lax.rem(x + k, N_X)
    z_peer = lambda k: lax.rem(z + k, N_Z)
    greet([
        (1, N_CTX, lambda k: (dp, ctx_peer(k))),
        (1, 4, lambda k: (y_peer(k), me)),
        (0, 1, lambda k: (sib, me)),
    ])

    def first_copy(src, owner, peer):
        return remote(
            part_ref.at[src], landed.at[pl.ds(REACH * owner, REACH)], send1.at[src], recv1.at[owner], (dp, peer)
        )

    def second_copy(src, owner, peer):
        return remote(total.at[src], back.at[owner], send2.at[src], recv2.at[owner], (dp, peer))

    def y_copy(owner, peer):
        return remote(grads.at[owner], grads.at[owner], send3.at[peer], recv3.at[owner], (peer, me))

    def sib_copy(owner):
        return remote(grads.at[owner], grads.at[owner], send4.at[owner], recv4.at[owner], (sib, me))

    def x_copy(src, owner, peer):
        return remote(wsend.at[src], xland.at[owner], send5.at[src], recv5.at[owner], (dp, z * N_X + peer))

    def z_copy(src, owner, peer):
        return remote(zsend.at[src], zland.at[owner], send6.at[src], recv6.at[owner], (dp, peer * N_X + x))

    loop(1, N_CTX, lambda k: first_copy(ctx_peer(k), me, ctx_peer(k)).start())
    landed[pl.ds(REACH * me, REACH)] = part_ref[me]
    landed[N_CTX * REACH] = jnp.zeros((PIECE, HD), BF16)

    def fill(slot):
        span = span_ref[0, slot]
        for w in range(BACK):
            later = span + 1 + w
            source = slot_ref[0, jnp.minimum(later, SLOTS - 1)] * BACK + (BACK - 1 - w)
            give[slot * BACK + w] = jnp.where(later < SLOTS, source, N_CTX * REACH)

    loop(0, SLOTS, fill)
    for d in range(N_DP):
        turned = lax.dot_general(perm_ref[...], x_ref[d], NT, preferred_element_type=F32)
        xt[:, d * ROWS : (d + 1) * ROWS] = turned.astype(BF16)
    loop(1, N_CTX, lambda k: first_copy(me, ctx_peer(k), ctx_peer(k)).wait_recv())

    def sum_up(j):
        for s in range(2):
            at = (2 * j + s) * BACK
            acc = landed[give[at]].astype(F32)
            for w in range(1, BACK):
                acc += landed[give[at + w]].astype(F32)
            total[j, s] = acc.astype(BF16)

    def serve(k):
        sum_up(ctx_peer(k))
        second_copy(ctx_peer(k), me, ctx_peer(k)).start()

    loop(1, N_CTX, serve)
    sum_up(me)
    back[me] = total[me]
    loop(1, N_CTX, lambda k: first_copy(ctx_peer(k), me, ctx_peer(k)).wait_send())
    loop(1, N_CTX, lambda k: second_copy(me, ctx_peer(k), ctx_peer(k)).wait_recv())
    for kind in range(2):
        for r in range(SPAN // PIECE):
            for j in range(KVH):
                for s in range(2):
                    rows = slice(s * SPAN + r * PIECE, s * SPAN + (r + 1) * PIECE)
                    cols = slice(j * HD, (j + 1) * HD)
                    g = back[kind * 16 + r * KVH + j, s].astype(F32) + own_ref[kind, rows, cols]
                    if kind == 0:
                        g = g * cos_ref[rows] - swap_halves(g) * sin_ref[rows]
                    grads[dp, rows, kind * KVC + j * HD : kind * KVC + (j + 1) * HD] = g.astype(BF16)
    loop(1, 4, lambda k: y_copy(dp, y_peer(k)).start())
    sib_copy(dp).start()
    for k in range(1, 4):
        y_copy(y_peer(k), y_peer(k)).wait_recv()
        sib_copy(y_peer(k)).start()
    loop(1, N_CTX, lambda k: second_copy(ctx_peer(k), me, ctx_peer(k)).wait_send())
    loop(0, 4, lambda k: sib_copy(sib_peer(k)).wait_recv())
    for n in range(4):
        cols = slice(n * 256, (n + 1) * 256)
        acc = jnp.dot(xt[:, :256], grads[0:2, :, cols].reshape(256, 256), preferred_element_type=F32)
        for d in range(1, 4):
            acc += jnp.dot(
                xt[:, d * 256 : (d + 1) * 256],
                grads[2 * d : 2 * d + 2, :, cols].reshape(256, 256),
                preferred_element_type=F32,
            )
        wsend[:, :, cols] = acc.astype(BF16).reshape(N_X, W_X, 256)
    loop(1, N_X, lambda k: x_copy(x_peer(k), x, x_peer(k)).start())
    loop(1, 4, lambda k: y_copy(dp, y_peer(k)).wait_send())
    loop(0, 4, lambda k: sib_copy(y_peer(k)).wait_send())
    xland[x] = wsend[x]
    loop(1, N_X, lambda k: x_copy(x, x_peer(k), x_peer(k)).wait_recv())
    acc = xland[0].astype(F32)
    for n in range(1, N_X):
        acc += xland[n].astype(F32)
    pad = jnp.zeros((PIECE - W_DEV, 2 * KVC), F32)
    for n in range(N_Z):
        block = jnp.concatenate([acc[n * W_DEV : (n + 1) * W_DEV], pad], axis=0)
        zsend[n] = block.astype(BF16)
    loop(1, N_Z, lambda k: z_copy(z_peer(k), z, z_peer(k)).start())
    zland[z] = zsend[z]
    loop(1, N_X, lambda k: x_copy(x_peer(k), x, x_peer(k)).wait_send())
    loop(1, N_Z, lambda k: z_copy(z, z_peer(k), z_peer(k)).wait_recv())
    acc = zland[0].astype(F32)
    for n in range(1, N_Z):
        acc += zland[n].astype(F32)
    out_ref[...] = acc[:W_DEV]
    loop(1, N_Z, lambda k: z_copy(z_peer(k), z, z_peer(k)).wait_send())


def per_device(queries, keys, values, grad_out, inputs, span_map, doc_lengths):
    smem = pl.BlockSpec(memory_space=pltpu.SMEM)
    vmem = pl.BlockSpec(memory_space=pltpu.VMEM)
    hbm = pl.BlockSpec(memory_space=pl.ANY)
    dma = pltpu.SemaphoreType.DMA
    params = functools.partial(pltpu.CompilerParams, vmem_limit_bytes=VMEM_LIMIT)
    shape = jax.ShapeDtypeStruct

    pack, cos, sin, slot_of = pl.pallas_call(
        prep_kernel,
        out_shape=[
            shape((N_CTX, 2, PIECE, HD), BF16),
            shape((ROWS, HD), F32),
            shape((ROWS, HD), F32),
            shape((1, SLOTS), jnp.int32),
        ],
        in_specs=[smem, smem, vmem, vmem, vmem],
        out_specs=[vmem, vmem, vmem, smem],
        compiler_params=params(),
        name="prep",
    )(span_map, doc_lengths, jnp.asarray(rope_lanes()), keys, values)

    win, x = pl.pallas_call(
        gather_kernel,
        out_shape=[
            shape((N_CTX, REACH, PIECE, HD), BF16),
            shape((N_DP, ROWS, W_DP), BF16),
        ],
        in_specs=[smem, smem, vmem, hbm],
        out_specs=[vmem, vmem],
        scratch_shapes=[
            pltpu.VMEM((SLOTS, PIECE, HD), BF16),
            pltpu.VMEM((N_CTX, REACH, PIECE, HD), BF16),
            pltpu.SMEM((SLOTS * BACK,), jnp.int32),
            dma((N_CTX,)), dma((N_CTX,)),
            dma((N_CTX,)), dma((N_CTX,)),
            dma((N_DP,)), dma((N_DP,)),
            dma,
        ],
        compiler_params=params(collective_id=0, has_side_effects=True),
        name="gather",
    )(span_map, slot_of, pack, inputs)

    pieces = (2, SPAN // PIECE, KVH)
    block = (2, SPAN // PIECE, 1)
    dq, part, own = pl.pallas_call(
        attend_kernel,
        grid=(KVH,),
        out_shape=[
            shape((ROWS, KVH * G * HD), BF16),
            shape(pieces + (REACH, PIECE, HD), BF16),
            shape((2, ROWS, KVC), F32),
        ],
        in_specs=[
            smem,
            smem,
            pl.BlockSpec((ROWS, G * HD), lambda j: (0, j)),
            pl.BlockSpec((ROWS, G * HD), lambda j: (0, j)),
            pl.BlockSpec(block + (REACH, PIECE, HD), lambda j: (0, 0, j, 0, 0, 0)),
            pl.BlockSpec(block + (2, PIECE, HD), lambda j: (0, 0, j, 0, 0, 0)),
            pl.BlockSpec((ROWS, HD), lambda j: (0, 0)),
            pl.BlockSpec((ROWS, HD), lambda j: (0, 0)),
        ],
        out_specs=[
            pl.BlockSpec((ROWS, G * HD), lambda j: (0, j)),
            pl.BlockSpec(block + (REACH, PIECE, HD), lambda j: (0, 0, j, 0, 0, 0)),
            pl.BlockSpec((2, ROWS, HD), lambda j: (0, 0, j)),
        ],
        scratch_shapes=[pltpu.VMEM((2, (BACK + 1) * SPAN, HD), F32)],
        compiler_params=params(),
        name="attend",
    )(
        span_map, doc_lengths, queries, grad_out,
        win.reshape(pieces + (REACH, PIECE, HD)), pack.reshape(pieces + (2, PIECE, HD)), cos, sin,
    )

    weight = pl.pallas_call(
        reduce_kernel,
        out_shape=shape((W_DEV, 2 * KVC), F32),
        in_specs=[smem, smem, vmem, vmem, vmem, vmem, vmem, vmem],
        out_specs=vmem,
        scratch_shapes=[
            pltpu.VMEM((N_CTX * REACH + 1, PIECE, HD), BF16),
            pltpu.SMEM((SLOTS * BACK,), jnp.int32),
            pltpu.VMEM((N_CTX, 2, PIECE, HD), BF16),
            pltpu.VMEM((N_CTX, 2, PIECE, HD), BF16),
            pltpu.VMEM((N_DP, ROWS, 2 * KVC), BF16),
            pltpu.VMEM((W_DP, N_DP * ROWS), BF16),
            pltpu.VMEM((N_X, W_X, 2 * KVC), BF16),
            pltpu.VMEM((N_X, W_X, 2 * KVC), BF16),
            pltpu.VMEM((N_Z, PIECE, 2 * KVC), BF16),
            pltpu.VMEM((N_Z, PIECE, 2 * KVC), BF16),
            dma((N_CTX,)), dma((N_CTX,)),
            dma((N_CTX,)), dma((N_CTX,)),
            dma((N_DP,)), dma((N_DP,)),
            dma((N_DP,)), dma((N_DP,)),
            dma((N_X,)), dma((N_X,)),
            dma((N_Z,)), dma((N_Z,)),
        ],
        compiler_params=params(collective_id=1, has_side_effects=True),
        name="reduce",
    )(
        span_map, slot_of, part.reshape(N_CTX, REACH, PIECE, HD), own, cos, sin, x,
        jnp.asarray(feature_order(), BF16),
    )
    return dq, weight


def solution(mesh):
    rows = P(("dp", "ctx"), None)
    return jax.shard_map(
        per_device,
        mesh=mesh,
        in_specs=(rows, rows, rows, rows, rows, P("dp", None), P("dp", None)),
        out_specs=(rows, rows),
        check_vma=False,
    )
```

```python
import functools

import jax
import jax.numpy as jnp
import numpy as np
from jax import lax
from jax.experimental import pallas as pl
from jax.experimental.pallas import tpu as pltpu
from jax.sharding import PartitionSpec as P

MESH = pl.DeviceIdType.MESH
BF16 = jnp.bfloat16
F32 = jnp.float32
I32 = jnp.int32

KVH = 4
G = 8
HD = 128
ROT = 64
ROPE_BASE = 10000000.0
SPAN = 64
BACK = 4
ROWS = 2 * SPAN
KEYS = (BACK + 1) * SPAN
N_CTX = 32
N_DP = 8
N_X = 4
N_Z = 8
SLOTS = 2 * N_CTX
NDOC = 32
KVC = KVH * HD
PIECE = 16
N_ROW = SPAN // PIECE
N_PIECE = N_ROW * KVH
REACH = 2 * BACK
DW = 3072
W_DP = DW // N_DP
W_DEV = W_DP // N_CTX
W_X = W_DP // N_X
CHUNKS = 4
W_COL = 2 * KVC // CHUNKS
MASKED = -1e30
SCALE = HD**-0.5
VMEM_LIMIT = 60 * 1024 * 1024

NT = (((1,), (1,)), ((), ()))
TN = (((0,), (0,)), ((), ()))


def rope_lanes():
    half = ROT // 2
    freq = ROPE_BASE ** (-(np.arange(half, dtype=np.float64) * 2.0 / ROT))
    row = np.zeros((1, HD), np.float32)
    row[0, :half] = freq
    row[0, half:ROT] = freq
    return row


def feature_order():
    order = np.arange(W_DP).reshape(N_Z, N_X, W_DEV).transpose(1, 0, 2).reshape(-1)
    return np.eye(W_DP, dtype=np.float32)[order]


def swap_halves(x):
    lane = lax.broadcasted_iota(I32, x.shape, 1)
    return jnp.where(lane < ROT // 2, pltpu.roll(x, HD - ROT // 2, 1), pltpu.roll(x, ROT // 2, 1))


def begin_of(pos, len_ref):
    def step(d, carry):
        start, begin = carry
        return start + len_ref[0, d], jnp.where(pos >= start, start, begin)

    _, begin = lax.fori_loop(0, NDOC, step, (jnp.int32(0), jnp.zeros_like(pos)), unroll=True)
    return begin


def loop(first, last, body):
    def step(k, carry):
        body(k)
        return carry

    lax.fori_loop(first, last, step, 0)


def remote(src, dst, send, recv, device):
    return pltpu.make_async_remote_copy(
        src_ref=src, dst_ref=dst, send_sem=send, recv_sem=recv, device_id=device, device_id_type=MESH
    )


def lanes(at, size):
    return pl.ds(pl.multiple_of(at, HD), size)


def kernel(
    span_h, len_h, freq_h, perm_h, q_h, k_h, v_h, do_h, in_h, dq_h, out_ref,
    span, lens, slot_of, take, give,
    slot_v, freq, perm, q, keys, vals, do, cos, sin, bias, qrot, dq,
    pack, held, chosen, win, part, own, landed, total, back, x_in, xt,
    grads, wsend, xland, zsend, zland,
    local, send1, recv1, send2, recv2, send3, recv3, send4, recv4, send5, recv5,
    send6, recv6, send7, recv7, send8, recv8, send9, recv9,
):
    dp, me = lax.axis_index("dp"), lax.axis_index("ctx")
    z, x = me // N_X, lax.rem(me, N_X)
    sib = dp + 1 - 2 * lax.rem(dp, 2)
    ctx_peer = lambda k: lax.rem(me + k, N_CTX)
    dp_peer = lambda k: lax.rem(dp + k, N_DP)
    y_peer = lambda k: lax.rem(dp + 2 * k, N_DP)
    sib_peer = lambda k: lax.rem(sib + 2 * k, N_DP)
    x_peer = lambda k: lax.rem(x + k, N_X)
    z_peer = lambda k: lax.rem(z + k, N_Z)
    piece_here = lax.rem(z, N_ROW) * KVH + x

    def near(k):
        dz, dx = k // N_X, lax.rem(k, N_X)
        two = jnp.where(lax.rem(dx, 2) == 0, 2, N_Z - 2)
        return jnp.where(dz == 2, two, jnp.where(dz == 3, N_Z - 1, dz)), dx

    def reader(k):
        dz, dx = near(k)
        return lax.rem(z + dz, N_Z) * N_X + lax.rem(x + dx, N_X)

    def holder(k):
        dz, dx = near(k)
        return lax.rem(z + N_Z - dz, N_Z) * N_X + lax.rem(x + N_X - dx, N_X)

    def piece_of(device):
        return lax.rem(device, N_PIECE)

    own_cols = lanes(dp * W_DP, W_DP)
    fetches = [
        pltpu.make_async_copy(src, dst, local.at[n])
        for n, (src, dst) in enumerate([
            (span_h, span), (len_h, lens), (freq_h, freq), (k_h, keys), (v_h, vals),
            (q_h, q), (do_h, do), (perm_h, perm), (in_h.at[:, own_cols], x_in.at[dp]),
        ])
    ]
    for copy in fetches:
        copy.start()
    barrier = pltpu.get_barrier_semaphore()

    def greet(device):
        pl.semaphore_signal(barrier, inc=1, device_id=device, device_id_type=MESH)

    loop(1, N_CTX, lambda k: greet((dp, ctx_peer(k))))
    loop(1, N_DP, lambda k: greet((dp_peer(k), me)))

    for copy in fetches[:5]:
        copy.wait()
    lane_row = lax.broadcasted_iota(I32, (1, HD), 1)
    slots = jnp.zeros((1, HD), I32)
    for n in range(SLOTS):
        slots = jnp.where(lane_row == span[0, n], n, slots)
    slot_v[...] = slots
    slot_copy = pltpu.make_async_copy(slot_v, slot_of, local.at[9])
    slot_copy.start()
    row = lax.broadcasted_iota(I32, (ROWS, HD), 0)
    lane = lax.broadcasted_iota(I32, (ROWS, HD), 1)
    mine = (span[0, 2 * me], span[0, 2 * me + 1])
    pos = jnp.where(row >= SPAN, mine[1] * SPAN + row - SPAN, mine[0] * SPAN + row)
    rel = (pos - begin_of(pos, lens)).astype(F32)
    angle = rel * freq[...]
    sine = jnp.sin(angle)
    cos[...] = jnp.where(lane < ROT, jnp.cos(angle), 1.0)
    sin[...] = jnp.where(lane < ROT // 2, -sine, jnp.where(lane < ROT, sine, 0.0))
    for j in range(KVH):
        k = keys[:, j * HD : (j + 1) * HD].astype(F32)
        k = (k * cos[...] + swap_halves(k) * sin[...]).astype(BF16)
        v = vals[:, j * HD : (j + 1) * HD]
        for s in range(2):
            for r in range(N_ROW):
                at = s * SPAN + r * PIECE
                pack[r * KVH + j, s, 0] = k[at : at + PIECE]
                pack[r * KVH + j, s, 1] = v[at : at + PIECE]
    slot_copy.wait()
    pl.semaphore_wait(barrier, N_CTX - 1 + N_DP - 1)

    def copy1(src, owner, peer):
        return remote(
            pack.at[piece_of(src)], held.at[pl.ds(2 * owner, 2)], send1.at[src], recv1.at[owner], (dp, peer)
        )

    def copy5(src, owner, peer):
        cols = lanes(src * W_DP, W_DP)
        return remote(in_h.at[:, cols], x_in.at[owner], send5.at[src], recv5.at[owner], (peer, me))

    loop(1, N_CTX, lambda k: copy1(ctx_peer(k), me, ctx_peer(k)).start())
    loop(1, N_DP, lambda k: copy5(dp_peer(k), dp, dp_peer(k)).start())
    held[pl.ds(2 * me, 2)] = pack[piece_here]

    def fill(slot):
        at = span[0, slot]
        for w in range(BACK):
            take[slot * BACK + w] = slot_of[0, jnp.maximum(at - BACK + w, 0)]
            later = at + 1 + w
            source = slot_of[0, jnp.minimum(later, SLOTS - 1)] * BACK + (BACK - 1 - w)
            give[slot * BACK + w] = jnp.where(later < SLOTS, source, N_CTX * REACH)

    loop(0, SLOTS, fill)
    for s in range(2):
        lane8 = lax.broadcasted_iota(I32, (8, HD), 1)
        qpos = mine[s] * SPAN + jnp.where(lane8 >= SPAN, lane8 - SPAN, lane8)
        qbegin = begin_of(qpos, lens)
        n = lax.broadcasted_iota(I32, (KEYS, HD), 0)
        r, w, t = n >> 6, (n >> 4) & 3, n & 15
        earlier = (mine[s] - BACK + w) * SPAN + r * PIECE + t
        kpos = jnp.where(n < BACK * SPAN, earlier, mine[s] * SPAN + (n - BACK * SPAN))
        allowed = (kpos <= qpos[0:1]) & (kpos >= qbegin[0:1])
        bias[s] = jnp.where(allowed, 0.0, MASKED)
    fetches[5].wait()

    def rotate(h):
        v = q[:, lanes(h * HD, HD)].astype(F32)
        qrot[:, lanes(h * HD, HD)] = (v * cos[...] + swap_halves(v) * sin[...]).astype(BF16)

    loop(0, KVH * G, rotate)
    empty = jnp.zeros((REACH, 2, PIECE, HD), BF16)

    def clear(dz, dx):
        device = lax.rem(z + dz, N_Z) * N_X + lax.rem(x + dx, N_X)
        landed[pl.ds(REACH * device, REACH)] = empty

    loop(0, 12, lambda k: clear(3 + k // N_X, lax.rem(k, N_X)))
    loop(0, 2, lambda k: clear(2, 2 * k + 1))
    loop(0, 2, lambda k: clear(6, 2 * k))
    landed[N_CTX * REACH] = jnp.zeros((2, PIECE, HD), BF16)
    loop(1, N_CTX, lambda k: copy1(me, ctx_peer(k), ctx_peer(k)).wait_recv())

    def choose(s, k):
        device = reader(k)
        for w in range(BACK):
            chosen[s, k, w] = held[take[device * REACH + s * BACK + w]]

    def copy2(s, k, peer, piece):
        return remote(chosen.at[s, k], win.at[s, piece], send2.at[s, k], recv2.at[s, k], (dp, peer))

    for s in range(2):

        def serve(k, s=s):
            choose(s, k)
            copy2(s, k, reader(k), piece_here).start()

        loop(1, N_PIECE, serve)
        choose(s, 0)
        win[s, piece_here] = chosen[s, 0]
    fetches[6].wait()
    fetches[7].wait()
    fetches[8].wait()
    loop(1, N_DP, lambda k: copy5(dp, dp_peer(k), dp_peer(k)).wait_recv())
    for d in range(N_DP):
        turned = lax.dot_general(perm[...], x_in[d], NT, preferred_element_type=F32)
        xt[:, d * ROWS : (d + 1) * ROWS] = turned.astype(BF16)

    def copy3(s, k, src, owner, peer):
        return remote(
            part.at[s, src],
            landed.at[pl.ds(REACH * owner + BACK * s, BACK)],
            send3.at[s, k],
            recv3.at[s, k],
            (dp, peer),
        )

    for s in range(2):
        loop(1, N_PIECE, lambda k, s=s: copy2(s, k, holder(k), piece_of(holder(k))).wait_recv())
        rows = slice(s * SPAN, (s + 1) * SPAN)

        def attend(n, s=s, rows=rows):
            j = lax.rem(x + n, KVH)

            def window(kind):
                parts = [win[s, r * KVH + j, :, kind].reshape(BACK * PIECE, HD) for r in range(N_ROW)]
                parts += [pack[r * KVH + j, s, kind] for r in range(N_ROW)]
                return jnp.concatenate(parts, axis=0)

            def stacked(ref):
                parts = [ref[rows, lanes((j * G + g) * HD, HD)] for g in range(G)]
                return jnp.concatenate(parts, axis=0)

            k, v = window(0), window(1)
            qs, dos = stacked(qrot), stacked(do)
            mask = jnp.concatenate([bias[s]] * (G * SPAN // HD), axis=1)
            scores = lax.dot_general(k, qs, NT, preferred_element_type=F32)
            scores = scores * (SCALE * float(np.log2(np.e))) + mask
            weight = jnp.exp2(scores - jnp.max(scores, axis=0, keepdims=True))
            probs = weight * (1.0 / jnp.sum(weight, axis=0, keepdims=True))
            dprobs = lax.dot_general(v, dos, NT, preferred_element_type=F32)
            delta = jnp.sum(probs * dprobs, axis=0, keepdims=True)
            dscores = (probs * (dprobs - delta)).astype(BF16)
            low = probs.astype(BF16)
            dk = jnp.dot(dscores, qs, preferred_element_type=F32) * SCALE
            dv = jnp.dot(low, dos, preferred_element_type=F32)
            for kind, grad in ((0, dk), (1, dv)):
                earlier = grad[: BACK * SPAN].astype(BF16).reshape(N_ROW, BACK, PIECE, HD)
                for r in range(N_ROW):
                    part[s, r * KVH + j, :, kind] = earlier[r]
                own[kind, rows, lanes(j * HD, HD)] = grad[BACK * SPAN :]
            dx = lax.rem(N_X - n, N_X)

            def hand_over(dz):
                at = dz * N_X + dx

                @pl.when(at > 0)
                def _():
                    copy3(s, at, piece_of(holder(at)), me, holder(at)).start()

            loop(0, N_ROW, hand_over)
            dqt = lax.dot_general(k, dscores, TN, preferred_element_type=F32)
            turned = dqt.T * SCALE
            for g in range(G):
                u = turned[g * SPAN : (g + 1) * SPAN]
                u = u * cos[rows] - swap_halves(u) * sin[rows]
                dq[rows, lanes((j * G + g) * HD, HD)] = u.astype(BF16)

        loop(0, KVH, attend)
        landed[pl.ds(REACH * me + BACK * s, BACK)] = part[s, piece_here]
    dq_copy = pltpu.make_async_copy(dq, dq_h, local.at[10])
    dq_copy.start()
    for s in range(2):
        loop(1, N_PIECE, lambda k, s=s: copy3(s, k, piece_here, reader(k), reader(k)).wait_recv())

    def copy4(kind, src, owner, peer):
        return remote(
            total.at[kind, src], back.at[kind, owner], send4.at[kind, src], recv4.at[kind, owner], (dp, peer)
        )

    def sum_up(kind, device):
        for s in range(2):
            at = (2 * device + s) * BACK
            acc = landed[give[at], kind].astype(F32)
            for w in range(1, BACK):
                acc += landed[give[at + w], kind].astype(F32)
            total[kind, device, s] = acc.astype(BF16)

    for kind in range(2):

        def give_back(k, kind=kind):
            sum_up(kind, ctx_peer(k))
            copy4(kind, ctx_peer(k), me, ctx_peer(k)).start()

        loop(1, N_CTX, give_back)
        sum_up(kind, me)
        back[kind, me] = total[kind, me]

    def copy6(c, owner, peer):
        return remote(grads.at[owner, c], grads.at[owner, c], send6.at[c, peer], recv6.at[c, owner], (peer, me))

    def copy7(c, owner):
        return remote(grads.at[owner, c], grads.at[owner, c], send7.at[c, owner], recv7.at[c, owner], (sib, me))

    for kind in range(2):
        loop(1, N_CTX, lambda k, kind=kind: copy4(kind, me, ctx_peer(k), ctx_peer(k)).wait_recv())
        for half in range(2):
            c = 2 * kind + half
            for j in (2 * half, 2 * half + 1):
                for r in range(N_ROW):
                    for s in range(2):
                        rows = slice(s * SPAN + r * PIECE, s * SPAN + (r + 1) * PIECE)
                        piece = r * KVH + j
                        g = back[kind, piece, s].astype(F32) + back[kind, N_PIECE + piece, s].astype(F32)
                        g += own[kind, rows, j * HD : (j + 1) * HD]
                        if kind == 0:
                            g = g * cos[rows] - swap_halves(g) * sin[rows]
                        cols = slice((j - 2 * half) * HD, (j - 2 * half + 1) * HD)
                        grads[dp, c, rows, cols] = g.astype(BF16)
            loop(1, 4, lambda k, c=c: copy6(c, dp, y_peer(k)).start())
            copy7(c, dp).start()

    def copy8(c, src, owner, peer):
        return remote(wsend.at[c, src], xland.at[c, owner], send8.at[c, src], recv8.at[c, owner], (dp, z * N_X + peer))

    def copy9(c, src, owner, peer):
        return remote(zsend.at[c, src], zland.at[c, owner], send9.at[c, src], recv9.at[c, owner], (dp, peer * N_X + x))

    def forward(c):
        for k in range(1, 4):
            copy6(c, y_peer(k), y_peer(k)).wait_recv()
            copy7(c, y_peer(k)).start()

    def multiply(c):
        loop(0, 4, lambda k: copy7(c, sib_peer(k)).wait_recv())
        w = jnp.dot(xt[...], grads[:, c].reshape(N_DP * ROWS, W_COL), preferred_element_type=F32)
        wsend[c] = w.astype(BF16).reshape(N_X, W_X, W_COL)
        loop(1, N_X, lambda k: copy8(c, x_peer(k), x, x_peer(k)).start())
        xland[c, x] = wsend[c, x]

    def sum_x(c):
        loop(1, N_X, lambda k: copy8(c, x, x_peer(k), x_peer(k)).wait_recv())
        acc = xland[c, 0].astype(F32)
        for n in range(1, N_X):
            acc += xland[c, n].astype(F32)
        pad = jnp.zeros((PIECE - W_DEV, W_COL), F32)
        for n in range(N_Z):
            block = jnp.concatenate([acc[n * W_DEV : (n + 1) * W_DEV], pad], axis=0)
            zsend[c, n] = block.astype(BF16)
        loop(1, N_Z, lambda k: copy9(c, z_peer(k), z, z_peer(k)).start())
        zland[c, z] = zsend[c, z]

    def sum_z(c):
        loop(1, N_Z, lambda k: copy9(c, z, z_peer(k), z_peer(k)).wait_recv())
        acc = zland[c, 0].astype(F32)
        for n in range(1, N_Z):
            acc += zland[c, n].astype(F32)
        out_ref[:, c * W_COL : (c + 1) * W_COL] = acc[:W_DEV]

    forward(0)
    for c in range(CHUNKS):
        if c + 1 < CHUNKS:
            forward(c + 1)
        multiply(c)
    for c in range(CHUNKS):
        sum_x(c)
    for c in range(CHUNKS):
        sum_z(c)

    loop(1, N_CTX, lambda k: copy1(ctx_peer(k), me, ctx_peer(k)).wait_send())
    loop(1, N_DP, lambda k: copy5(dp_peer(k), dp, dp_peer(k)).wait_send())
    for s in range(2):
        loop(1, N_PIECE, lambda k, s=s: copy2(s, k, reader(k), piece_here).wait_send())
        loop(1, N_PIECE, lambda k, s=s: copy3(s, k, piece_of(holder(k)), me, holder(k)).wait_send())
    for kind in range(2):
        loop(1, N_CTX, lambda k, kind=kind: copy4(kind, ctx_peer(k), me, ctx_peer(k)).wait_send())
    for c in range(CHUNKS):
        loop(1, 4, lambda k, c=c: copy6(c, dp, y_peer(k)).wait_send())
        loop(0, 4, lambda k, c=c: copy7(c, y_peer(k)).wait_send())
        loop(1, N_X, lambda k, c=c: copy8(c, x_peer(k), x, x_peer(k)).wait_send())
        loop(1, N_Z, lambda k, c=c: copy9(c, z_peer(k), z, z_peer(k)).wait_send())
    dq_copy.wait()


def per_device(queries, keys, values, grad_out, inputs, span_map, doc_lengths):
    vmem, smem, dma = pltpu.VMEM, pltpu.SMEM, pltpu.SemaphoreType.DMA
    hbm = pl.BlockSpec(memory_space=pl.ANY)
    wide = KVH * G * HD
    tile = (PIECE, HD)
    return pl.pallas_call(
        kernel,
        out_shape=[
            jax.ShapeDtypeStruct((ROWS, wide), BF16),
            jax.ShapeDtypeStruct((W_DEV, 2 * KVC), F32),
        ],
        in_specs=[hbm] * 9,
        out_specs=[hbm, pl.BlockSpec(memory_space=pltpu.VMEM)],
        scratch_shapes=[
            smem((1, SLOTS), I32),
            smem((1, NDOC), I32),
            smem((1, HD), I32),
            smem((SLOTS * BACK,), I32),
            smem((SLOTS * BACK,), I32),
            vmem((1, HD), I32),
            vmem((1, HD), F32),
            vmem((W_DP, W_DP), BF16),
            vmem((ROWS, wide), BF16),
            vmem((ROWS, KVC), BF16),
            vmem((ROWS, KVC), BF16),
            vmem((ROWS, wide), BF16),
            vmem((ROWS, HD), F32),
            vmem((ROWS, HD), F32),
            vmem((2, KEYS, HD), F32),
            vmem((ROWS, wide), BF16),
            vmem((ROWS, wide), BF16),
            vmem((N_PIECE, 2, 2) + tile, BF16),
            vmem((SLOTS, 2) + tile, BF16),
            vmem((2, N_PIECE, BACK, 2) + tile, BF16),
            vmem((2, N_PIECE, BACK, 2) + tile, BF16),
            vmem((2, N_PIECE, BACK, 2) + tile, BF16),
            vmem((2, ROWS, KVC), F32),
            vmem((N_CTX * REACH + 1, 2) + tile, BF16),
            vmem((2, N_CTX, 2) + tile, BF16),
            vmem((2, N_CTX, 2) + tile, BF16),
            vmem((N_DP, ROWS, W_DP), BF16),
            vmem((W_DP, N_DP * ROWS), BF16),
            vmem((N_DP, CHUNKS, ROWS, W_COL), BF16),
            vmem((CHUNKS, N_X, W_X, W_COL), BF16),
            vmem((CHUNKS, N_X, W_X, W_COL), BF16),
            vmem((CHUNKS, N_Z, PIECE, W_COL), BF16),
            vmem((CHUNKS, N_Z, PIECE, W_COL), BF16),
            dma((11,)),
            dma((N_CTX,)), dma((N_CTX,)),
            dma((2, N_PIECE)), dma((2, N_PIECE)),
            dma((2, N_PIECE)), dma((2, N_PIECE)),
            dma((2, N_CTX)), dma((2, N_CTX)),
            dma((N_DP,)), dma((N_DP,)),
            dma((CHUNKS, N_DP)), dma((CHUNKS, N_DP)),
            dma((CHUNKS, N_DP)), dma((CHUNKS, N_DP)),
            dma((CHUNKS, N_X)), dma((CHUNKS, N_X)),
            dma((CHUNKS, N_Z)), dma((CHUNKS, N_Z)),
        ],
        compiler_params=pltpu.CompilerParams(
            collective_id=0, has_side_effects=True, vmem_limit_bytes=VMEM_LIMIT
        ),
        name="packed_backward",
    )(
        span_map, doc_lengths, jnp.asarray(rope_lanes()), jnp.asarray(feature_order(), BF16),
        queries, keys, values, grad_out, inputs,
    )


def solution(mesh):
    rows = P(("dp", "ctx"), None)
    return jax.shard_map(
        per_device,
        mesh=mesh,
        in_specs=(rows, rows, rows, rows, rows, P("dp", None), P("dp", None)),
        out_specs=(rows, rows),
        check_vma=False,
    )
```

```python
import functools

import jax
import jax.numpy as jnp
import numpy as np
from jax import lax
from jax.experimental import pallas as pl
from jax.experimental.pallas import tpu as pltpu
from jax.sharding import PartitionSpec as P

MESH = pl.DeviceIdType.MESH
BF16 = jnp.bfloat16
F32 = jnp.float32
I32 = jnp.int32

KVH = 4
G = 8
HD = 128
ROT = 64
ROPE_BASE = 10000000.0
SPAN = 64
BACK = 4
ROWS = 2 * SPAN
KEYS = (BACK + 1) * SPAN
N_CTX = 32
N_DP = 8
N_X = 4
N_Z = 8
SLOTS = 2 * N_CTX
NDOC = 32
KVC = KVH * HD
PIECE = 16
N_ROW = SPAN // PIECE
N_PIECE = N_ROW * KVH
REACH = 2 * BACK
DW = 3072
W_DP = DW // N_DP
W_DEV = W_DP // N_CTX
W_X = W_DP // N_X
CHUNKS = 4
W_COL = 2 * KVC // CHUNKS
N_Y = N_DP // 2
LINE = 4
MASKED = -1e30
SCALE = HD**-0.5
VMEM_LIMIT = 60 * 1024 * 1024

NT = (((1,), (1,)), ((), ()))
TN = (((0,), (0,)), ((), ()))


def rope_lanes():
    half = ROT // 2
    freq = ROPE_BASE ** (-(np.arange(half, dtype=np.float64) * 2.0 / ROT))
    return np.tile(freq.astype(np.float32), HD // half)[None]


def feature_order():
    order = np.arange(W_DP).reshape(N_Z, N_X, W_DEV).transpose(1, 0, 2).reshape(-1)
    return np.eye(W_DP, dtype=np.float32)[order]


def swap_halves(x):
    lane = lax.broadcasted_iota(I32, x.shape, 1)
    return jnp.where(lane < ROT // 2, pltpu.roll(x, HD - ROT // 2, 1), pltpu.roll(x, ROT // 2, 1))


def begin_of(pos, len_ref):
    def step(d, carry):
        start, begin = carry
        return start + len_ref[0, d], jnp.where(pos >= start, start, begin)

    _, begin = lax.fori_loop(0, NDOC, step, (jnp.int32(0), jnp.zeros_like(pos)), unroll=True)
    return begin


def loop(first, last, body):
    def step(k, carry):
        body(k)
        return carry

    lax.fori_loop(first, last, step, 0)


def remote(src, dst, send, recv, device):
    return pltpu.make_async_remote_copy(
        src_ref=src, dst_ref=dst, send_sem=send, recv_sem=recv, device_id=device, device_id_type=MESH
    )


def rope_tables(pos, lens, freq, cos, sin):
    rel = (pos - begin_of(pos, lens)).astype(F32)
    angle = rel * freq[...]
    packed_cos, packed_sin = jnp.cos(angle), jnp.sin(angle)
    lane = lax.broadcasted_iota(I32, pos.shape, 1)
    half, rows = ROT // 2, pos.shape[0]

    def turn(v, shift):
        shift = shift % HD
        return pltpu.roll(v, shift, 1) if shift else v

    for n in range(HD // half):
        pair = lambda v: (turn(v, -half * n), turn(v, half - half * n))
        (c0, c1), (s0, s1) = pair(packed_cos), pair(packed_sin)
        cos[n * rows : (n + 1) * rows] = jnp.where(lane < half, c0, jnp.where(lane < ROT, c1, 1.0))
        sin[n * rows : (n + 1) * rows] = jnp.where(lane < half, -s0, jnp.where(lane < ROT, s1, 0.0))


def lanes(at, size):
    return pl.ds(pl.multiple_of(at, HD), size)


def kernel(
    span_h, len_h, freq_h, perm_h, q_h, k_h, v_h, do_h, in_h, dq_h, out_ref,
    span, lens, slot_of, take, give,
    slot_v, freq, perm, q, keys, vals, do, feats, cos, sin, bias, qrot, dq,
    pack, held, chosen, win, part, own, landed, total, back, turned, xta, xtb,
    grads, wsend, wland, zsend, zland,
    local, send1, recv1, send2, recv2, send3, recv3, send4, recv4, send5, recv5, send0, recv0,
    send6, recv6, send7, recv7, send8, recv8, send9, recv9,
):
    dp, me = lax.axis_index("dp"), lax.axis_index("ctx")
    z, x = me // N_X, lax.rem(me, N_X)
    y, core = dp // 2, lax.rem(dp, 2)
    sib = dp + 1 - 2 * core
    team = 2 * x + core
    ctx_peer = lambda k: lax.rem(me + k, N_CTX)
    dp_peer = lambda k: lax.rem(dp + k, N_DP)
    y_peer = lambda k: lax.rem(dp + 2 * k, N_DP)
    sib_peer = lambda k: lax.rem(sib + 2 * k, N_DP)
    x_peer = lambda k: lax.rem(x + k, N_X)
    team_peer = lambda k: lax.rem(team + k, 2 * N_X)
    z_peer = lambda k: lax.rem(z + k, N_Z)
    piece_here = lax.rem(z, N_ROW) * KVH + x

    def near(k):
        dz, dx = k // N_X, lax.rem(k, N_X)
        two = jnp.where(lax.rem(dx, 2) == 0, 2, N_Z - 2)
        return jnp.where(dz == 2, two, jnp.where(dz == 3, N_Z - 1, dz)), dx

    def reader(k):
        dz, dx = near(k)
        return lax.rem(z + dz, N_Z) * N_X + lax.rem(x + dx, N_X)

    def holder(k):
        dz, dx = near(k)
        return lax.rem(z + N_Z - dz, N_Z) * N_X + lax.rem(x + N_X - dx, N_X)

    def piece_of(device):
        return lax.rem(device, N_PIECE)

    fetches = [
        pltpu.make_async_copy(src, dst, local.at[n])
        for n, (src, dst) in enumerate([
            (k_h, keys), (v_h, vals), (span_h, span), (len_h, lens), (freq_h, freq),
            (perm_h, perm), (in_h, feats), (q_h, q), (do_h, do),
        ])
    ]
    for copy in fetches:
        copy.start()
    barrier = pltpu.get_barrier_semaphore()

    def greet(device):
        pl.semaphore_signal(barrier, inc=1, device_id=device, device_id_type=MESH)

    loop(1, N_CTX, lambda k: greet((dp, ctx_peer(k))))
    loop(1, N_DP, lambda k: greet((dp_peer(k), me)))
    loop(1, N_X, lambda k: greet((sib, z * N_X + x_peer(k))))
    for copy in fetches[:2]:
        copy.wait()
    for s in range(2):
        for r in range(N_ROW):
            rows = slice(s * SPAN + r * PIECE, s * SPAN + (r + 1) * PIECE)
            for j in range(KVH):
                cols = slice(j * HD, (j + 1) * HD)
                pack[r * KVH + j, s, 0] = keys[rows, cols]
                pack[r * KVH + j, s, 1] = vals[rows, cols]
    pl.semaphore_wait(barrier, N_CTX - 1 + N_DP - 1 + N_X - 1)

    def copy1(src, owner, peer):
        return remote(
            pack.at[piece_of(src)], held.at[pl.ds(2 * owner, 2)], send1.at[src], recv1.at[owner], (dp, peer)
        )

    loop(1, N_CTX, lambda k: copy1(ctx_peer(k), me, ctx_peer(k)).start())
    held[pl.ds(2 * me, 2)] = pack[piece_here]

    def copy5(src, owner, peer):
        return remote(
            turned.at[src // 2, lax.rem(src, 2)],
            xta.at[:, :, lanes(owner * ROWS, ROWS)],
            send5.at[src],
            recv5.at[owner],
            (peer, me),
        )

    def copy0(src, owner, peer):
        device = (dp - core + lax.rem(peer, 2), z * N_X + peer // 2)
        return remote(
            turned.at[:, lax.rem(src, 2), src // 2],
            xtb.at[:, :, lanes(owner * ROWS, ROWS)],
            send0.at[src],
            recv0.at[owner],
            device,
        )

    fetches[5].wait()
    fetches[6].wait()
    for d in range(N_DP):
        w = lax.dot_general(perm[...], feats[:, d * W_DP : (d + 1) * W_DP], NT, preferred_element_type=F32)
        turned[d // 2, d % 2] = w.astype(BF16).reshape(N_X, W_X, ROWS)
    loop(1, N_DP, lambda k: copy5(dp_peer(k), dp, dp_peer(k)).start())
    loop(1, 2 * N_X, lambda k: copy0(team_peer(k), team, team_peer(k)).start())
    xta[:, :, lanes(dp * ROWS, ROWS)] = turned[y, core]
    xtb[:, :, lanes(team * ROWS, ROWS)] = turned[:, core, x]

    for copy in fetches[2:5]:
        copy.wait()
    lane_row = lax.broadcasted_iota(I32, (1, HD), 1)
    slots = jnp.zeros((1, HD), I32)
    for n in range(SLOTS):
        slots = jnp.where(lane_row == span[0, n], n, slots)
    slot_v[...] = slots
    slot_copy = pltpu.make_async_copy(slot_v, slot_of, local.at[9])
    slot_copy.start()
    mine = (span[0, 2 * me], span[0, 2 * me + 1])
    for s in range(2):
        own_rows = SPAN // 4
        row = lax.broadcasted_iota(I32, (own_rows, HD), 0)
        group = lax.broadcasted_iota(I32, (own_rows, HD), 1) >> 5
        at = pl.ds(BACK * SPAN, SPAN)
        rope_tables(mine[s] * SPAN + group * own_rows + row, lens, freq, cos.at[s, at], sin.at[s, at])
        row = lax.broadcasted_iota(I32, (SPAN, HD), 0)
        group = lax.broadcasted_iota(I32, (SPAN, HD), 1) >> 5
        pos = (mine[s] - BACK + (row >> 4)) * SPAN + group * PIECE + (row & 15)
        at = pl.ds(0, BACK * SPAN)
        rope_tables(pos, lens, freq, cos.at[s, at], sin.at[s, at])
    slot_copy.wait()

    def fill(slot):
        at = span[0, slot]
        for w in range(BACK):
            take[slot * BACK + w] = slot_of[0, jnp.maximum(at - BACK + w, 0)]
            later = at + 1 + w
            source = slot_of[0, jnp.minimum(later, SLOTS - 1)] * BACK + (BACK - 1 - w)
            give[slot * BACK + w] = jnp.where(later < SLOTS, source, N_CTX * REACH)

    loop(0, SLOTS, fill)
    for s in range(2):
        lane8 = lax.broadcasted_iota(I32, (8, HD), 1)
        qpos = mine[s] * SPAN + jnp.where(lane8 >= SPAN, lane8 - SPAN, lane8)
        qbegin = begin_of(qpos, lens)
        n = lax.broadcasted_iota(I32, (KEYS, HD), 0)
        r, w, t = n >> 6, (n >> 4) & 3, n & 15
        earlier = (mine[s] - BACK + w) * SPAN + r * PIECE + t
        kpos = jnp.where(n < BACK * SPAN, earlier, mine[s] * SPAN + (n - BACK * SPAN))
        allowed = (kpos <= qpos[0:1]) & (kpos >= qbegin[0:1])
        bias[s] = jnp.where(allowed, 0.0, MASKED)
    fetches[7].wait()

    def rotate(h):
        for s in range(2):
            rows = slice(s * SPAN, (s + 1) * SPAN)
            v = q[rows, lanes(h * HD, HD)].astype(F32)
            v = v * cos[s, BACK * SPAN :] + swap_halves(v) * sin[s, BACK * SPAN :]
            qrot[rows, lanes(h * HD, HD)] = v.astype(BF16)

    loop(0, KVH * G, rotate)
    empty = jnp.zeros((REACH, 2, PIECE, HD), BF16)

    def clear(dz, dx):
        device = lax.rem(z + dz, N_Z) * N_X + lax.rem(x + dx, N_X)
        landed[pl.ds(REACH * device, REACH)] = empty

    loop(0, 12, lambda k: clear(3 + k // N_X, lax.rem(k, N_X)))
    loop(0, 2, lambda k: clear(2, 2 * k + 1))
    loop(0, 2, lambda k: clear(6, 2 * k))
    landed[N_CTX * REACH] = jnp.zeros((2, PIECE, HD), BF16)
    loop(1, N_CTX, lambda k: copy1(me, ctx_peer(k), ctx_peer(k)).wait_recv())

    def choose(s, k):
        device = reader(k)
        for w in range(BACK):
            chosen[s, k, w] = held[take[device * REACH + s * BACK + w]]

    def copy2(s, k, peer, piece):
        return remote(chosen.at[s, k], win.at[s, piece], send2.at[s, k], recv2.at[s, k], (dp, peer))

    for s in range(2):

        def serve(k, s=s):
            choose(s, k)
            copy2(s, k, reader(k), piece_here).start()

        loop(1, N_PIECE, serve)
        choose(s, 0)
        win[s, piece_here] = chosen[s, 0]
    fetches[8].wait()

    def copy3(s, k, src, owner, peer):
        return remote(
            part.at[s, src],
            landed.at[pl.ds(REACH * owner + BACK * s, BACK)],
            send3.at[s, k],
            recv3.at[s, k],
            (dp, peer),
        )

    for s in range(2):
        loop(1, N_PIECE, lambda k, s=s: copy2(s, k, holder(k), piece_of(holder(k))).wait_recv())
        rows = slice(s * SPAN, (s + 1) * SPAN)

        def attend(n, s=s, rows=rows):
            j = lax.rem(x + n, KVH)

            def window(kind):
                parts = [win[s, r * KVH + j, :, kind].reshape(BACK * PIECE, HD) for r in range(N_ROW)]
                parts += [pack[r * KVH + j, s, kind] for r in range(N_ROW)]
                return jnp.concatenate(parts, axis=0)

            def stacked(ref):
                parts = [ref[rows, lanes((j * G + g) * HD, HD)] for g in range(G)]
                return jnp.concatenate(parts, axis=0)

            k, v = window(0).astype(F32), window(1)
            k = (k * cos[s] + swap_halves(k) * sin[s]).astype(BF16)
            qs, dos = stacked(qrot), stacked(do)
            mask = jnp.concatenate([bias[s]] * (G * SPAN // HD), axis=1)
            scores = lax.dot_general(k, qs, NT, preferred_element_type=F32)
            scores = scores * (SCALE * float(np.log2(np.e))) + mask
            weight = jnp.exp2(scores - jnp.max(scores, axis=0, keepdims=True))
            probs = weight * (1.0 / jnp.sum(weight, axis=0, keepdims=True))
            dprobs = lax.dot_general(v, dos, NT, preferred_element_type=F32)
            delta = jnp.sum(probs * dprobs, axis=0, keepdims=True)
            dscores = (probs * (dprobs - delta)).astype(BF16)
            low = probs.astype(BF16)
            dk = jnp.dot(dscores, qs, preferred_element_type=F32) * SCALE
            dv = jnp.dot(low, dos, preferred_element_type=F32)
            for kind, grad in ((0, dk), (1, dv)):
                earlier = grad[: BACK * SPAN].astype(BF16).reshape(N_ROW, BACK, PIECE, HD)
                for r in range(N_ROW):
                    part[s, r * KVH + j, :, kind] = earlier[r]
                own[kind, rows, lanes(j * HD, HD)] = grad[BACK * SPAN :]
            dx = lax.rem(N_X - n, N_X)

            def hand_over(dz):
                at = dz * N_X + dx

                @pl.when(at > 0)
                def _():
                    copy3(s, at, piece_of(holder(at)), me, holder(at)).start()

            loop(0, N_ROW, hand_over)
            dqt = lax.dot_general(k, dscores, TN, preferred_element_type=F32)
            upright = dqt.T * SCALE
            for g in range(G):
                u = upright[g * SPAN : (g + 1) * SPAN]
                u = u * cos[s, BACK * SPAN :] - swap_halves(u) * sin[s, BACK * SPAN :]
                dq[rows, lanes((j * G + g) * HD, HD)] = u.astype(BF16)

        loop(0, KVH, attend)
        landed[pl.ds(REACH * me + BACK * s, BACK)] = part[s, piece_here]
    dq_copy = pltpu.make_async_copy(dq, dq_h, local.at[10])
    dq_copy.start()
    for s in range(2):
        loop(1, N_PIECE, lambda k, s=s: copy3(s, k, piece_here, reader(k), reader(k)).wait_recv())

    def copy4(kind, src, owner, peer):
        return remote(
            total.at[kind, src], back.at[kind, owner], send4.at[kind, src], recv4.at[kind, owner], (dp, peer)
        )

    def sum_up(kind, device):
        for s in range(2):
            at = (2 * device + s) * BACK
            acc = landed[give[at], kind].astype(F32)
            for w in range(1, BACK):
                acc += landed[give[at + w], kind].astype(F32)
            total[kind, device, s] = acc.astype(BF16)

    for kind in range(2):

        def give_back(k, kind=kind):
            sum_up(kind, ctx_peer(k))
            copy4(kind, ctx_peer(k), me, ctx_peer(k)).start()

        loop(1, N_CTX, give_back)
        sum_up(kind, me)
        back[kind, me] = total[kind, me]

    def line(half, k):
        if half == 0:
            return y_peer(k), (y_peer(k), me)
        return 2 * x_peer(k) + core, (dp, z * N_X + x_peer(k))

    def across(half, k):
        return sib_peer(k) if half == 0 else 2 * x_peer(k) + 1 - core

    def copy6(c, owner, k):
        _, device = line(c % 2, k)
        return remote(grads.at[c, owner], grads.at[c, owner], send6.at[c, k], recv6.at[c, owner], device)

    def copy7(c, owner):
        return remote(grads.at[c, owner], grads.at[c, owner], send7.at[c, owner], recv7.at[c, owner], (sib, me))

    member = lambda c: (dp, team)[c % 2]

    def assemble(c):
        kind, half = c // 2, c % 2
        for n in range(2):
            j = 2 * half + n
            for r in range(N_ROW):
                for s in range(2):
                    rows = slice(s * SPAN + r * PIECE, s * SPAN + (r + 1) * PIECE)
                    piece = r * KVH + j
                    g = back[kind, piece, s].astype(F32) + back[kind, N_PIECE + piece, s].astype(F32)
                    g += own[kind, rows, j * HD : (j + 1) * HD]
                    if kind == 0:
                        at = slice(BACK * SPAN + r * PIECE, BACK * SPAN + (r + 1) * PIECE)
                        g = g * cos[s, at] - swap_halves(g) * sin[s, at]
                    grads[c, member(c), rows, n * HD : (n + 1) * HD] = g.astype(BF16)
        loop(1, LINE, lambda k: copy6(c, member(c), k).start())
        copy7(c, member(c)).start()

    def forward(c):
        for k in range(1, LINE):
            owner, _ = line(c % 2, k)
            copy6(c, owner, k).wait_recv()
            copy7(c, owner).start()

    def rest(half, k):
        if half == 0:
            return x_peer(k), (dp, z * N_X + x_peer(k))
        return y_peer(k) // 2, (y_peer(k), me)

    place = lambda c: (x, y)[c % 2]

    def copy8(c, src, owner, k):
        _, device = rest(c % 2, k)
        return remote(wsend.at[c, src], wland.at[c, owner], send8.at[c, src], recv8.at[c, owner], device)

    def copy9(c, src, owner, peer):
        return remote(zsend.at[c, src], zland.at[c, owner], send9.at[c, src], recv9.at[c, owner], (dp, peer * N_X + x))

    def multiply(c):
        loop(0, LINE, lambda k: copy7(c, across(c % 2, k)).wait_recv())
        xt = (xta, xtb)[c % 2][...].reshape(W_DP, N_DP * ROWS)
        w = jnp.dot(xt, grads[c].reshape(N_DP * ROWS, W_COL), preferred_element_type=F32)
        wsend[c] = w.astype(BF16).reshape(LINE, W_X, W_COL)
        loop(1, LINE, lambda k: copy8(c, rest(c % 2, k)[0], place(c), k).start())
        wland[c, place(c)] = wsend[c, place(c)]

    def sum_line(c):
        loop(1, LINE, lambda k: copy8(c, place(c), rest(c % 2, k)[0], k).wait_recv())
        acc = wland[c, 0].astype(F32)
        for n in range(1, LINE):
            acc += wland[c, n].astype(F32)
        pad = jnp.zeros((PIECE - W_DEV, W_COL), F32)
        for n in range(N_Z):
            block = jnp.concatenate([acc[n * W_DEV : (n + 1) * W_DEV], pad], axis=0)
            zsend[c, n] = block.astype(BF16)
        loop(1, N_Z, lambda k: copy9(c, z_peer(k), z, z_peer(k)).start())
        zland[c, z] = zsend[c, z]

    def sum_z(c):
        loop(1, N_Z, lambda k: copy9(c, z, z_peer(k), z_peer(k)).wait_recv())
        acc = zland[c, 0].astype(F32)
        for n in range(1, N_Z):
            acc += zland[c, n].astype(F32)
        out_ref[:, c * W_COL : (c + 1) * W_COL] = acc[:W_DEV]

    loop(1, N_DP, lambda k: copy5(dp, dp_peer(k), dp_peer(k)).wait_recv())
    loop(1, 2 * N_X, lambda k: copy0(team, team_peer(k), team_peer(k)).wait_recv())
    loop(1, N_CTX, lambda k: copy4(0, me, ctx_peer(k), ctx_peer(k)).wait_recv())
    assemble(0)
    assemble(1)
    forward(0)
    forward(1)
    loop(1, N_CTX, lambda k: copy4(1, me, ctx_peer(k), ctx_peer(k)).wait_recv())
    assemble(2)
    assemble(3)
    multiply(0)
    multiply(1)
    forward(2)
    forward(3)
    multiply(2)
    multiply(3)
    for c in range(CHUNKS):
        sum_line(c)
    for c in range(CHUNKS):
        sum_z(c)

    loop(1, N_CTX, lambda k: copy1(ctx_peer(k), me, ctx_peer(k)).wait_send())
    loop(1, N_DP, lambda k: copy5(dp_peer(k), dp, dp_peer(k)).wait_send())
    loop(1, 2 * N_X, lambda k: copy0(team_peer(k), team, team_peer(k)).wait_send())
    for s in range(2):
        loop(1, N_PIECE, lambda k, s=s: copy2(s, k, reader(k), piece_here).wait_send())
        loop(1, N_PIECE, lambda k, s=s: copy3(s, k, piece_of(holder(k)), me, holder(k)).wait_send())
    for kind in range(2):
        loop(1, N_CTX, lambda k, kind=kind: copy4(kind, ctx_peer(k), me, ctx_peer(k)).wait_send())
    for c in range(CHUNKS):
        loop(1, LINE, lambda k, c=c: copy6(c, member(c), k).wait_send())
        copy7(c, member(c)).wait_send()
        loop(1, LINE, lambda k, c=c: copy7(c, line(c % 2, k)[0]).wait_send())
        loop(1, LINE, lambda k, c=c: copy8(c, rest(c % 2, k)[0], place(c), k).wait_send())
        loop(1, N_Z, lambda k, c=c: copy9(c, z_peer(k), z, z_peer(k)).wait_send())
    dq_copy.wait()


def per_device(queries, keys, values, grad_out, inputs, span_map, doc_lengths):
    vmem, smem, dma = pltpu.VMEM, pltpu.SMEM, pltpu.SemaphoreType.DMA
    hbm = pl.BlockSpec(memory_space=pl.ANY)
    wide = KVH * G * HD
    tile = (PIECE, HD)
    return pl.pallas_call(
        kernel,
        out_shape=[
            jax.ShapeDtypeStruct((ROWS, wide), BF16),
            jax.ShapeDtypeStruct((W_DEV, 2 * KVC), F32),
        ],
        in_specs=[hbm] * 9,
        out_specs=[hbm, pl.BlockSpec(memory_space=pltpu.VMEM)],
        scratch_shapes=[
            smem((1, SLOTS), I32),
            smem((1, NDOC), I32),
            smem((1, HD), I32),
            smem((SLOTS * BACK,), I32),
            smem((SLOTS * BACK,), I32),
            vmem((1, HD), I32),
            vmem((1, HD), F32),
            vmem((W_DP, W_DP), BF16),
            vmem((ROWS, wide), BF16),
            vmem((ROWS, KVC), BF16),
            vmem((ROWS, KVC), BF16),
            vmem((ROWS, wide), BF16),
            vmem((ROWS, DW), BF16),
            vmem((2, KEYS, HD), F32),
            vmem((2, KEYS, HD), F32),
            vmem((2, KEYS, HD), F32),
            vmem((ROWS, wide), BF16),
            vmem((ROWS, wide), BF16),
            vmem((N_PIECE, 2, 2) + tile, BF16),
            vmem((SLOTS, 2) + tile, BF16),
            vmem((2, N_PIECE, BACK, 2) + tile, BF16),
            vmem((2, N_PIECE, BACK, 2) + tile, BF16),
            vmem((2, N_PIECE, BACK, 2) + tile, BF16),
            vmem((2, ROWS, KVC), F32),
            vmem((N_CTX * REACH + 1, 2) + tile, BF16),
            vmem((2, N_CTX, 2) + tile, BF16),
            vmem((2, N_CTX, 2) + tile, BF16),
            vmem((N_Y, 2, N_X, W_X, ROWS), BF16),
            vmem((N_X, W_X, N_DP * ROWS), BF16),
            vmem((N_Y, W_X, N_DP * ROWS), BF16),
            vmem((CHUNKS, N_DP, ROWS, W_COL), BF16),
            vmem((CHUNKS, N_X, W_X, W_COL), BF16),
            vmem((CHUNKS, N_X, W_X, W_COL), BF16),
            vmem((CHUNKS, N_Z, PIECE, W_COL), BF16),
            vmem((CHUNKS, N_Z, PIECE, W_COL), BF16),
            dma((11,)),
            dma((N_CTX,)), dma((N_CTX,)),
            dma((2, N_PIECE)), dma((2, N_PIECE)),
            dma((2, N_PIECE)), dma((2, N_PIECE)),
            dma((2, N_CTX)), dma((2, N_CTX)),
            dma((N_DP,)), dma((N_DP,)),
            dma((N_DP,)), dma((N_DP,)),
            dma((CHUNKS, LINE)), dma((CHUNKS, N_DP)),
            dma((CHUNKS, N_DP)), dma((CHUNKS, N_DP)),
            dma((CHUNKS, N_X)), dma((CHUNKS, N_X)),
            dma((CHUNKS, N_Z)), dma((CHUNKS, N_Z)),
        ],
        compiler_params=pltpu.CompilerParams(
            collective_id=0, has_side_effects=True, vmem_limit_bytes=VMEM_LIMIT
        ),
        name="packed_backward",
    )(
        span_map, doc_lengths, jnp.asarray(rope_lanes()), jnp.asarray(feature_order(), BF16),
        queries, keys, values, grad_out, inputs,
    )


def solution(mesh):
    rows = P(("dp", "ctx"), None)
    return jax.shard_map(
        per_device,
        mesh=mesh,
        in_specs=(rows, rows, rows, rows, rows, P("dp", None), P("dp", None)),
        out_specs=(rows, rows),
        check_vma=False,
    )
```

```python
import functools

import jax
import jax.numpy as jnp
import numpy as np
from jax import lax
from jax.experimental import pallas as pl
from jax.experimental.pallas import tpu as pltpu
from jax.sharding import PartitionSpec as P

MESH = pl.DeviceIdType.MESH
BF16 = jnp.bfloat16
F32 = jnp.float32
I32 = jnp.int32

KVH = 4
G = 8
HD = 128
ROT = 64
ROPE_BASE = 10000000.0
SPAN = 64
BACK = 4
ROWS = 2 * SPAN
KEYS = (BACK + 1) * SPAN
N_CTX = 32
N_DP = 8
N_X = 4
N_Z = 8
SLOTS = 2 * N_CTX
NDOC = 32
KVC = KVH * HD
PIECE = 16
N_ROW = SPAN // PIECE
N_PIECE = N_ROW * KVH
REACH = 2 * BACK
DW = 3072
W_DP = DW // N_DP
W_DEV = W_DP // N_CTX
W_X = W_DP // N_X
CHUNKS = 4
W_COL = 2 * KVC // CHUNKS
N_Y = N_DP // 2
LINE = 4
MASKED = -1e30
SCALE = HD**-0.5
VMEM_LIMIT = 60 * 1024 * 1024

NT = (((1,), (1,)), ((), ()))
TN = (((0,), (0,)), ((), ()))


def rope_lanes():
    half = ROT // 2
    freq = ROPE_BASE ** (-(np.arange(half, dtype=np.float64) * 2.0 / ROT))
    return np.tile(freq.astype(np.float32), HD // half)[None]


def feature_order():
    order = np.arange(W_DP).reshape(N_Z, N_X, W_DEV).transpose(1, 0, 2).reshape(-1)
    return np.eye(W_DP, dtype=np.float32)[order]


def swap_halves(x):
    lane = lax.broadcasted_iota(I32, x.shape, 1)
    return jnp.where(lane < ROT // 2, pltpu.roll(x, HD - ROT // 2, 1), pltpu.roll(x, ROT // 2, 1))


def begin_of(pos, len_ref):
    def step(d, carry):
        start, begin = carry
        return start + len_ref[0, d], jnp.where(pos >= start, start, begin)

    _, begin = lax.fori_loop(0, NDOC, step, (jnp.int32(0), jnp.zeros_like(pos)), unroll=True)
    return begin


def loop(first, last, body):
    def step(k, carry):
        body(k)
        return carry

    lax.fori_loop(first, last, step, 0)


def remote(src, dst, send, recv, device):
    return pltpu.make_async_remote_copy(
        src_ref=src, dst_ref=dst, send_sem=send, recv_sem=recv, device_id=device, device_id_type=MESH
    )


def rope_tables(pos, lens, freq, cos, sin):
    rel = (pos - begin_of(pos, lens)).astype(F32)
    angle = rel * freq[...]
    packed_cos, packed_sin = jnp.cos(angle), jnp.sin(angle)
    lane = lax.broadcasted_iota(I32, pos.shape, 1)
    half, rows = ROT // 2, pos.shape[0]

    def turn(v, shift):
        shift = shift % HD
        return pltpu.roll(v, shift, 1) if shift else v

    for n in range(HD // half):
        pair = lambda v: (turn(v, -half * n), turn(v, half - half * n))
        (c0, c1), (s0, s1) = pair(packed_cos), pair(packed_sin)
        cos[n * rows : (n + 1) * rows] = jnp.where(lane < half, c0, jnp.where(lane < ROT, c1, 1.0))
        sin[n * rows : (n + 1) * rows] = jnp.where(lane < half, -s0, jnp.where(lane < ROT, s1, 0.0))


def settle(ref, sem):
    pltpu.make_async_copy(ref, ref, sem).wait()


def lanes(at, size):
    return pl.ds(pl.multiple_of(at, HD), size)


def kernel(
    span_h, len_h, freq_h, perm_h, q_h, k_h, v_h, do_h, in_h, dq_h, out_ref,
    span, lens, slot_of, take, give,
    slot_v, freq, perm, q, keys, vals, do, feats, cos, sin, bias, qrot, dq,
    pack, held, chosen, win, part, own, kept_k, kept_ds, landed, total, back, turned, xta, xtb,
    grads, wsend, wland, zsend, zland,
    local, send1, recv1, send2, recv2, send3, recv3, send4, recv4, send5, recv5, send0, recv0,
    send6, recv6, send7, recv7, send8, recv8, send9, recv9,
):
    dp, me = lax.axis_index("dp"), lax.axis_index("ctx")
    z, x = me // N_X, lax.rem(me, N_X)
    y, core = dp // 2, lax.rem(dp, 2)
    sib = dp + 1 - 2 * core
    team = core * N_X + x
    ctx_peer = lambda k: lax.rem(me + k, N_CTX)
    dp_peer = lambda k: lax.rem(dp + k, N_DP)
    y_peer = lambda k: lax.rem(dp + 2 * k, N_DP)
    x_peer = lambda k: lax.rem(x + k, N_X)
    team_peer = lambda k: lax.rem(team + k, 2 * N_X)
    z_peer = lambda k: lax.rem(z + k, N_Z)
    piece_here = lax.rem(z, N_ROW) * KVH + x

    def near(k):
        dz, dx = k // N_X, lax.rem(k, N_X)
        two = jnp.where(lax.rem(dx, 2) == 0, 2, N_Z - 2)
        return jnp.where(dz == 2, two, jnp.where(dz == 3, N_Z - 1, dz)), dx

    def reader(k):
        dz, dx = near(k)
        return lax.rem(z + dz, N_Z) * N_X + lax.rem(x + dx, N_X)

    def holder(k):
        dz, dx = near(k)
        return lax.rem(z + N_Z - dz, N_Z) * N_X + lax.rem(x + N_X - dx, N_X)

    def piece_of(device):
        return lax.rem(device, N_PIECE)

    fetches = [
        pltpu.make_async_copy(src, dst, local.at[n])
        for n, (src, dst) in enumerate([
            (k_h, keys), (v_h, vals), (span_h, span), (len_h, lens), (freq_h, freq),
            (perm_h, perm), (in_h, feats), (q_h, q), (do_h, do),
        ])
    ]
    for copy in fetches:
        copy.start()
    barrier = pltpu.get_barrier_semaphore()

    def greet(device):
        pl.semaphore_signal(barrier, inc=1, device_id=device, device_id_type=MESH)

    loop(1, N_CTX, lambda k: greet((dp, ctx_peer(k))))
    loop(1, N_DP, lambda k: greet((dp_peer(k), me)))
    loop(1, N_X, lambda k: greet((sib, z * N_X + x_peer(k))))
    for copy in fetches[:2]:
        copy.wait()
    for s in range(2):
        for r in range(N_ROW):
            rows = slice(s * SPAN + r * PIECE, s * SPAN + (r + 1) * PIECE)
            for j in range(KVH):
                cols = slice(j * HD, (j + 1) * HD)
                pack[r * KVH + j, s, 0] = keys[rows, cols]
                pack[r * KVH + j, s, 1] = vals[rows, cols]
    pl.semaphore_wait(barrier, N_CTX - 1 + N_DP - 1 + N_X - 1)

    def copy1(src, owner, peer):
        return remote(
            pack.at[piece_of(src)], held.at[pl.ds(2 * owner, 2)], send1, recv1, (dp, peer)
        )

    loop(1, N_CTX, lambda k: copy1(ctx_peer(k), me, ctx_peer(k)).start())
    held[pl.ds(2 * me, 2)] = pack[piece_here]

    def copy5(peer):
        return remote(
            turned.at[peer // 2, lax.rem(peer, 2)],
            xta.at[:, :, lanes((core * N_Y + y) * ROWS, ROWS)],
            send5,
            recv5,
            (peer, me),
        )

    def copy0(peer):
        return remote(
            turned.at[:, peer // N_X, lax.rem(peer, N_X)],
            xtb.at[:, :, lanes(team * ROWS, ROWS)],
            send0,
            recv0,
            (dp - core + peer // N_X, z * N_X + lax.rem(peer, N_X)),
        )

    fetches[5].wait()
    fetches[6].wait()
    for d in range(N_DP):
        w = lax.dot_general(perm[...], feats[:, d * W_DP : (d + 1) * W_DP], NT, preferred_element_type=F32)
        turned[d // 2, d % 2] = w.astype(BF16).reshape(N_X, W_X, ROWS)
    loop(1, N_DP, lambda k: copy5(dp_peer(k)).start())
    loop(1, 2 * N_X, lambda k: copy0(team_peer(k)).start())
    xta[:, :, lanes((core * N_Y + y) * ROWS, ROWS)] = turned[y, core]
    xtb[:, :, lanes(team * ROWS, ROWS)] = turned[:, core, x]

    for copy in fetches[2:5]:
        copy.wait()
    lane_row = lax.broadcasted_iota(I32, (1, HD), 1)
    slots = jnp.zeros((1, HD), I32)
    for n in range(SLOTS):
        slots = jnp.where(lane_row == span[0, n], n, slots)
    slot_v[...] = slots
    slot_copy = pltpu.make_async_copy(slot_v, slot_of, local.at[9])
    slot_copy.start()
    mine = (span[0, 2 * me], span[0, 2 * me + 1])
    for s in range(2):
        own_rows = SPAN // 4
        row = lax.broadcasted_iota(I32, (own_rows, HD), 0)
        group = lax.broadcasted_iota(I32, (own_rows, HD), 1) >> 5
        at = pl.ds(BACK * SPAN, SPAN)
        rope_tables(mine[s] * SPAN + group * own_rows + row, lens, freq, cos.at[s, at], sin.at[s, at])
        row = lax.broadcasted_iota(I32, (SPAN, HD), 0)
        group = lax.broadcasted_iota(I32, (SPAN, HD), 1) >> 5
        pos = (mine[s] - BACK + (row >> 4)) * SPAN + group * PIECE + (row & 15)
        at = pl.ds(0, BACK * SPAN)
        rope_tables(pos, lens, freq, cos.at[s, at], sin.at[s, at])
    slot_copy.wait()

    def fill(slot):
        at = span[0, slot]
        for w in range(BACK):
            take[slot * BACK + w] = slot_of[0, jnp.maximum(at - BACK + w, 0)]
            later = at + 1 + w
            source = slot_of[0, jnp.minimum(later, SLOTS - 1)] * BACK + (BACK - 1 - w)
            give[slot * BACK + w] = jnp.where(later < SLOTS, source, N_CTX * REACH)

    loop(0, SLOTS, fill)
    for s in range(2):
        lane8 = lax.broadcasted_iota(I32, (8, HD), 1)
        qpos = mine[s] * SPAN + jnp.where(lane8 >= SPAN, lane8 - SPAN, lane8)
        qbegin = begin_of(qpos, lens)
        n = lax.broadcasted_iota(I32, (KEYS, HD), 0)
        r, w, t = n >> 6, (n >> 4) & 3, n & 15
        earlier = (mine[s] - BACK + w) * SPAN + r * PIECE + t
        kpos = jnp.where(n < BACK * SPAN, earlier, mine[s] * SPAN + (n - BACK * SPAN))
        allowed = (kpos <= qpos[0:1]) & (kpos >= qbegin[0:1])
        bias[s] = jnp.where(allowed, 0.0, MASKED)
    fetches[7].wait()

    def rotate(h):
        for s in range(2):
            rows = slice(s * SPAN, (s + 1) * SPAN)
            v = q[rows, lanes(h * HD, HD)].astype(F32)
            v = v * cos[s, BACK * SPAN :] + swap_halves(v) * sin[s, BACK * SPAN :]
            qrot[rows, lanes(h * HD, HD)] = v.astype(BF16)

    loop(0, KVH * G, rotate)
    empty = jnp.zeros((REACH, 2, PIECE, HD), BF16)

    def clear(dz, dx):
        device = lax.rem(z + dz, N_Z) * N_X + lax.rem(x + dx, N_X)
        landed[pl.ds(REACH * device, REACH)] = empty

    loop(0, 12, lambda k: clear(3 + k // N_X, lax.rem(k, N_X)))
    loop(0, 2, lambda k: clear(2, 2 * k + 1))
    loop(0, 2, lambda k: clear(6, 2 * k))
    landed[N_CTX * REACH] = jnp.zeros((2, PIECE, HD), BF16)
    settle(held.at[pl.ds(0, 2 * (N_CTX - 1))], recv1)

    def choose(s, k):
        device = reader(k)
        for w in range(BACK):
            chosen[s, k, w] = held[take[device * REACH + s * BACK + w]]

    def copy2(s, k, peer, piece):
        return remote(chosen.at[s, k], win.at[s, piece], send2, recv2.at[s], (dp, peer))

    for s in range(2):

        def serve(k, s=s):
            choose(s, k)
            copy2(s, k, reader(k), piece_here).start()

        loop(1, N_PIECE, serve)
        choose(s, 0)
        win[s, piece_here] = chosen[s, 0]
    fetches[8].wait()

    def copy3(s, k, src, owner, peer):
        return remote(
            part.at[s, src],
            landed.at[pl.ds(REACH * owner + BACK * s, BACK)],
            send3,
            recv3,
            (dp, peer),
        )

    for s in range(2):
        settle(win.at[s, pl.ds(0, N_PIECE - 1)], recv2.at[s])
        rows = slice(s * SPAN, (s + 1) * SPAN)

        def attend(n, s=s, rows=rows):
            j = lax.rem(x + n, KVH)

            def window(kind):
                parts = [win[s, r * KVH + j, :, kind].reshape(BACK * PIECE, HD) for r in range(N_ROW)]
                parts += [pack[r * KVH + j, s, kind] for r in range(N_ROW)]
                return jnp.concatenate(parts, axis=0)

            def stacked(ref):
                parts = [ref[rows, lanes((j * G + g) * HD, HD)] for g in range(G)]
                return jnp.concatenate(parts, axis=0)

            k, v = window(0).astype(F32), window(1)
            k = (k * cos[s] + swap_halves(k) * sin[s]).astype(BF16)
            qs, dos = stacked(qrot), stacked(do)
            mask = jnp.concatenate([bias[s]] * (G * SPAN // HD), axis=1)
            scores = lax.dot_general(k, qs, NT, preferred_element_type=F32)
            scores = scores * (SCALE * float(np.log2(np.e))) + mask
            weight = jnp.exp2(scores - jnp.max(scores, axis=0, keepdims=True))
            probs = weight * (1.0 / jnp.sum(weight, axis=0, keepdims=True))
            dprobs = lax.dot_general(v, dos, NT, preferred_element_type=F32)
            delta = jnp.sum(probs * dprobs, axis=0, keepdims=True)
            dscores = (probs * (dprobs - delta)).astype(BF16)
            low = probs.astype(BF16)
            dk = jnp.dot(dscores, qs, preferred_element_type=F32) * SCALE
            dv = jnp.dot(low, dos, preferred_element_type=F32)
            for kind, grad in ((0, dk), (1, dv)):
                earlier = grad[: BACK * SPAN].astype(BF16).reshape(N_ROW, BACK, PIECE, HD)
                for r in range(N_ROW):
                    part[s, r * KVH + j, :, kind] = earlier[r]
                own[kind, rows, lanes(j * HD, HD)] = grad[BACK * SPAN :]
            dx = lax.rem(N_X - n, N_X)

            def hand_over(dz):
                at = dz * N_X + dx

                @pl.when(at > 0)
                def _():
                    copy3(s, at, piece_of(holder(at)), me, holder(at)).start()

            loop(0, N_ROW, hand_over)
            kept_k[s, j] = k
            kept_ds[s, j] = dscores

        loop(0, KVH, attend)
        landed[pl.ds(REACH * me + BACK * s, BACK)] = part[s, piece_here]

    def query_grads(j):
        for s in range(2):
            rows = slice(s * SPAN, (s + 1) * SPAN)
            across_keys = lax.dot_general(kept_k[s, j], kept_ds[s, j], TN, preferred_element_type=F32)
            upright = across_keys.T * SCALE
            for g in range(G):
                u = upright[g * SPAN : (g + 1) * SPAN]
                u = u * cos[s, BACK * SPAN :] - swap_halves(u) * sin[s, BACK * SPAN :]
                dq[rows, lanes((j * G + g) * HD, HD)] = u.astype(BF16)

    loop(0, KVH, query_grads)
    dq_copy = pltpu.make_async_copy(dq, dq_h, local.at[10])
    dq_copy.start()
    settle(landed.at[pl.ds(0, REACH * (N_PIECE - 1))], recv3)

    def copy4(kind, src, owner, peer):
        return remote(
            total.at[kind, src], back.at[kind, owner], send4, recv4.at[kind], (dp, peer)
        )

    def sum_up(kind, device):
        for s in range(2):
            at = (2 * device + s) * BACK
            acc = landed[give[at], kind].astype(F32)
            for w in range(1, BACK):
                acc += landed[give[at + w], kind].astype(F32)
            total[kind, device, s] = acc.astype(BF16)

    for kind in range(2):

        def give_back(k, kind=kind):
            sum_up(kind, ctx_peer(k))
            copy4(kind, ctx_peer(k), me, ctx_peer(k)).start()

        loop(1, N_CTX, give_back)
        sum_up(kind, me)
        back[kind, me] = total[kind, me]

    def line(half, k):
        return (y_peer(k), me) if half == 0 else (dp, z * N_X + x_peer(k))

    place = lambda c: (y, x)[c % 2]
    far_place = lambda c: (x, y)[c % 2]

    def copy6(c, k):
        mine = grads.at[c, core, place(c)]
        return remote(mine, mine, send6, recv6.at[c], line(c % 2, k))

    def copy7(c):
        return remote(grads.at[c, core], grads.at[c, core], send7, recv7.at[c], (sib, me))

    def assemble(c):
        kind, half = c // 2, c % 2
        for n in range(2):
            j = 2 * half + n
            for r in range(N_ROW):
                for s in range(2):
                    rows = slice(s * SPAN + r * PIECE, s * SPAN + (r + 1) * PIECE)
                    piece = r * KVH + j
                    g = back[kind, piece, s].astype(F32) + back[kind, N_PIECE + piece, s].astype(F32)
                    g += own[kind, rows, j * HD : (j + 1) * HD]
                    if kind == 0:
                        at = slice(BACK * SPAN + r * PIECE, BACK * SPAN + (r + 1) * PIECE)
                        g = g * cos[s, at] - swap_halves(g) * sin[s, at]
                    grads[c, core, place(c), rows, n * HD : (n + 1) * HD] = g.astype(BF16)
        loop(1, LINE, lambda k: copy6(c, k).start())

    def forward(c):
        settle(grads.at[c, 0, pl.ds(0, LINE - 1)], recv6.at[c])
        copy7(c).start()

    def rest(half, k):
        if half == 0:
            return x_peer(k), (dp, z * N_X + x_peer(k))
        return y_peer(k) // 2, (y_peer(k), me)

    def copy8(c, k):
        src, device = rest(c % 2, k)
        return remote(wsend.at[c, src], wland.at[c, far_place(c)], send8, recv8.at[c], device)

    def copy9(c, peer):
        return remote(zsend.at[c, peer], zland.at[c, z], send9, recv9.at[c], (dp, peer * N_X + x))

    def multiply(c):
        settle(grads.at[c, 0], recv7.at[c])
        xt = (xta, xtb)[c % 2][...].reshape(W_DP, N_DP * ROWS)
        w = jnp.dot(xt, grads[c].reshape(N_DP * ROWS, W_COL), preferred_element_type=F32)
        wsend[c] = w.astype(BF16).reshape(LINE, W_X, W_COL)
        loop(1, LINE, lambda k: copy8(c, k).start())
        wland[c, far_place(c)] = wsend[c, far_place(c)]

    def sum_line(c):
        settle(wland.at[c, pl.ds(0, LINE - 1)], recv8.at[c])
        acc = wland[c, 0].astype(F32)
        for n in range(1, LINE):
            acc += wland[c, n].astype(F32)
        pad = jnp.zeros((PIECE - W_DEV, W_COL), F32)
        for n in range(N_Z):
            block = jnp.concatenate([acc[n * W_DEV : (n + 1) * W_DEV], pad], axis=0)
            zsend[c, n] = block.astype(BF16)
        loop(1, N_Z, lambda k: copy9(c, z_peer(k)).start())
        zland[c, z] = zsend[c, z]

    def sum_z(c):
        settle(zland.at[c, pl.ds(0, N_Z - 1)], recv9.at[c])
        acc = zland[c, 0].astype(F32)
        for n in range(1, N_Z):
            acc += zland[c, n].astype(F32)
        out_ref[:, c * W_COL : (c + 1) * W_COL] = acc[:W_DEV]

    settle(xta.at[:, :, pl.ds(0, (N_DP - 1) * ROWS)], recv5)
    settle(xtb.at[:, :, pl.ds(0, (N_DP - 1) * ROWS)], recv0)
    settle(back.at[0, pl.ds(0, N_CTX - 1)], recv4.at[0])
    assemble(0)
    assemble(1)
    settle(back.at[1, pl.ds(0, N_CTX - 1)], recv4.at[1])
    assemble(2)
    assemble(3)
    forward(0)
    forward(1)
    multiply(0)
    multiply(1)
    forward(2)
    forward(3)
    multiply(2)
    multiply(3)
    for c in range(CHUNKS):
        sum_line(c)
    for c in range(CHUNKS):
        sum_z(c)

    settle(held.at[pl.ds(0, 2 * (N_CTX - 1))], send1)
    settle(xta.at[:, :, pl.ds(0, (N_DP - 1) * ROWS)], send5)
    settle(xtb.at[:, :, pl.ds(0, (N_DP - 1) * ROWS)], send0)
    settle(chosen.at[:, pl.ds(0, N_PIECE - 1)], send2)
    settle(part.at[:, pl.ds(0, N_PIECE - 1)], send3)
    settle(total.at[:, pl.ds(0, N_CTX - 1)], send4)
    settle(grads.at[:, 0, pl.ds(0, LINE - 1)], send6)
    settle(grads.at[:, 0], send7)
    settle(wsend.at[:, pl.ds(0, LINE - 1)], send8)
    settle(zsend.at[:, pl.ds(0, N_Z - 1)], send9)
    dq_copy.wait()


def per_device(queries, keys, values, grad_out, inputs, span_map, doc_lengths):
    vmem, smem, dma = pltpu.VMEM, pltpu.SMEM, pltpu.SemaphoreType.DMA
    hbm = pl.BlockSpec(memory_space=pl.ANY)
    wide = KVH * G * HD
    tile = (PIECE, HD)
    return pl.pallas_call(
        kernel,
        out_shape=[
            jax.ShapeDtypeStruct((ROWS, wide), BF16),
            jax.ShapeDtypeStruct((W_DEV, 2 * KVC), F32),
        ],
        in_specs=[hbm] * 9,
        out_specs=[hbm, pl.BlockSpec(memory_space=pltpu.VMEM)],
        scratch_shapes=[
            smem((1, SLOTS), I32),
            smem((1, NDOC), I32),
            smem((1, HD), I32),
            smem((SLOTS * BACK,), I32),
            smem((SLOTS * BACK,), I32),
            vmem((1, HD), I32),
            vmem((1, HD), F32),
            vmem((W_DP, W_DP), BF16),
            vmem((ROWS, wide), BF16),
            vmem((ROWS, KVC), BF16),
            vmem((ROWS, KVC), BF16),
            vmem((ROWS, wide), BF16),
            vmem((ROWS, DW), BF16),
            vmem((2, KEYS, HD), F32),
            vmem((2, KEYS, HD), F32),
            vmem((2, KEYS, HD), F32),
            vmem((ROWS, wide), BF16),
            vmem((ROWS, wide), BF16),
            vmem((N_PIECE, 2, 2) + tile, BF16),
            vmem((SLOTS, 2) + tile, BF16),
            vmem((2, N_PIECE, BACK, 2) + tile, BF16),
            vmem((2, N_PIECE, BACK, 2) + tile, BF16),
            vmem((2, N_PIECE, BACK, 2) + tile, BF16),
            vmem((2, ROWS, KVC), F32),
            vmem((2, KVH, KEYS, HD), BF16),
            vmem((2, KVH, KEYS, G * SPAN), BF16),
            vmem((N_CTX * REACH + 1, 2) + tile, BF16),
            vmem((2, N_CTX, 2) + tile, BF16),
            vmem((2, N_CTX, 2) + tile, BF16),
            vmem((N_Y, 2, N_X, W_X, ROWS), BF16),
            vmem((N_X, W_X, N_DP * ROWS), BF16),
            vmem((N_Y, W_X, N_DP * ROWS), BF16),
            vmem((CHUNKS, 2, LINE, ROWS, W_COL), BF16),
            vmem((CHUNKS, N_X, W_X, W_COL), BF16),
            vmem((CHUNKS, N_X, W_X, W_COL), BF16),
            vmem((CHUNKS, N_Z, PIECE, W_COL), BF16),
            vmem((CHUNKS, N_Z, PIECE, W_COL), BF16),
            dma((11,)),
            dma, dma,
            dma, dma((2,)),
            dma, dma,
            dma, dma((2,)),
            dma, dma,
            dma, dma,
            dma, dma((CHUNKS,)),
            dma, dma((CHUNKS,)),
            dma, dma((CHUNKS,)),
            dma, dma((CHUNKS,)),
        ],
        compiler_params=pltpu.CompilerParams(
            collective_id=0, has_side_effects=True, vmem_limit_bytes=VMEM_LIMIT
        ),
        name="packed_backward",
    )(
        span_map, doc_lengths, jnp.asarray(rope_lanes()), jnp.asarray(feature_order(), BF16),
        queries, keys, values, grad_out, inputs,
    )


def solution(mesh):
    rows = P(("dp", "ctx"), None)
    return jax.shard_map(
        per_device,
        mesh=mesh,
        in_specs=(rows, rows, rows, rows, rows, P("dp", None), P("dp", None)),
        out_specs=(rows, rows),
        check_vma=False,
    )
```

```python
import functools

import jax
import jax.numpy as jnp
import numpy as np
from jax import lax
from jax.experimental import pallas as pl
from jax.experimental.pallas import tpu as pltpu
from jax.sharding import PartitionSpec as P

MESH = pl.DeviceIdType.MESH
BF16 = jnp.bfloat16
F32 = jnp.float32
I32 = jnp.int32

KVH = 4
G = 8
HD = 128
ROT = 64
ROPE_BASE = 10000000.0
SPAN = 64
BACK = 4
ROWS = 2 * SPAN
KEYS = (BACK + 1) * SPAN
N_CTX = 32
N_DP = 8
N_X = 4
N_Z = 8
SLOTS = 2 * N_CTX
NDOC = 32
KVC = KVH * HD
PIECE = 16
N_ROW = SPAN // PIECE
N_PIECE = N_ROW * KVH
REACH = 2 * BACK
DW = 3072
W_DP = DW // N_DP
W_DEV = W_DP // N_CTX
W_X = W_DP // N_X
CHUNKS = 4
HEADS = 2 * KVH // CHUNKS
W_COL = 2 * KVC // CHUNKS
N_Y = N_DP // 2
LINE = 4
MASKED = -1e30
SCALE = HD**-0.5
VMEM_LIMIT = 60 * 1024 * 1024

NT = (((1,), (1,)), ((), ()))
TN = (((0,), (0,)), ((), ()))


def rope_lanes():
    half = ROT // 2
    freq = ROPE_BASE ** (-(np.arange(half, dtype=np.float64) * 2.0 / ROT))
    return np.tile(freq.astype(np.float32), HD // half)[None]


def feature_order():
    order = np.arange(W_DP).reshape(N_Z, N_X, W_DEV).transpose(1, 0, 2).reshape(-1)
    return np.eye(W_DP, dtype=np.float32)[order]


def swap_halves(x):
    lane = lax.broadcasted_iota(I32, x.shape, 1)
    return jnp.where(lane < ROT // 2, pltpu.roll(x, HD - ROT // 2, 1), pltpu.roll(x, ROT // 2, 1))


def begin_of(pos, len_ref):
    def step(d, carry):
        start, begin = carry
        return start + len_ref[0, d], jnp.where(pos >= start, start, begin)

    _, begin = lax.fori_loop(0, NDOC, step, (jnp.int32(0), jnp.zeros_like(pos)), unroll=True)
    return begin


def loop(first, last, body):
    def step(k, carry):
        body(k)
        return carry

    lax.fori_loop(first, last, step, 0)


def remote(src, dst, send, recv, device):
    return pltpu.make_async_remote_copy(
        src_ref=src, dst_ref=dst, send_sem=send, recv_sem=recv, device_id=device, device_id_type=MESH
    )


def rope_tables(pos, lens, freq, cos, sin):
    rel = (pos - begin_of(pos, lens)).astype(F32)
    angle = rel * freq[...]
    packed_cos, packed_sin = jnp.cos(angle), jnp.sin(angle)
    lane = lax.broadcasted_iota(I32, pos.shape, 1)
    half, rows = ROT // 2, pos.shape[0]

    def turn(v, shift):
        shift = shift % HD
        return pltpu.roll(v, shift, 1) if shift else v

    for n in range(HD // half):
        pair = lambda v: (turn(v, -half * n), turn(v, half - half * n))
        (c0, c1), (s0, s1) = pair(packed_cos), pair(packed_sin)
        cos[n * rows : (n + 1) * rows] = jnp.where(lane < half, c0, jnp.where(lane < ROT, c1, 1.0))
        sin[n * rows : (n + 1) * rows] = jnp.where(lane < half, -s0, jnp.where(lane < ROT, s1, 0.0))


def settle(ref, sem):
    pltpu.make_async_copy(ref, ref, sem).wait()


def lanes(at, size):
    return pl.ds(pl.multiple_of(at, HD), size)


def kernel(
    span_h, len_h, freq_h, perm_h, q_h, k_h, v_h, do_h, in_h, dq_h, out_ref,
    span, lens, slot_of, take, give,
    slot_v, freq, perm, q, keys, vals, do, feats, cos, sin, bias, qrot, dq,
    pack, held_k, held_v, chosen, win, part, own, kept_k, kept_ds, landed_k, landed_v, total, back, turned, xt,
    grads, wsend, wland, zsend, zland,
    local, send1, recv1, send2, recv2, send3, recv3, send4, recv4, send5, recv5,
    send6, recv6, send7, recv7, send8, recv8, send9, recv9,
):
    dp, me = lax.axis_index("dp"), lax.axis_index("ctx")
    z, x = me // N_X, lax.rem(me, N_X)
    y, core = dp // 2, lax.rem(dp, 2)
    sib = dp + 1 - 2 * core
    ctx_peer = lambda k: lax.rem(me + k, N_CTX)
    def far_peer(k):
        n = N_CTX - 1 - k
        step = n // 2 + 1
        return ctx_peer(jnp.where(lax.rem(n, 2) == 0, step, N_CTX - step))

    dp_peer = lambda k: lax.rem(dp + k, N_DP)
    y_peer = lambda k: lax.rem(dp + 2 * k, N_DP)
    x_peer = lambda k: lax.rem(x + k, N_X)
    z_peer = lambda k: lax.rem(z + k, N_Z)
    piece_here = lax.rem(z, N_ROW) * KVH + x

    def near(k):
        dz, dx = k // N_X, lax.rem(k, N_X)
        two = jnp.where(lax.rem(dx, 2) == 0, 2, N_Z - 2)
        return jnp.where(dz == 2, two, jnp.where(dz == 3, N_Z - 1, dz)), dx

    def reader(k):
        dz, dx = near(k)
        return lax.rem(z + dz, N_Z) * N_X + lax.rem(x + dx, N_X)

    def holder(k):
        dz, dx = near(k)
        return lax.rem(z + N_Z - dz, N_Z) * N_X + lax.rem(x + N_X - dx, N_X)

    def piece_of(device):
        return lax.rem(device, N_PIECE)

    held, landed = (held_k, held_v), (landed_k, landed_v)

    fetches = [
        pltpu.make_async_copy(src, dst, local.at[n])
        for n, (src, dst) in enumerate([
            (k_h, keys), (v_h, vals), (span_h, span), (len_h, lens), (freq_h, freq),
            (perm_h, perm), (in_h, feats), (q_h, q), (do_h, do),
        ])
    ]
    for copy in fetches:
        copy.start()
    barrier = pltpu.get_barrier_semaphore()

    def greet(device):
        pl.semaphore_signal(barrier, inc=1, device_id=device, device_id_type=MESH)

    loop(1, N_CTX, lambda k: greet((dp, ctx_peer(k))))
    loop(1, N_DP, lambda k: greet((dp_peer(k), me)))
    for copy in fetches[:2]:
        copy.wait()
    for s in range(2):
        for r in range(N_ROW):
            rows = slice(s * SPAN + r * PIECE, s * SPAN + (r + 1) * PIECE)
            for j in range(KVH):
                cols = slice(j * HD, (j + 1) * HD)
                pack[0, r * KVH + j, s] = keys[rows, cols]
                pack[1, r * KVH + j, s] = vals[rows, cols]
    pl.semaphore_wait(barrier, N_CTX - 1 + N_DP - 1)

    def copy1(kind, peer):
        return remote(
            pack.at[kind, piece_of(peer)], held[kind].at[pl.ds(2 * me, 2)], send1.at[kind], recv1.at[kind], (dp, peer)
        )

    def spread(kind):
        loop(1, N_CTX, lambda k: copy1(kind, far_peer(k)).start())
        held[kind][pl.ds(2 * me, 2)] = pack[kind, piece_here]

    spread(0)

    def copy5(peer):
        return remote(
            turned.at[peer],
            xt.at[:, lanes((core * N_Y + y) * ROWS, ROWS)],
            send5,
            recv5,
            (peer, me),
        )

    fetches[5].wait()
    fetches[6].wait()
    for d in range(N_DP):
        w = lax.dot_general(perm[...], feats[:, d * W_DP : (d + 1) * W_DP], NT, preferred_element_type=F32)
        turned[d] = w.astype(BF16)
    loop(1, N_DP, lambda k: copy5(dp_peer(k)).start())
    xt[:, lanes((core * N_Y + y) * ROWS, ROWS)] = turned[dp]

    for copy in fetches[2:5]:
        copy.wait()
    lane_row = lax.broadcasted_iota(I32, (1, HD), 1)
    slots = jnp.zeros((1, HD), I32)
    for n in range(SLOTS):
        slots = jnp.where(lane_row == span[0, n], n, slots)
    slot_v[...] = slots
    slot_copy = pltpu.make_async_copy(slot_v, slot_of, local.at[9])
    slot_copy.start()
    mine = (span[0, 2 * me], span[0, 2 * me + 1])
    for s in range(2):
        own_rows = SPAN // 4
        row = lax.broadcasted_iota(I32, (own_rows, HD), 0)
        group = lax.broadcasted_iota(I32, (own_rows, HD), 1) >> 5
        at = pl.ds(BACK * SPAN, SPAN)
        rope_tables(mine[s] * SPAN + group * own_rows + row, lens, freq, cos.at[s, at], sin.at[s, at])
        row = lax.broadcasted_iota(I32, (SPAN, HD), 0)
        group = lax.broadcasted_iota(I32, (SPAN, HD), 1) >> 5
        pos = (mine[s] - BACK + (row >> 4)) * SPAN + group * PIECE + (row & 15)
        at = pl.ds(0, BACK * SPAN)
        rope_tables(pos, lens, freq, cos.at[s, at], sin.at[s, at])
    slot_copy.wait()
    settle(held[0].at[pl.ds(0, 2 * (N_CTX - 1))], send1.at[0])
    spread(1)

    def fill(slot):
        at = span[0, slot]
        for w in range(BACK):
            take[slot * BACK + w] = slot_of[0, jnp.maximum(at - BACK + w, 0)]
            later = at + 1 + w
            source = slot_of[0, jnp.minimum(later, SLOTS - 1)] * BACK + (BACK - 1 - w)
            give[slot * BACK + w] = jnp.where(later < SLOTS, source, N_CTX * REACH)

    loop(0, SLOTS, fill)
    for s in range(2):
        lane8 = lax.broadcasted_iota(I32, (8, HD), 1)
        qpos = mine[s] * SPAN + jnp.where(lane8 >= SPAN, lane8 - SPAN, lane8)
        qbegin = begin_of(qpos, lens)
        n = lax.broadcasted_iota(I32, (KEYS, HD), 0)
        r, w, t = n >> 6, (n >> 4) & 3, n & 15
        earlier = (mine[s] - BACK + w) * SPAN + r * PIECE + t
        kpos = jnp.where(n < BACK * SPAN, earlier, mine[s] * SPAN + (n - BACK * SPAN))
        allowed = (kpos <= qpos[0:1]) & (kpos >= qbegin[0:1])
        bias[s] = jnp.where(allowed, 0.0, MASKED)
    fetches[7].wait()

    def rotate(h):
        for s in range(2):
            rows = slice(s * SPAN, (s + 1) * SPAN)
            v = q[rows, lanes(h * HD, HD)].astype(F32)
            v = v * cos[s, BACK * SPAN :] + swap_halves(v) * sin[s, BACK * SPAN :]
            qrot[rows, lanes(h * HD, HD)] = v.astype(BF16)

    loop(0, KVH * G, rotate)
    empty = jnp.zeros((REACH, PIECE, HD), BF16)

    def clear(dz, dx):
        device = lax.rem(z + dz, N_Z) * N_X + lax.rem(x + dx, N_X)
        for side in landed:
            side[pl.ds(REACH * device, REACH)] = empty

    loop(0, 12, lambda k: clear(3 + k // N_X, lax.rem(k, N_X)))
    loop(0, 2, lambda k: clear(2, 2 * k + 1))
    loop(0, 2, lambda k: clear(6, 2 * k))
    for side in landed:
        side[N_CTX * REACH] = jnp.zeros((PIECE, HD), BF16)

    def choose(kind, s, k):
        device = reader(k)
        for w in range(BACK):
            chosen[kind, s, k, w] = held[kind][take[device * REACH + s * BACK + w]]

    def copy2(kind, s, k):
        return remote(
            chosen.at[kind, s, k], win.at[kind, s, piece_here], send2, recv2.at[s], (dp, reader(k))
        )

    for kind in range(2):
        settle(held[kind].at[pl.ds(0, 2 * (N_CTX - 1))], recv1.at[kind])
        for s in range(2):

            def serve(k, kind=kind, s=s):
                k = 1 + lax.rem(k + 6, N_PIECE - 1)
                choose(kind, s, k)
                copy2(kind, s, k).start()

            loop(1, N_PIECE, serve)
            choose(kind, s, 0)
            win[kind, s, piece_here] = chosen[kind, s, 0]
    fetches[8].wait()

    def copy3(kind, s, k):
        return remote(
            part.at[kind, s, piece_of(holder(k))],
            landed[kind].at[pl.ds(REACH * me + BACK * s, BACK)],
            send3,
            recv3.at[kind],
            (dp, holder(k)),
        )

    def hand_over(kind, s, n, grad):
        j = lax.rem(x + n, KVH)
        earlier = grad[: BACK * SPAN].astype(BF16).reshape(N_ROW, BACK, PIECE, HD)
        for r in range(N_ROW):
            part[kind, s, r * KVH + j] = earlier[r]
        own[kind, s * SPAN : (s + 1) * SPAN, lanes(j * HD, HD)] = grad[BACK * SPAN :]

        def send(dz):
            at = dz * N_X + lax.rem(N_X - n, N_X)

            @pl.when(at > 0)
            def _():
                copy3(kind, s, at).start()

        loop(0, N_ROW, send)

    def stacked(ref, s, j):
        rows = slice(s * SPAN, (s + 1) * SPAN)
        return jnp.concatenate([ref[rows, lanes((j * G + g) * HD, HD)] for g in range(G)], axis=0)

    for s in range(2):
        settle(win.at[:, s, pl.ds(0, N_PIECE - 1)], recv2.at[s])

        def attend(n, s=s):
            j = lax.rem(x + n, KVH)

            def window(kind):
                parts = [win[kind, s, r * KVH + j].reshape(BACK * PIECE, HD) for r in range(N_ROW)]
                parts += [pack[kind, r * KVH + j, s] for r in range(N_ROW)]
                return jnp.concatenate(parts, axis=0)

            k, v = window(0).astype(F32), window(1)
            k = (k * cos[s] + swap_halves(k) * sin[s]).astype(BF16)
            qs, dos = stacked(qrot, s, j), stacked(do, s, j)
            mask = jnp.concatenate([bias[s]] * (G * SPAN // HD), axis=1)
            scores = lax.dot_general(k, qs, NT, preferred_element_type=F32)
            scores = scores * (SCALE * float(np.log2(np.e))) + mask
            weight = jnp.exp2(scores - jnp.max(scores, axis=0, keepdims=True))
            probs = weight * (1.0 / jnp.sum(weight, axis=0, keepdims=True))
            dprobs = lax.dot_general(v, dos, NT, preferred_element_type=F32)
            delta = jnp.sum(probs * dprobs, axis=0, keepdims=True)
            dscores = (probs * (dprobs - delta)).astype(BF16)
            low = probs.astype(BF16)
            hand_over(1, s, n, jnp.dot(low, dos, preferred_element_type=F32))
            kept_k[s, j] = k
            kept_ds[s, j] = dscores

        def key_part(n, s=s):
            j = lax.rem(x + n, KVH)
            dk = jnp.dot(kept_ds[s, j], stacked(qrot, s, j), preferred_element_type=F32)
            hand_over(0, s, n, dk * SCALE)

        loop(0, KVH, attend)
        loop(0, KVH, key_part)
        for kind in range(2):
            landed[kind][pl.ds(REACH * me + BACK * s, BACK)] = part[kind, s, piece_here]

    def query_grads(j):
        for s in range(2):
            rows = slice(s * SPAN, (s + 1) * SPAN)
            across_keys = lax.dot_general(kept_k[s, j], kept_ds[s, j], TN, preferred_element_type=F32)
            upright = across_keys.T * SCALE
            for g in range(G):
                u = upright[g * SPAN : (g + 1) * SPAN]
                u = u * cos[s, BACK * SPAN :] - swap_halves(u) * sin[s, BACK * SPAN :]
                dq[rows, lanes((j * G + g) * HD, HD)] = u.astype(BF16)

    loop(0, KVH, query_grads)
    dq_copy = pltpu.make_async_copy(dq, dq_h, local.at[10])
    dq_copy.start()

    def copy4(kind, src, owner, peer):
        return remote(
            total.at[kind, src], back.at[kind, owner], send4, recv4.at[kind], (dp, peer)
        )

    def sum_up(kind, device):
        for s in range(2):
            at = (2 * device + s) * BACK
            acc = landed[kind][give[at]].astype(F32)
            for w in range(1, BACK):
                acc += landed[kind][give[at + w]].astype(F32)
            total[kind, device, s] = acc.astype(BF16)

    for kind in (1, 0):
        settle(landed[kind].at[pl.ds(0, REACH * (N_PIECE - 1))], recv3.at[kind])

        def give_back(k, kind=kind):
            sum_up(kind, far_peer(k))
            copy4(kind, far_peer(k), me, far_peer(k)).start()

        loop(1, N_CTX, give_back)
        sum_up(kind, me)
        back[kind, me] = total[kind, me]

    def copy6(c, k):
        mine = grads.at[c, core, y]
        return remote(mine, mine, send6, recv6.at[c], (y_peer(k), me))

    def copy7(c):
        return remote(grads.at[c, core], grads.at[c, core], send7, recv7.at[c], (sib, me))

    def assemble(c):
        kind = c * HEADS // KVH
        for n in range(HEADS):
            j = (c * HEADS + n) % KVH
            for r in range(N_ROW):
                for s in range(2):
                    rows = slice(s * SPAN + r * PIECE, s * SPAN + (r + 1) * PIECE)
                    piece = r * KVH + j
                    g = back[kind, piece, s].astype(F32) + back[kind, N_PIECE + piece, s].astype(F32)
                    g += own[kind, rows, j * HD : (j + 1) * HD]
                    if kind == 0:
                        at = slice(BACK * SPAN + r * PIECE, BACK * SPAN + (r + 1) * PIECE)
                        g = g * cos[s, at] - swap_halves(g) * sin[s, at]
                    grads[c, core, y, rows, n * HD : (n + 1) * HD] = g.astype(BF16)
        loop(1, LINE, lambda k: copy6(c, k).start())

    def forward(c):
        settle(grads.at[c, 0, pl.ds(0, LINE - 1)], recv6.at[c])
        copy7(c).start()

    def copy8(c, k):
        peer = x_peer(k)
        return remote(wsend.at[c, peer], wland.at[c, x], send8, recv8.at[c], (dp, z * N_X + peer))

    def copy9(c, peer):
        return remote(zsend.at[c, peer], zland.at[c, z], send9, recv9.at[c], (dp, peer * N_X + x))

    def multiply(c):
        settle(grads.at[c, 0], recv7.at[c])
        w = jnp.dot(xt[...], grads[c].reshape(N_DP * ROWS, W_COL), preferred_element_type=F32)
        wsend[c] = w.astype(BF16).reshape(LINE, W_X, W_COL)
        loop(1, LINE, lambda k: copy8(c, k).start())
        wland[c, x] = wsend[c, x]

    def sum_line(c):
        settle(wland.at[c, pl.ds(0, LINE - 1)], recv8.at[c])
        acc = wland[c, 0].astype(F32)
        for n in range(1, LINE):
            acc += wland[c, n].astype(F32)
        pad = jnp.zeros((PIECE - W_DEV, W_COL), F32)
        for n in range(N_Z):
            block = jnp.concatenate([acc[n * W_DEV : (n + 1) * W_DEV], pad], axis=0)
            zsend[c, n] = block.astype(BF16)
        loop(1, N_Z, lambda k: copy9(c, z_peer(k)).start())
        zland[c, z] = zsend[c, z]

    def sum_z(c):
        settle(zland.at[c, pl.ds(0, N_Z - 1)], recv9.at[c])
        acc = zland[c, 0].astype(F32)
        for n in range(1, N_Z):
            acc += zland[c, n].astype(F32)
        out_ref[:, c * W_COL : (c + 1) * W_COL] = acc[:W_DEV]

    settle(xt.at[:, pl.ds(0, (N_DP - 1) * ROWS)], recv5)
    settle(back.at[1, pl.ds(0, N_CTX - 1)], recv4.at[1])
    values, keyed = range(CHUNKS // 2, CHUNKS), range(CHUNKS // 2)
    for c in values:
        assemble(c)
    settle(back.at[0, pl.ds(0, N_CTX - 1)], recv4.at[0])
    for c in keyed:
        assemble(c)
    for part_of in (values, keyed):
        for c in part_of:
            forward(c)
        for c in part_of:
            multiply(c)
    for c in (*values, *keyed):
        sum_line(c)
    for c in (*values, *keyed):
        sum_z(c)

    settle(held[1].at[pl.ds(0, 2 * (N_CTX - 1))], send1.at[1])
    settle(xt.at[:, pl.ds(0, (N_DP - 1) * ROWS)], send5)
    settle(chosen.at[:, :, pl.ds(0, N_PIECE - 1)], send2)
    settle(part.at[:, :, pl.ds(0, N_PIECE - 1)], send3)
    settle(total.at[:, pl.ds(0, N_CTX - 1)], send4)
    settle(grads.at[:, 0, pl.ds(0, LINE - 1)], send6)
    settle(grads.at[:, 0], send7)
    settle(wsend.at[:, pl.ds(0, LINE - 1)], send8)
    settle(zsend.at[:, pl.ds(0, N_Z - 1)], send9)
    dq_copy.wait()


def per_device(queries, keys, values, grad_out, inputs, span_map, doc_lengths):
    vmem, smem, dma = pltpu.VMEM, pltpu.SMEM, pltpu.SemaphoreType.DMA
    hbm = pl.BlockSpec(memory_space=pl.ANY)
    wide = KVH * G * HD
    tile = (PIECE, HD)
    return pl.pallas_call(
        kernel,
        out_shape=[
            jax.ShapeDtypeStruct((ROWS, wide), BF16),
            jax.ShapeDtypeStruct((W_DEV, 2 * KVC), F32),
        ],
        in_specs=[hbm] * 9,
        out_specs=[hbm, pl.BlockSpec(memory_space=pltpu.VMEM)],
        scratch_shapes=[
            smem((1, SLOTS), I32),
            smem((1, NDOC), I32),
            smem((1, HD), I32),
            smem((SLOTS * BACK,), I32),
            smem((SLOTS * BACK,), I32),
            vmem((1, HD), I32),
            vmem((1, HD), F32),
            vmem((W_DP, W_DP), BF16),
            vmem((ROWS, wide), BF16),
            vmem((ROWS, KVC), BF16),
            vmem((ROWS, KVC), BF16),
            vmem((ROWS, wide), BF16),
            vmem((ROWS, DW), BF16),
            vmem((2, KEYS, HD), F32),
            vmem((2, KEYS, HD), F32),
            vmem((2, KEYS, HD), F32),
            vmem((ROWS, wide), BF16),
            vmem((ROWS, wide), BF16),
            vmem((2, N_PIECE, 2) + tile, BF16),
            vmem((SLOTS,) + tile, BF16),
            vmem((SLOTS,) + tile, BF16),
            vmem((2, 2, N_PIECE, BACK) + tile, BF16),
            vmem((2, 2, N_PIECE, BACK) + tile, BF16),
            vmem((2, 2, N_PIECE, BACK) + tile, BF16),
            vmem((2, ROWS, KVC), F32),
            vmem((2, KVH, KEYS, HD), BF16),
            vmem((2, KVH, KEYS, G * SPAN), BF16),
            vmem((N_CTX * REACH + 1,) + tile, BF16),
            vmem((N_CTX * REACH + 1,) + tile, BF16),
            vmem((2, N_CTX, 2) + tile, BF16),
            vmem((2, N_CTX, 2) + tile, BF16),
            vmem((N_DP, W_DP, ROWS), BF16),
            vmem((W_DP, N_DP * ROWS), BF16),
            vmem((CHUNKS, 2, LINE, ROWS, W_COL), BF16),
            vmem((CHUNKS, N_X, W_X, W_COL), BF16),
            vmem((CHUNKS, N_X, W_X, W_COL), BF16),
            vmem((CHUNKS, N_Z, PIECE, W_COL), BF16),
            vmem((CHUNKS, N_Z, PIECE, W_COL), BF16),
            dma((11,)),
            dma((2,)), dma((2,)),
            dma, dma((2,)),
            dma, dma((2,)),
            dma, dma((2,)),
            dma, dma,
            dma, dma((CHUNKS,)),
            dma, dma((CHUNKS,)),
            dma, dma((CHUNKS,)),
            dma, dma((CHUNKS,)),
        ],
        compiler_params=pltpu.CompilerParams(
            collective_id=0, has_side_effects=True, vmem_limit_bytes=VMEM_LIMIT
        ),
        name="packed_backward",
    )(
        span_map, doc_lengths, jnp.asarray(rope_lanes()), jnp.asarray(feature_order(), BF16),
        queries, keys, values, grad_out, inputs,
    )

def solution(mesh):
    rows = P(("dp", "ctx"), None)
    return jax.shard_map(
        per_device,
        mesh=mesh,
        in_specs=(rows, rows, rows, rows, rows, P("dp", None), P("dp", None)),
        out_specs=(rows, rows),
        check_vma=False,
    )
```

```python
import functools

import jax
import jax.numpy as jnp
import numpy as np
from jax import lax
from jax.experimental import pallas as pl
from jax.experimental.pallas import tpu as pltpu
from jax.sharding import PartitionSpec as P

MESH = pl.DeviceIdType.MESH
BF16 = jnp.bfloat16
F32 = jnp.float32
I32 = jnp.int32

KVH = 4
G = 8
HD = 128
ROT = 64
ROPE_BASE = 10000000.0
SPAN = 64
BACK = 4
ROWS = 2 * SPAN
KEYS = (BACK + 1) * SPAN
N_CTX = 32
N_DP = 8
N_X = 4
N_Z = 8
SLOTS = 2 * N_CTX
NDOC = 32
KVC = KVH * HD
PIECE = 16
N_ROW = SPAN // PIECE
N_PIECE = N_ROW * KVH
REACH = 2 * BACK
DW = 3072
W_DP = DW // N_DP
W_DEV = W_DP // N_CTX
W_X = W_DP // N_X
CHUNKS = 4
HEADS = 2 * KVH // CHUNKS
W_COL = 2 * KVC // CHUNKS
N_Y = N_DP // 2
LINE = 4
MASKED = -1e30
SCALE = HD**-0.5
VMEM_LIMIT = 60 * 1024 * 1024

NT = (((1,), (1,)), ((), ()))
TN = (((0,), (0,)), ((), ()))


def rope_lanes():
    half = ROT // 2
    freq = ROPE_BASE ** (-(np.arange(half, dtype=np.float64) * 2.0 / ROT))
    return np.tile(freq.astype(np.float32), HD // half)[None]


def feature_order():
    order = np.arange(W_DP).reshape(N_Z, N_X, W_DEV).transpose(1, 0, 2).reshape(-1)
    return np.eye(W_DP, dtype=np.float32)[order]


def swap_halves(x):
    lane = lax.broadcasted_iota(I32, x.shape, 1)
    return jnp.where(lane < ROT // 2, pltpu.roll(x, HD - ROT // 2, 1), pltpu.roll(x, ROT // 2, 1))


def begin_of(pos, len_ref):
    def step(d, carry):
        start, begin = carry
        return start + len_ref[0, d], jnp.where(pos >= start, start, begin)

    _, begin = lax.fori_loop(0, NDOC, step, (jnp.int32(0), jnp.zeros_like(pos)), unroll=True)
    return begin


def loop(first, last, body):
    def step(k, carry):
        body(k)
        return carry

    lax.fori_loop(first, last, step, 0)


def remote(src, dst, send, recv, device):
    return pltpu.make_async_remote_copy(
        src_ref=src, dst_ref=dst, send_sem=send, recv_sem=recv, device_id=device, device_id_type=MESH
    )


def rope_tables(pos, lens, freq, cos, sin):
    rel = (pos - begin_of(pos, lens)).astype(F32)
    angle = rel * freq[...]
    packed_cos, packed_sin = jnp.cos(angle), jnp.sin(angle)
    lane = lax.broadcasted_iota(I32, pos.shape, 1)
    half, rows = ROT // 2, pos.shape[0]

    def turn(v, shift):
        shift = shift % HD
        return pltpu.roll(v, shift, 1) if shift else v

    for n in range(HD // half):
        pair = lambda v: (turn(v, -half * n), turn(v, half - half * n))
        (c0, c1), (s0, s1) = pair(packed_cos), pair(packed_sin)
        cos[n * rows : (n + 1) * rows] = jnp.where(lane < half, c0, jnp.where(lane < ROT, c1, 1.0))
        sin[n * rows : (n + 1) * rows] = jnp.where(lane < half, -s0, jnp.where(lane < ROT, s1, 0.0))


def settle(ref, sem):
    pltpu.make_async_copy(ref, ref, sem).wait()


def lanes(at, size):
    return pl.ds(pl.multiple_of(at, HD), size)


def kernel(
    span_h, len_h, freq_h, perm_h, q_h, k_h, v_h, do_h, in_h, dq_h, out_ref,
    span, lens, slot_of, take, give,
    slot_v, freq, perm, q, keys, vals, do, feats, cos, sin, bias, qrot, dq,
    pack, held_k, held_v, chosen, win, part, own, kept_k, kept_ds, landed_k, landed_v, total, back, turned, xt,
    grads, wsend, wland, zsend, zland,
    local, send1, recv1, send2, recv2, send3, recv3, send4, recv4, send5, recv5,
    send6, recv6, send7, recv7, send8, recv8, send9, recv9,
):
    dp, me = lax.axis_index("dp"), lax.axis_index("ctx")
    z, x = me // N_X, lax.rem(me, N_X)
    y, core = dp // 2, lax.rem(dp, 2)
    sib = dp + 1 - 2 * core
    ctx_peer = lambda k: lax.rem(me + k, N_CTX)
    def far_peer(k):
        n = N_CTX - 1 - k
        step = n // 2 + 1
        return ctx_peer(jnp.where(lax.rem(n, 2) == 0, step, N_CTX - step))

    dp_peer = lambda k: lax.rem(dp + k, N_DP)
    y_peer = lambda k: lax.rem(dp + 2 * k, N_DP)
    x_peer = lambda k: lax.rem(x + k, N_X)
    z_peer = lambda k: lax.rem(z + k, N_Z)
    piece_here = lax.rem(z, N_ROW) * KVH + x

    def near(k):
        dz, dx = k // N_X, lax.rem(k, N_X)
        two = jnp.where(lax.rem(dx, 2) == 0, 2, N_Z - 2)
        return jnp.where(dz == 2, two, jnp.where(dz == 3, N_Z - 1, dz)), dx

    def reader(k):
        dz, dx = near(k)
        return lax.rem(z + dz, N_Z) * N_X + lax.rem(x + dx, N_X)

    def holder(k):
        dz, dx = near(k)
        return lax.rem(z + N_Z - dz, N_Z) * N_X + lax.rem(x + N_X - dx, N_X)

    def piece_of(device):
        return lax.rem(device, N_PIECE)

    held, landed = (held_k, held_v), (landed_k, landed_v)

    fetches = [
        pltpu.make_async_copy(src, dst, local.at[n])
        for n, (src, dst) in enumerate([
            (k_h, keys), (v_h, vals), (span_h, span), (len_h, lens), (freq_h, freq),
            (perm_h, perm), (in_h, feats), (q_h, q), (do_h, do),
        ])
    ]
    for copy in fetches:
        copy.start()
    barrier = pltpu.get_barrier_semaphore()

    def greet(device):
        pl.semaphore_signal(barrier, inc=1, device_id=device, device_id_type=MESH)

    loop(1, N_CTX, lambda k: greet((dp, ctx_peer(k))))
    loop(1, N_DP, lambda k: greet((dp_peer(k), me)))
    for copy in fetches[:2]:
        copy.wait()
    for s in range(2):
        for r in range(N_ROW):
            rows = slice(s * SPAN + r * PIECE, s * SPAN + (r + 1) * PIECE)
            for j in range(KVH):
                cols = slice(j * HD, (j + 1) * HD)
                pack[0, r * KVH + j, s] = keys[rows, cols]
                pack[1, r * KVH + j, s] = vals[rows, cols]
    pl.semaphore_wait(barrier, N_CTX - 1 + N_DP - 1)

    def copy1(kind, peer):
        return remote(
            pack.at[kind, piece_of(peer)], held[kind].at[pl.ds(2 * me, 2)], send1.at[kind], recv1.at[kind], (dp, peer)
        )

    def spread(kind):
        loop(1, N_CTX, lambda k: copy1(kind, far_peer(k)).start())
        held[kind][pl.ds(2 * me, 2)] = pack[kind, piece_here]

    spread(0)

    def copy5(peer):
        return remote(
            turned.at[peer],
            xt.at[:, lanes((core * N_Y + y) * ROWS, ROWS)],
            send5,
            recv5,
            (peer, me),
        )

    fetches[5].wait()
    fetches[6].wait()
    for d in range(N_DP):
        w = lax.dot_general(perm[...], feats[:, d * W_DP : (d + 1) * W_DP], NT, preferred_element_type=F32)
        turned[d] = w.astype(BF16)
    loop(1, N_DP, lambda k: copy5(dp_peer(k)).start())
    xt[:, lanes((core * N_Y + y) * ROWS, ROWS)] = turned[dp]

    for copy in fetches[2:5]:
        copy.wait()
    lane_row = lax.broadcasted_iota(I32, (1, HD), 1)
    slots = jnp.zeros((1, HD), I32)
    for n in range(SLOTS):
        slots = jnp.where(lane_row == span[0, n], n, slots)
    slot_v[...] = slots
    slot_copy = pltpu.make_async_copy(slot_v, slot_of, local.at[9])
    slot_copy.start()
    mine = (span[0, 2 * me], span[0, 2 * me + 1])
    for s in range(2):
        own_rows = SPAN // 4
        row = lax.broadcasted_iota(I32, (own_rows, HD), 0)
        group = lax.broadcasted_iota(I32, (own_rows, HD), 1) >> 5
        at = pl.ds(BACK * SPAN, SPAN)
        rope_tables(mine[s] * SPAN + group * own_rows + row, lens, freq, cos.at[s, at], sin.at[s, at])
        row = lax.broadcasted_iota(I32, (SPAN, HD), 0)
        group = lax.broadcasted_iota(I32, (SPAN, HD), 1) >> 5
        pos = (mine[s] - BACK + (row >> 4)) * SPAN + group * PIECE + (row & 15)
        at = pl.ds(0, BACK * SPAN)
        rope_tables(pos, lens, freq, cos.at[s, at], sin.at[s, at])
    slot_copy.wait()
    settle(held[0].at[pl.ds(0, 2 * (N_CTX - 1))], send1.at[0])
    spread(1)

    def fill(slot):
        at = span[0, slot]
        for w in range(BACK):
            take[slot * BACK + w] = slot_of[0, jnp.maximum(at - BACK + w, 0)]
            later = at + 1 + w
            source = slot_of[0, jnp.minimum(later, SLOTS - 1)] * BACK + (BACK - 1 - w)
            give[slot * BACK + w] = jnp.where(later < SLOTS, source, N_CTX * REACH)

    loop(0, SLOTS, fill)
    for s in range(2):
        lane8 = lax.broadcasted_iota(I32, (8, HD), 1)
        qpos = mine[s] * SPAN + jnp.where(lane8 >= SPAN, lane8 - SPAN, lane8)
        qbegin = begin_of(qpos, lens)
        n = lax.broadcasted_iota(I32, (KEYS, HD), 0)
        r, w, t = n >> 6, (n >> 4) & 3, n & 15
        earlier = (mine[s] - BACK + w) * SPAN + r * PIECE + t
        kpos = jnp.where(n < BACK * SPAN, earlier, mine[s] * SPAN + (n - BACK * SPAN))
        allowed = (kpos <= qpos[0:1]) & (kpos >= qbegin[0:1])
        bias[s] = jnp.where(allowed, 0.0, MASKED)
    fetches[7].wait()

    def rotate(h):
        for s in range(2):
            rows = slice(s * SPAN, (s + 1) * SPAN)
            v = q[rows, lanes(h * HD, HD)].astype(F32)
            v = v * cos[s, BACK * SPAN :] + swap_halves(v) * sin[s, BACK * SPAN :]
            qrot[rows, lanes(h * HD, HD)] = v.astype(BF16)

    loop(0, KVH * G, rotate)
    empty = jnp.zeros((REACH, PIECE, HD), BF16)

    def clear(dz, dx):
        device = lax.rem(z + dz, N_Z) * N_X + lax.rem(x + dx, N_X)
        for side in landed:
            side[pl.ds(REACH * device, REACH)] = empty

    loop(0, 12, lambda k: clear(3 + k // N_X, lax.rem(k, N_X)))
    loop(0, 2, lambda k: clear(2, 2 * k + 1))
    loop(0, 2, lambda k: clear(6, 2 * k))
    for side in landed:
        side[N_CTX * REACH] = jnp.zeros((PIECE, HD), BF16)

    def choose(kind, s, k):
        device = reader(k)
        for w in range(BACK):
            chosen[kind, s, k, w] = held[kind][take[device * REACH + s * BACK + w]]

    def copy2(kind, s, k):
        return remote(
            chosen.at[kind, s, k], win.at[kind, s, piece_here], send2, recv2.at[s, lax.rem(k, N_X)], (dp, reader(k))
        )

    for kind in range(2):
        settle(held[kind].at[pl.ds(0, 2 * (N_CTX - 1))], recv1.at[kind])
        for s in range(2):

            def serve(k, kind=kind, s=s):
                n = k - N_X
                k = jnp.where(n < 0, k * N_X, lax.rem(n, N_ROW) * N_X + N_X - 1 - n // N_ROW)
                choose(kind, s, k)
                copy2(kind, s, k).start()

            loop(1, N_PIECE, serve)
            choose(kind, s, 0)
            win[kind, s, piece_here] = chosen[kind, s, 0]
    fetches[8].wait()

    def copy3(kind, s, k):
        return remote(
            part.at[kind, s, piece_of(holder(k))],
            landed[kind].at[pl.ds(REACH * me + BACK * s, BACK)],
            send3,
            recv3.at[kind],
            (dp, holder(k)),
        )

    def hand_over(kind, s, n, grad):
        j = lax.rem(x + n, KVH)
        earlier = grad[: BACK * SPAN].astype(BF16).reshape(N_ROW, BACK, PIECE, HD)
        for r in range(N_ROW):
            part[kind, s, r * KVH + j] = earlier[r]
        own[kind, s * SPAN : (s + 1) * SPAN, lanes(j * HD, HD)] = grad[BACK * SPAN :]

        def send(dz):
            at = dz * N_X + lax.rem(N_X - n, N_X)

            @pl.when(at > 0)
            def _():
                copy3(kind, s, at).start()

        loop(0, N_ROW, send)

    def stacked(ref, s, j):
        rows = slice(s * SPAN, (s + 1) * SPAN)
        return jnp.concatenate([ref[rows, lanes((j * G + g) * HD, HD)] for g in range(G)], axis=0)

    for s in range(2):

        def attend(n, s=s):
            j = lax.rem(x + n, KVH)

            def window(kind):
                parts = [win[kind, s, r * KVH + j].reshape(BACK * PIECE, HD) for r in range(N_ROW)]
                parts += [pack[kind, r * KVH + j, s] for r in range(N_ROW)]
                return jnp.concatenate(parts, axis=0)

            k, v = window(0).astype(F32), window(1)
            k = (k * cos[s] + swap_halves(k) * sin[s]).astype(BF16)
            qs, dos = stacked(qrot, s, j), stacked(do, s, j)
            mask = jnp.concatenate([bias[s]] * (G * SPAN // HD), axis=1)
            scores = lax.dot_general(k, qs, NT, preferred_element_type=F32)
            scores = scores * (SCALE * float(np.log2(np.e))) + mask
            weight = jnp.exp2(scores - jnp.max(scores, axis=0, keepdims=True))
            probs = weight * (1.0 / jnp.sum(weight, axis=0, keepdims=True))
            dprobs = lax.dot_general(v, dos, NT, preferred_element_type=F32)
            delta = jnp.sum(probs * dprobs, axis=0, keepdims=True)
            dscores = (probs * (dprobs - delta)).astype(BF16)
            low = probs.astype(BF16)
            hand_over(1, s, n, jnp.dot(low, dos, preferred_element_type=F32))
            kept_k[s, j] = k
            kept_ds[s, j] = dscores

        def key_part(n, s=s):
            j = lax.rem(x + n, KVH)
            dk = jnp.dot(kept_ds[s, j], stacked(qrot, s, j), preferred_element_type=F32)
            hand_over(0, s, n, dk * SCALE)

        def attend_next(n, s=s):
            settle(win.at[:, s, pl.ds(0, N_ROW)], recv2.at[s, N_X - n])
            attend(n)

        settle(win.at[:, s, pl.ds(0, N_ROW - 1)], recv2.at[s, 0])
        attend(0)
        loop(1, KVH, attend_next)
        loop(0, KVH, key_part)
        for kind in range(2):
            landed[kind][pl.ds(REACH * me + BACK * s, BACK)] = part[kind, s, piece_here]

    def query_grads(j):
        for s in range(2):
            rows = slice(s * SPAN, (s + 1) * SPAN)
            across_keys = lax.dot_general(kept_k[s, j], kept_ds[s, j], TN, preferred_element_type=F32)
            upright = across_keys.T * SCALE
            for g in range(G):
                u = upright[g * SPAN : (g + 1) * SPAN]
                u = u * cos[s, BACK * SPAN :] - swap_halves(u) * sin[s, BACK * SPAN :]
                dq[rows, lanes((j * G + g) * HD, HD)] = u.astype(BF16)

    loop(0, KVH, query_grads)
    dq_copy = pltpu.make_async_copy(dq, dq_h, local.at[10])
    dq_copy.start()

    def copy4(kind, src, owner, peer):
        return remote(
            total.at[kind, src], back.at[kind, owner], send4.at[kind], recv4.at[kind], (dp, peer)
        )

    def sum_up(kind, device):
        for s in range(2):
            at = (2 * device + s) * BACK
            acc = landed[kind][give[at]].astype(F32)
            for w in range(1, BACK):
                acc += landed[kind][give[at + w]].astype(F32)
            total[kind, device, s] = acc.astype(BF16)

    for kind in (1, 0):
        settle(landed[kind].at[pl.ds(0, REACH * (N_PIECE - 1))], recv3.at[kind])
        if kind == 0:
            settle(total.at[1, pl.ds(0, N_CTX - 1)], send4.at[1])

        def give_back(k, kind=kind):
            sum_up(kind, far_peer(k))
            copy4(kind, far_peer(k), me, far_peer(k)).start()

        loop(1, N_CTX, give_back)
        sum_up(kind, me)
        back[kind, me] = total[kind, me]

    def copy6(c, k):
        mine = grads.at[c, core, y]
        return remote(mine, mine, send6, recv6.at[c], (y_peer(k), me))

    def copy7(c):
        return remote(grads.at[c, core], grads.at[c, core], send7, recv7.at[c], (sib, me))

    def assemble(c):
        kind = c * HEADS // KVH
        for n in range(HEADS):
            j = (c * HEADS + n) % KVH
            for r in range(N_ROW):
                for s in range(2):
                    rows = slice(s * SPAN + r * PIECE, s * SPAN + (r + 1) * PIECE)
                    piece = r * KVH + j
                    g = back[kind, piece, s].astype(F32) + back[kind, N_PIECE + piece, s].astype(F32)
                    g += own[kind, rows, j * HD : (j + 1) * HD]
                    if kind == 0:
                        at = slice(BACK * SPAN + r * PIECE, BACK * SPAN + (r + 1) * PIECE)
                        g = g * cos[s, at] - swap_halves(g) * sin[s, at]
                    grads[c, core, y, rows, n * HD : (n + 1) * HD] = g.astype(BF16)
        loop(1, LINE, lambda k: copy6(c, k).start())

    def forward(c):
        settle(grads.at[c, 0, pl.ds(0, LINE - 1)], recv6.at[c])
        copy7(c).start()

    def copy8(c, k):
        peer = x_peer(k)
        return remote(wsend.at[c, peer], wland.at[c, x], send8, recv8.at[c], (dp, z * N_X + peer))

    def copy9(c, peer):
        return remote(zsend.at[c, peer], zland.at[c, z], send9, recv9.at[c], (dp, peer * N_X + x))

    def multiply(c):
        settle(grads.at[c, 0], recv7.at[c])
        w = jnp.dot(xt[...], grads[c].reshape(N_DP * ROWS, W_COL), preferred_element_type=F32)
        wsend[c] = w.astype(BF16).reshape(LINE, W_X, W_COL)
        loop(1, LINE, lambda k: copy8(c, k).start())
        wland[c, x] = wsend[c, x]

    def sum_line(c):
        settle(wland.at[c, pl.ds(0, LINE - 1)], recv8.at[c])
        acc = wland[c, 0].astype(F32)
        for n in range(1, LINE):
            acc += wland[c, n].astype(F32)
        pad = jnp.zeros((PIECE - W_DEV, W_COL), F32)
        for n in range(N_Z):
            block = jnp.concatenate([acc[n * W_DEV : (n + 1) * W_DEV], pad], axis=0)
            zsend[c, n] = block.astype(BF16)
        loop(1, N_Z, lambda k: copy9(c, z_peer(k)).start())
        zland[c, z] = zsend[c, z]

    def sum_z(c):
        settle(zland.at[c, pl.ds(0, N_Z - 1)], recv9.at[c])
        acc = zland[c, 0].astype(F32)
        for n in range(1, N_Z):
            acc += zland[c, n].astype(F32)
        out_ref[:, c * W_COL : (c + 1) * W_COL] = acc[:W_DEV]

    settle(xt.at[:, pl.ds(0, (N_DP - 1) * ROWS)], recv5)
    settle(back.at[1, pl.ds(0, N_CTX - 1)], recv4.at[1])
    values, keyed = range(CHUNKS // 2, CHUNKS), range(CHUNKS // 2)
    for c in values:
        assemble(c)
    settle(back.at[0, pl.ds(0, N_CTX - 1)], recv4.at[0])
    for c in keyed:
        assemble(c)
    for part_of in (values, keyed):
        for c in part_of:
            forward(c)
        for c in part_of:
            multiply(c)
    for c in (*values, *keyed):
        sum_line(c)
    for c in (*values, *keyed):
        sum_z(c)

    settle(held[1].at[pl.ds(0, 2 * (N_CTX - 1))], send1.at[1])
    settle(xt.at[:, pl.ds(0, (N_DP - 1) * ROWS)], send5)
    settle(chosen.at[:, :, pl.ds(0, N_PIECE - 1)], send2)
    settle(part.at[:, :, pl.ds(0, N_PIECE - 1)], send3)
    settle(total.at[0, pl.ds(0, N_CTX - 1)], send4.at[0])
    settle(grads.at[:, 0, pl.ds(0, LINE - 1)], send6)
    settle(grads.at[:, 0], send7)
    settle(wsend.at[:, pl.ds(0, LINE - 1)], send8)
    settle(zsend.at[:, pl.ds(0, N_Z - 1)], send9)
    dq_copy.wait()


def per_device(queries, keys, values, grad_out, inputs, span_map, doc_lengths):
    vmem, smem, dma = pltpu.VMEM, pltpu.SMEM, pltpu.SemaphoreType.DMA
    hbm = pl.BlockSpec(memory_space=pl.ANY)
    wide = KVH * G * HD
    tile = (PIECE, HD)
    return pl.pallas_call(
        kernel,
        out_shape=[
            jax.ShapeDtypeStruct((ROWS, wide), BF16),
            jax.ShapeDtypeStruct((W_DEV, 2 * KVC), F32),
        ],
        in_specs=[hbm] * 9,
        out_specs=[hbm, pl.BlockSpec(memory_space=pltpu.VMEM)],
        scratch_shapes=[
            smem((1, SLOTS), I32),
            smem((1, NDOC), I32),
            smem((1, HD), I32),
            smem((SLOTS * BACK,), I32),
            smem((SLOTS * BACK,), I32),
            vmem((1, HD), I32),
            vmem((1, HD), F32),
            vmem((W_DP, W_DP), BF16),
            vmem((ROWS, wide), BF16),
            vmem((ROWS, KVC), BF16),
            vmem((ROWS, KVC), BF16),
            vmem((ROWS, wide), BF16),
            vmem((ROWS, DW), BF16),
            vmem((2, KEYS, HD), F32),
            vmem((2, KEYS, HD), F32),
            vmem((2, KEYS, HD), F32),
            vmem((ROWS, wide), BF16),
            vmem((ROWS, wide), BF16),
            vmem((2, N_PIECE, 2) + tile, BF16),
            vmem((SLOTS,) + tile, BF16),
            vmem((SLOTS,) + tile, BF16),
            vmem((2, 2, N_PIECE, BACK) + tile, BF16),
            vmem((2, 2, N_PIECE, BACK) + tile, BF16),
            vmem((2, 2, N_PIECE, BACK) + tile, BF16),
            vmem((2, ROWS, KVC), F32),
            vmem((2, KVH, KEYS, HD), BF16),
            vmem((2, KVH, KEYS, G * SPAN), BF16),
            vmem((N_CTX * REACH + 1,) + tile, BF16),
            vmem((N_CTX * REACH + 1,) + tile, BF16),
            vmem((2, N_CTX, 2) + tile, BF16),
            vmem((2, N_CTX, 2) + tile, BF16),
            vmem((N_DP, W_DP, ROWS), BF16),
            vmem((W_DP, N_DP * ROWS), BF16),
            vmem((CHUNKS, 2, LINE, ROWS, W_COL), BF16),
            vmem((CHUNKS, N_X, W_X, W_COL), BF16),
            vmem((CHUNKS, N_X, W_X, W_COL), BF16),
            vmem((CHUNKS, N_Z, PIECE, W_COL), BF16),
            vmem((CHUNKS, N_Z, PIECE, W_COL), BF16),
            dma((11,)),
            dma((2,)), dma((2,)),
            dma, dma((2, N_X)),
            dma, dma((2,)),
            dma((2,)), dma((2,)),
            dma, dma,
            dma, dma((CHUNKS,)),
            dma, dma((CHUNKS,)),
            dma, dma((CHUNKS,)),
            dma, dma((CHUNKS,)),
        ],
        compiler_params=pltpu.CompilerParams(
            collective_id=0, has_side_effects=True, vmem_limit_bytes=VMEM_LIMIT
        ),
        name="packed_backward",
    )(
        span_map, doc_lengths, jnp.asarray(rope_lanes()), jnp.asarray(feature_order(), BF16),
        queries, keys, values, grad_out, inputs,
    )

def solution(mesh):
    rows = P(("dp", "ctx"), None)
    return jax.shard_map(
        per_device,
        mesh=mesh,
        in_specs=(rows, rows, rows, rows, rows, P("dp", None), P("dp", None)),
        out_specs=(rows, rows),
        check_vma=False,
    )
```

```python
import functools

import jax
import jax.numpy as jnp
import numpy as np
from jax import lax
from jax.experimental import pallas as pl
from jax.experimental.pallas import tpu as pltpu
from jax.sharding import PartitionSpec as P

MESH = pl.DeviceIdType.MESH
BF16 = jnp.bfloat16
F32 = jnp.float32
I32 = jnp.int32

KVH = 4
G = 8
HD = 128
ROT = 64
ROPE_BASE = 10000000.0
SPAN = 64
BACK = 4
ROWS = 2 * SPAN
KEYS = (BACK + 1) * SPAN
N_CTX = 32
N_DP = 8
N_X = 4
N_Z = 8
SLOTS = 2 * N_CTX
NDOC = 32
KVC = KVH * HD
PIECE = 16
N_ROW = SPAN // PIECE
N_PIECE = N_ROW * KVH
REACH = 2 * BACK
DW = 3072
W_DP = DW // N_DP
W_DEV = W_DP // N_CTX
W_X = W_DP // N_X
CHUNKS = 8
HEADS = 2 * KVH // CHUNKS
W_COL = 2 * KVC // CHUNKS
N_Y = N_DP // 2
LINE = 4
MASKED = -1e30
SCALE = HD**-0.5
VMEM_LIMIT = 60 * 1024 * 1024

NT = (((1,), (1,)), ((), ()))
TN = (((0,), (0,)), ((), ()))


def rope_lanes():
    half = ROT // 2
    freq = ROPE_BASE ** (-(np.arange(half, dtype=np.float64) * 2.0 / ROT))
    return np.tile(freq.astype(np.float32), HD // half)[None]


def feature_order():
    order = np.arange(W_DP).reshape(N_Z, N_X, W_DEV).transpose(1, 0, 2).reshape(-1)
    return np.eye(W_DP, dtype=np.float32)[order]


def swap_halves(x):
    lane = lax.broadcasted_iota(I32, x.shape, 1)
    return jnp.where(lane < ROT // 2, pltpu.roll(x, HD - ROT // 2, 1), pltpu.roll(x, ROT // 2, 1))


def begin_of(pos, len_ref):
    def step(d, carry):
        start, begin = carry
        return start + len_ref[0, d], jnp.where(pos >= start, start, begin)

    _, begin = lax.fori_loop(0, NDOC, step, (jnp.int32(0), jnp.zeros_like(pos)), unroll=True)
    return begin


def loop(first, last, body):
    def step(k, carry):
        body(k)
        return carry

    lax.fori_loop(first, last, step, 0)


def remote(src, dst, send, recv, device):
    return pltpu.make_async_remote_copy(
        src_ref=src, dst_ref=dst, send_sem=send, recv_sem=recv, device_id=device, device_id_type=MESH
    )


def rope_tables(pos, lens, freq, cos, sin):
    rel = (pos - begin_of(pos, lens)).astype(F32)
    angle = rel * freq[...]
    packed_cos, packed_sin = jnp.cos(angle), jnp.sin(angle)
    lane = lax.broadcasted_iota(I32, pos.shape, 1)
    half, rows = ROT // 2, pos.shape[0]

    def turn(v, shift):
        shift = shift % HD
        return pltpu.roll(v, shift, 1) if shift else v

    for n in range(HD // half):
        pair = lambda v: (turn(v, -half * n), turn(v, half - half * n))
        (c0, c1), (s0, s1) = pair(packed_cos), pair(packed_sin)
        cos[n * rows : (n + 1) * rows] = jnp.where(lane < half, c0, jnp.where(lane < ROT, c1, 1.0))
        sin[n * rows : (n + 1) * rows] = jnp.where(lane < half, -s0, jnp.where(lane < ROT, s1, 0.0))


def settle(ref, sem):
    pltpu.make_async_copy(ref, ref, sem).wait()


def lanes(at, size):
    return pl.ds(pl.multiple_of(at, HD), size)


def kernel(
    span_h, len_h, freq_h, perm_h, q_h, k_h, v_h, do_h, in_h, dq_h, out_ref,
    span, lens, slot_of, take, give,
    slot_v, freq, perm, q, keys, vals, do, feats, cos, sin, bias, qrot, dq,
    pack, held_k, held_v, chosen, win, part, own, kept_k, kept_ds, landed_k, landed_v, total, back, turned, xt,
    grads, wsend, wland, zsend, zland,
    local, send1, recv1, send2, recv2, send3, recv3, send4, recv4, send5, recv5,
    send6, recv6, send7, recv7, send8, recv8, send9, recv9,
):
    dp, me = lax.axis_index("dp"), lax.axis_index("ctx")
    z, x = me // N_X, lax.rem(me, N_X)
    y, core = dp // 2, lax.rem(dp, 2)
    sib = dp + 1 - 2 * core
    ctx_peer = lambda k: lax.rem(me + k, N_CTX)
    def far_peer(k):
        n = N_CTX - 1 - k
        step = n // 2 + 1
        return ctx_peer(jnp.where(lax.rem(n, 2) == 0, step, N_CTX - step))

    dp_peer = lambda k: lax.rem(dp + k, N_DP)
    y_peer = lambda k: lax.rem(dp + 2 * k, N_DP)
    x_peer = lambda k: lax.rem(x + k, N_X)
    z_peer = lambda k: lax.rem(z + k, N_Z)
    piece_here = lax.rem(z, N_ROW) * KVH + x

    def near(k):
        dz, dx = k // N_X, lax.rem(k, N_X)
        two = jnp.where(lax.rem(dx, 2) == 0, 2, N_Z - 2)
        return jnp.where(dz == 2, two, jnp.where(dz == 3, N_Z - 1, dz)), dx

    def reader(k):
        dz, dx = near(k)
        return lax.rem(z + dz, N_Z) * N_X + lax.rem(x + dx, N_X)

    def holder(k):
        dz, dx = near(k)
        return lax.rem(z + N_Z - dz, N_Z) * N_X + lax.rem(x + N_X - dx, N_X)

    def piece_of(device):
        return lax.rem(device, N_PIECE)

    held, landed = (held_k, held_v), (landed_k, landed_v)

    fetches = [
        pltpu.make_async_copy(src, dst, local.at[n])
        for n, (src, dst) in enumerate([
            (k_h, keys), (v_h, vals), (span_h, span), (len_h, lens), (freq_h, freq),
            (perm_h, perm), (in_h, feats), (q_h, q), (do_h, do),
        ])
    ]
    for copy in fetches:
        copy.start()
    barrier = pltpu.get_barrier_semaphore()

    def greet(device):
        pl.semaphore_signal(barrier, inc=1, device_id=device, device_id_type=MESH)

    loop(1, N_CTX, lambda k: greet((dp, ctx_peer(k))))
    loop(1, N_DP, lambda k: greet((dp_peer(k), me)))
    for copy in fetches[:2]:
        copy.wait()
    for s in range(2):
        for r in range(N_ROW):
            rows = slice(s * SPAN + r * PIECE, s * SPAN + (r + 1) * PIECE)
            for j in range(KVH):
                cols = slice(j * HD, (j + 1) * HD)
                pack[0, r * KVH + j, s] = keys[rows, cols]
                pack[1, r * KVH + j, s] = vals[rows, cols]
    pl.semaphore_wait(barrier, N_CTX - 1 + N_DP - 1)

    def copy1(kind, peer):
        return remote(
            pack.at[kind, piece_of(peer)], held[kind].at[pl.ds(2 * me, 2)], send1.at[kind], recv1.at[kind], (dp, peer)
        )

    def spread(kind):
        loop(1, N_CTX, lambda k: copy1(kind, far_peer(k)).start())
        held[kind][pl.ds(2 * me, 2)] = pack[kind, piece_here]

    spread(0)

    def copy5(peer):
        return remote(
            turned.at[peer],
            xt.at[:, lanes((core * N_Y + y) * ROWS, ROWS)],
            send5,
            recv5,
            (peer, me),
        )

    fetches[5].wait()
    fetches[6].wait()
    for d in range(N_DP):
        w = lax.dot_general(perm[...], feats[:, d * W_DP : (d + 1) * W_DP], NT, preferred_element_type=F32)
        turned[d] = w.astype(BF16)
    loop(1, N_DP, lambda k: copy5(dp_peer(k)).start())
    xt[:, lanes((core * N_Y + y) * ROWS, ROWS)] = turned[dp]

    for copy in fetches[2:5]:
        copy.wait()
    lane_row = lax.broadcasted_iota(I32, (1, HD), 1)
    slots = jnp.zeros((1, HD), I32)
    for n in range(SLOTS):
        slots = jnp.where(lane_row == span[0, n], n, slots)
    slot_v[...] = slots
    slot_copy = pltpu.make_async_copy(slot_v, slot_of, local.at[9])
    slot_copy.start()
    mine = (span[0, 2 * me], span[0, 2 * me + 1])
    for s in range(2):
        own_rows = SPAN // 4
        row = lax.broadcasted_iota(I32, (own_rows, HD), 0)
        group = lax.broadcasted_iota(I32, (own_rows, HD), 1) >> 5
        at = pl.ds(BACK * SPAN, SPAN)
        rope_tables(mine[s] * SPAN + group * own_rows + row, lens, freq, cos.at[s, at], sin.at[s, at])
        row = lax.broadcasted_iota(I32, (SPAN, HD), 0)
        group = lax.broadcasted_iota(I32, (SPAN, HD), 1) >> 5
        pos = (mine[s] - BACK + (row >> 4)) * SPAN + group * PIECE + (row & 15)
        at = pl.ds(0, BACK * SPAN)
        rope_tables(pos, lens, freq, cos.at[s, at], sin.at[s, at])
    slot_copy.wait()
    settle(held[0].at[pl.ds(0, 2 * (N_CTX - 1))], send1.at[0])
    spread(1)

    def fill(slot):
        at = span[0, slot]
        for w in range(BACK):
            take[slot * BACK + w] = slot_of[0, jnp.maximum(at - BACK + w, 0)]
            later = at + 1 + w
            source = slot_of[0, jnp.minimum(later, SLOTS - 1)] * BACK + (BACK - 1 - w)
            give[slot * BACK + w] = jnp.where(later < SLOTS, source, N_CTX * REACH)

    loop(0, SLOTS, fill)
    for s in range(2):
        lane8 = lax.broadcasted_iota(I32, (8, HD), 1)
        qpos = mine[s] * SPAN + jnp.where(lane8 >= SPAN, lane8 - SPAN, lane8)
        qbegin = begin_of(qpos, lens)
        n = lax.broadcasted_iota(I32, (KEYS, HD), 0)
        r, w, t = n >> 6, (n >> 4) & 3, n & 15
        earlier = (mine[s] - BACK + w) * SPAN + r * PIECE + t
        kpos = jnp.where(n < BACK * SPAN, earlier, mine[s] * SPAN + (n - BACK * SPAN))
        allowed = (kpos <= qpos[0:1]) & (kpos >= qbegin[0:1])
        bias[s] = jnp.where(allowed, 0.0, MASKED)
    fetches[7].wait()

    def rotate(h):
        for s in range(2):
            rows = slice(s * SPAN, (s + 1) * SPAN)
            v = q[rows, lanes(h * HD, HD)].astype(F32)
            v = v * cos[s, BACK * SPAN :] + swap_halves(v) * sin[s, BACK * SPAN :]
            qrot[rows, lanes(h * HD, HD)] = v.astype(BF16)

    loop(0, KVH * G, rotate)
    empty = jnp.zeros((REACH, PIECE, HD), BF16)

    def clear(dz, dx):
        device = lax.rem(z + dz, N_Z) * N_X + lax.rem(x + dx, N_X)
        for side in landed:
            side[pl.ds(REACH * device, REACH)] = empty

    loop(0, 12, lambda k: clear(3 + k // N_X, lax.rem(k, N_X)))
    loop(0, 2, lambda k: clear(2, 2 * k + 1))
    loop(0, 2, lambda k: clear(6, 2 * k))
    for side in landed:
        side[N_CTX * REACH] = jnp.zeros((PIECE, HD), BF16)

    def choose(kind, s, k):
        device = reader(k)
        for w in range(BACK):
            chosen[kind, s, k, w] = held[kind][take[device * REACH + s * BACK + w]]

    def copy2(kind, s, k):
        return remote(
            chosen.at[kind, s, k], win.at[kind, s, piece_here], send2, recv2.at[s, lax.rem(k, N_X)], (dp, reader(k))
        )

    def hand_out(kind, s):
        def serve(k):
            n = k - N_X
            k = jnp.where(n < 0, k * N_X, lax.rem(n, N_ROW) * N_X + N_X - 1 - n // N_ROW)
            choose(kind, s, k)
            copy2(kind, s, k).start()

        loop(1, N_PIECE, serve)
        choose(kind, s, 0)
        win[kind, s, piece_here] = chosen[kind, s, 0]

    settle(held[0].at[pl.ds(0, 2 * (N_CTX - 1))], recv1.at[0])
    hand_out(0, 0)
    settle(held[1].at[pl.ds(0, 2 * (N_CTX - 1))], recv1.at[1])
    hand_out(1, 0)
    hand_out(0, 1)
    hand_out(1, 1)
    fetches[8].wait()

    def copy3(kind, s, k):
        return remote(
            part.at[kind, s, piece_of(holder(k))],
            landed[kind].at[pl.ds(REACH * me + BACK * s, BACK)],
            send3,
            recv3.at[kind],
            (dp, holder(k)),
        )

    def hand_over(kind, s, n, grad):
        j = lax.rem(x + n, KVH)
        earlier = grad[: BACK * SPAN].astype(BF16).reshape(N_ROW, BACK, PIECE, HD)
        for r in range(N_ROW):
            part[kind, s, r * KVH + j] = earlier[r]
        own[kind, s * SPAN : (s + 1) * SPAN, lanes(j * HD, HD)] = grad[BACK * SPAN :]

        def send(dz):
            at = dz * N_X + lax.rem(N_X - n, N_X)

            @pl.when(at > 0)
            def _():
                copy3(kind, s, at).start()

        loop(0, N_ROW, send)

    def stacked(ref, s, j):
        rows = slice(s * SPAN, (s + 1) * SPAN)
        return jnp.concatenate([ref[rows, lanes((j * G + g) * HD, HD)] for g in range(G)], axis=0)

    for s in range(2):

        def attend(n, s=s):
            j = lax.rem(x + n, KVH)

            def window(kind):
                parts = [win[kind, s, r * KVH + j].reshape(BACK * PIECE, HD) for r in range(N_ROW)]
                parts += [pack[kind, r * KVH + j, s] for r in range(N_ROW)]
                return jnp.concatenate(parts, axis=0)

            k, v = window(0).astype(F32), window(1)
            k = (k * cos[s] + swap_halves(k) * sin[s]).astype(BF16)
            qs, dos = stacked(qrot, s, j), stacked(do, s, j)
            mask = jnp.concatenate([bias[s]] * (G * SPAN // HD), axis=1)
            scores = lax.dot_general(k, qs, NT, preferred_element_type=F32)
            scores = scores * (SCALE * float(np.log2(np.e))) + mask
            weight = jnp.exp2(scores - jnp.max(scores, axis=0, keepdims=True))
            probs = weight * (1.0 / jnp.sum(weight, axis=0, keepdims=True))
            dprobs = lax.dot_general(v, dos, NT, preferred_element_type=F32)
            delta = jnp.sum(probs * dprobs, axis=0, keepdims=True)
            dscores = (probs * (dprobs - delta)).astype(BF16)
            low = probs.astype(BF16)
            hand_over(1, s, n, jnp.dot(low, dos, preferred_element_type=F32))
            kept_k[s, j] = k
            kept_ds[s, j] = dscores

        def key_part(n, s=s):
            j = lax.rem(x + n, KVH)
            dk = jnp.dot(kept_ds[s, j], stacked(qrot, s, j), preferred_element_type=F32)
            hand_over(0, s, n, dk * SCALE)

        def attend_next(n, s=s):
            settle(win.at[:, s, pl.ds(0, N_ROW)], recv2.at[s, N_X - n])
            attend(n)

        settle(win.at[:, s, pl.ds(0, N_ROW - 1)], recv2.at[s, 0])
        attend(0)
        loop(1, KVH, attend_next)
        loop(0, KVH, key_part)
        for kind in range(2):
            landed[kind][pl.ds(REACH * me + BACK * s, BACK)] = part[kind, s, piece_here]

    def query_grads(j):
        for s in range(2):
            rows = slice(s * SPAN, (s + 1) * SPAN)
            across_keys = lax.dot_general(kept_k[s, j], kept_ds[s, j], TN, preferred_element_type=F32)
            upright = across_keys.T * SCALE
            for g in range(G):
                u = upright[g * SPAN : (g + 1) * SPAN]
                u = u * cos[s, BACK * SPAN :] - swap_halves(u) * sin[s, BACK * SPAN :]
                dq[rows, lanes((j * G + g) * HD, HD)] = u.astype(BF16)

    loop(0, KVH, query_grads)
    dq_copy = pltpu.make_async_copy(dq, dq_h, local.at[10])
    dq_copy.start()

    def copy4(kind, src, owner, peer):
        return remote(
            total.at[kind, src], back.at[kind, owner], send4.at[kind], recv4.at[kind], (dp, peer)
        )

    def sum_up(kind, device):
        for s in range(2):
            at = (2 * device + s) * BACK
            acc = landed[kind][give[at]].astype(F32)
            for w in range(1, BACK):
                acc += landed[kind][give[at + w]].astype(F32)
            total[kind, device, s] = acc.astype(BF16)

    for kind in (1, 0):
        settle(landed[kind].at[pl.ds(0, REACH * (N_PIECE - 1))], recv3.at[kind])
        if kind == 0:
            settle(total.at[1, pl.ds(0, N_CTX - 1)], send4.at[1])

        def give_back(k, kind=kind):
            sum_up(kind, far_peer(k))
            copy4(kind, far_peer(k), me, far_peer(k)).start()

        loop(1, N_CTX, give_back)
        sum_up(kind, me)
        back[kind, me] = total[kind, me]

    def copy6(c, k):
        mine = grads.at[c, core, y]
        return remote(mine, mine, send6, recv6.at[c], (y_peer(k), me))

    def copy7(c):
        return remote(grads.at[c, core], grads.at[c, core], send7, recv7.at[c], (sib, me))

    def assemble(c):
        kind = c * HEADS // KVH
        for n in range(HEADS):
            j = (c * HEADS + n) % KVH
            for r in range(N_ROW):
                for s in range(2):
                    rows = slice(s * SPAN + r * PIECE, s * SPAN + (r + 1) * PIECE)
                    piece = r * KVH + j
                    g = back[kind, piece, s].astype(F32) + back[kind, N_PIECE + piece, s].astype(F32)
                    g += own[kind, rows, j * HD : (j + 1) * HD]
                    if kind == 0:
                        at = slice(BACK * SPAN + r * PIECE, BACK * SPAN + (r + 1) * PIECE)
                        g = g * cos[s, at] - swap_halves(g) * sin[s, at]
                    grads[c, core, y, rows, n * HD : (n + 1) * HD] = g.astype(BF16)
        loop(1, LINE, lambda k: copy6(c, k).start())

    def forward(c):
        settle(grads.at[c, 0, pl.ds(0, LINE - 1)], recv6.at[c])
        copy7(c).start()

    def copy8(c, k):
        peer = x_peer(k)
        return remote(wsend.at[c, peer], wland.at[c, x], send8, recv8.at[c], (dp, z * N_X + peer))

    def copy9(c, peer):
        return remote(zsend.at[c, peer], zland.at[c, z], send9, recv9.at[c], (dp, peer * N_X + x))

    def multiply(c):
        settle(grads.at[c, 0], recv7.at[c])
        w = jnp.dot(xt[...], grads[c].reshape(N_DP * ROWS, W_COL), preferred_element_type=F32)
        wsend[c] = w.astype(BF16).reshape(LINE, W_X, W_COL)
        loop(1, LINE, lambda k: copy8(c, k).start())
        wland[c, x] = wsend[c, x]

    def sum_line(c):
        settle(wland.at[c, pl.ds(0, LINE - 1)], recv8.at[c])
        acc = wland[c, 0].astype(F32)
        for n in range(1, LINE):
            acc += wland[c, n].astype(F32)
        pad = jnp.zeros((PIECE - W_DEV, W_COL), F32)
        for n in range(N_Z):
            block = jnp.concatenate([acc[n * W_DEV : (n + 1) * W_DEV], pad], axis=0)
            zsend[c, n] = block.astype(BF16)
        loop(1, N_Z, lambda k: copy9(c, z_peer(k)).start())
        zland[c, z] = zsend[c, z]

    def sum_z(c):
        settle(zland.at[c, pl.ds(0, N_Z - 1)], recv9.at[c])
        acc = zland[c, 0].astype(F32)
        for n in range(1, N_Z):
            acc += zland[c, n].astype(F32)
        out_ref[:, c * W_COL : (c + 1) * W_COL] = acc[:W_DEV]

    settle(xt.at[:, pl.ds(0, (N_DP - 1) * ROWS)], recv5)
    settle(back.at[1, pl.ds(0, N_CTX - 1)], recv4.at[1])
    values, keyed = range(CHUNKS // 2, CHUNKS), range(CHUNKS // 2)
    for c in values:
        assemble(c)
    settle(back.at[0, pl.ds(0, N_CTX - 1)], recv4.at[0])
    for c in keyed:
        assemble(c)
    for part_of in (values, keyed):
        for c in part_of:
            forward(c)
        for c in part_of:
            multiply(c)
    for c in (*values, *keyed):
        sum_line(c)
    for c in (*values, *keyed):
        sum_z(c)

    settle(held[1].at[pl.ds(0, 2 * (N_CTX - 1))], send1.at[1])
    settle(xt.at[:, pl.ds(0, (N_DP - 1) * ROWS)], send5)
    settle(chosen.at[:, :, pl.ds(0, N_PIECE - 1)], send2)
    settle(part.at[:, :, pl.ds(0, N_PIECE - 1)], send3)
    settle(total.at[0, pl.ds(0, N_CTX - 1)], send4.at[0])
    settle(grads.at[:, 0, pl.ds(0, LINE - 1)], send6)
    settle(grads.at[:, 0], send7)
    settle(wsend.at[:, pl.ds(0, LINE - 1)], send8)
    settle(zsend.at[:, pl.ds(0, N_Z - 1)], send9)
    dq_copy.wait()


def per_device(queries, keys, values, grad_out, inputs, span_map, doc_lengths):
    vmem, smem, dma = pltpu.VMEM, pltpu.SMEM, pltpu.SemaphoreType.DMA
    hbm = pl.BlockSpec(memory_space=pl.ANY)
    wide = KVH * G * HD
    tile = (PIECE, HD)
    return pl.pallas_call(
        kernel,
        out_shape=[
            jax.ShapeDtypeStruct((ROWS, wide), BF16),
            jax.ShapeDtypeStruct((W_DEV, 2 * KVC), F32),
        ],
        in_specs=[hbm] * 9,
        out_specs=[hbm, pl.BlockSpec(memory_space=pltpu.VMEM)],
        scratch_shapes=[
            smem((1, SLOTS), I32),
            smem((1, NDOC), I32),
            smem((1, HD), I32),
            smem((SLOTS * BACK,), I32),
            smem((SLOTS * BACK,), I32),
            vmem((1, HD), I32),
            vmem((1, HD), F32),
            vmem((W_DP, W_DP), BF16),
            vmem((ROWS, wide), BF16),
            vmem((ROWS, KVC), BF16),
            vmem((ROWS, KVC), BF16),
            vmem((ROWS, wide), BF16),
            vmem((ROWS, DW), BF16),
            vmem((2, KEYS, HD), F32),
            vmem((2, KEYS, HD), F32),
            vmem((2, KEYS, HD), F32),
            vmem((ROWS, wide), BF16),
            vmem((ROWS, wide), BF16),
            vmem((2, N_PIECE, 2) + tile, BF16),
            vmem((SLOTS,) + tile, BF16),
            vmem((SLOTS,) + tile, BF16),
            vmem((2, 2, N_PIECE, BACK) + tile, BF16),
            vmem((2, 2, N_PIECE, BACK) + tile, BF16),
            vmem((2, 2, N_PIECE, BACK) + tile, BF16),
            vmem((2, ROWS, KVC), F32),
            vmem((2, KVH, KEYS, HD), BF16),
            vmem((2, KVH, KEYS, G * SPAN), BF16),
            vmem((N_CTX * REACH + 1,) + tile, BF16),
            vmem((N_CTX * REACH + 1,) + tile, BF16),
            vmem((2, N_CTX, 2) + tile, BF16),
            vmem((2, N_CTX, 2) + tile, BF16),
            vmem((N_DP, W_DP, ROWS), BF16),
            vmem((W_DP, N_DP * ROWS), BF16),
            vmem((CHUNKS, 2, LINE, ROWS, W_COL), BF16),
            vmem((CHUNKS, N_X, W_X, W_COL), BF16),
            vmem((CHUNKS, N_X, W_X, W_COL), BF16),
            vmem((CHUNKS, N_Z, PIECE, W_COL), BF16),
            vmem((CHUNKS, N_Z, PIECE, W_COL), BF16),
            dma((11,)),
            dma((2,)), dma((2,)),
            dma, dma((2, N_X)),
            dma, dma((2,)),
            dma((2,)), dma((2,)),
            dma, dma,
            dma, dma((CHUNKS,)),
            dma, dma((CHUNKS,)),
            dma, dma((CHUNKS,)),
            dma, dma((CHUNKS,)),
        ],
        compiler_params=pltpu.CompilerParams(
            collective_id=0, has_side_effects=True, vmem_limit_bytes=VMEM_LIMIT
        ),
        name="packed_backward",
    )(
        span_map, doc_lengths, jnp.asarray(rope_lanes()), jnp.asarray(feature_order(), BF16),
        queries, keys, values, grad_out, inputs,
    )

def solution(mesh):
    rows = P(("dp", "ctx"), None)
    return jax.shard_map(
        per_device,
        mesh=mesh,
        in_specs=(rows, rows, rows, rows, rows, P("dp", None), P("dp", None)),
        out_specs=(rows, rows),
        check_vma=False,
    )
```

```python
import functools

import jax
import jax.numpy as jnp
import numpy as np
from jax import lax
from jax.experimental import pallas as pl
from jax.experimental.pallas import tpu as pltpu
from jax.sharding import PartitionSpec as P

MESH = pl.DeviceIdType.MESH
BF16 = jnp.bfloat16
F32 = jnp.float32
I32 = jnp.int32

KVH = 4
G = 8
HD = 128
ROT = 64
ROPE_BASE = 10000000.0
SPAN = 64
BACK = 4
ROWS = 2 * SPAN
KEYS = (BACK + 1) * SPAN
N_CTX = 32
N_DP = 8
N_X = 4
N_Z = 8
SLOTS = 2 * N_CTX
NDOC = 32
KVC = KVH * HD
PIECE = 16
N_ROW = SPAN // PIECE
N_PIECE = N_ROW * KVH
REACH = 2 * BACK
DW = 3072
W_DP = DW // N_DP
W_DEV = W_DP // N_CTX
W_X = W_DP // N_X
CHUNKS = 8
HEADS = 2 * KVH // CHUNKS
W_COL = 2 * KVC // CHUNKS
N_Y = N_DP // 2
LINE = 4
MASKED = -1e30
SCALE = HD**-0.5
VMEM_LIMIT = 60 * 1024 * 1024

NT = (((1,), (1,)), ((), ()))
TN = (((0,), (0,)), ((), ()))


def rope_lanes():
    half = ROT // 2
    freq = ROPE_BASE ** (-(np.arange(half, dtype=np.float64) * 2.0 / ROT))
    return np.tile(freq.astype(np.float32), HD // half)[None]


def feature_order():
    order = np.arange(W_DP).reshape(N_Z, N_X, W_DEV).transpose(1, 0, 2).reshape(-1)
    return np.eye(W_DP, dtype=np.float32)[order]


def swap_halves(x):
    lane = lax.broadcasted_iota(I32, x.shape, 1)
    return jnp.where(lane < ROT // 2, pltpu.roll(x, HD - ROT // 2, 1), pltpu.roll(x, ROT // 2, 1))


def begin_of(pos, len_ref):
    def step(d, carry):
        start, begin = carry
        return start + len_ref[0, d], jnp.where(pos >= start, start, begin)

    _, begin = lax.fori_loop(0, NDOC, step, (jnp.int32(0), jnp.zeros_like(pos)), unroll=True)
    return begin


def loop(first, last, body):
    def step(k, carry):
        body(k)
        return carry

    lax.fori_loop(first, last, step, 0)


def remote(src, dst, send, recv, device):
    return pltpu.make_async_remote_copy(
        src_ref=src, dst_ref=dst, send_sem=send, recv_sem=recv, device_id=device, device_id_type=MESH
    )


def rope_tables(pos, lens, freq, cos, sin):
    rel = (pos - begin_of(pos, lens)).astype(F32)
    angle = rel * freq[...]
    packed_cos, packed_sin = jnp.cos(angle), jnp.sin(angle)
    lane = lax.broadcasted_iota(I32, pos.shape, 1)
    half, rows = ROT // 2, pos.shape[0]

    def turn(v, shift):
        shift = shift % HD
        return pltpu.roll(v, shift, 1) if shift else v

    for n in range(HD // half):
        pair = lambda v: (turn(v, -half * n), turn(v, half - half * n))
        (c0, c1), (s0, s1) = pair(packed_cos), pair(packed_sin)
        cos[n * rows : (n + 1) * rows] = jnp.where(lane < half, c0, jnp.where(lane < ROT, c1, 1.0))
        sin[n * rows : (n + 1) * rows] = jnp.where(lane < half, -s0, jnp.where(lane < ROT, s1, 0.0))


def settle(ref, sem):
    pltpu.make_async_copy(ref, ref, sem).wait()


def lanes(at, size):
    return pl.ds(pl.multiple_of(at, HD), size)


def kernel(
    span_h, len_h, freq_h, perm_h, q_h, k_h, v_h, do_h, in_h, dq_h, out_ref,
    span, lens, slot_of, take, give,
    slot_v, freq, perm, q, keys, vals, do, feats, cos, sin, bias, qrot, dq,
    pack, held_k, held_v, chosen, win, part, own, kept_k, kept_ds, landed_k, landed_v, total, back, turned, xt,
    grads, wsend, wland, zsend, zland,
    local, send1, recv1, send2, recv2, send3, recv3, send4, recv4, send5, recv5,
    send6, recv6, send7, recv7, send8, recv8, send9, recv9,
):
    dp, me = lax.axis_index("dp"), lax.axis_index("ctx")
    z, x = me // N_X, lax.rem(me, N_X)
    y, core = dp // 2, lax.rem(dp, 2)
    sib = dp + 1 - 2 * core
    ctx_peer = lambda k: lax.rem(me + k, N_CTX)
    def far_peer(k):
        n = N_CTX - 1 - k
        step = n // 2 + 1
        return ctx_peer(jnp.where(lax.rem(n, 2) == 0, step, N_CTX - step))

    far_step = lambda k: 1 + lax.rem(k, LINE - 1)

    def far_z(k):
        n = N_Z - 1 - k
        step = n // 2 + 1
        return jnp.where(lax.rem(n, 2) == 0, step, N_Z - step)

    dp_peer = lambda k: lax.rem(dp + k, N_DP)
    y_peer = lambda k: lax.rem(dp + 2 * k, N_DP)
    x_peer = lambda k: lax.rem(x + k, N_X)
    z_peer = lambda k: lax.rem(z + k, N_Z)
    piece_here = lax.rem(z, N_ROW) * KVH + x

    def near(k):
        dz, dx = k // N_X, lax.rem(k, N_X)
        two = jnp.where(lax.rem(dx, 2) == 0, 2, N_Z - 2)
        return jnp.where(dz == 2, two, jnp.where(dz == 3, N_Z - 1, dz)), dx

    def reader(k):
        dz, dx = near(k)
        return lax.rem(z + dz, N_Z) * N_X + lax.rem(x + dx, N_X)

    def holder(k):
        dz, dx = near(k)
        return lax.rem(z + N_Z - dz, N_Z) * N_X + lax.rem(x + N_X - dx, N_X)

    def piece_of(device):
        return lax.rem(device, N_PIECE)

    held, landed = (held_k, held_v), (landed_k, landed_v)

    fetches = [
        pltpu.make_async_copy(src, dst, local.at[n])
        for n, (src, dst) in enumerate([
            (k_h, keys), (v_h, vals), (span_h, span), (len_h, lens), (freq_h, freq),
            (perm_h, perm), (in_h, feats), (q_h, q), (do_h, do),
        ])
    ]
    for copy in fetches:
        copy.start()
    barrier = pltpu.get_barrier_semaphore()

    def greet(device):
        pl.semaphore_signal(barrier, inc=1, device_id=device, device_id_type=MESH)

    loop(1, N_CTX, lambda k: greet((dp, ctx_peer(k))))
    loop(1, N_DP, lambda k: greet((dp_peer(k), me)))
    for copy in fetches[:2]:
        copy.wait()
    for s in range(2):
        for r in range(N_ROW):
            rows = slice(s * SPAN + r * PIECE, s * SPAN + (r + 1) * PIECE)
            for j in range(KVH):
                cols = slice(j * HD, (j + 1) * HD)
                pack[0, r * KVH + j, s] = keys[rows, cols]
                pack[1, r * KVH + j, s] = vals[rows, cols]
    pl.semaphore_wait(barrier, N_CTX - 1 + N_DP - 1)

    def copy1(kind, peer):
        return remote(
            pack.at[kind, piece_of(peer)], held[kind].at[pl.ds(2 * me, 2)], send1.at[kind], recv1.at[kind], (dp, peer)
        )

    def spread(kind):
        loop(1, N_CTX, lambda k: copy1(kind, far_peer(k)).start())
        held[kind][pl.ds(2 * me, 2)] = pack[kind, piece_here]

    spread(0)

    def copy5(peer):
        return remote(
            turned.at[peer],
            xt.at[:, lanes((core * N_Y + y) * ROWS, ROWS)],
            send5,
            recv5,
            (peer, me),
        )

    fetches[5].wait()
    fetches[6].wait()
    for d in range(N_DP):
        w = lax.dot_general(perm[...], feats[:, d * W_DP : (d + 1) * W_DP], NT, preferred_element_type=F32)
        turned[d] = w.astype(BF16)
    loop(1, N_DP, lambda k: copy5(dp_peer(k)).start())
    xt[:, lanes((core * N_Y + y) * ROWS, ROWS)] = turned[dp]

    for copy in fetches[2:5]:
        copy.wait()
    lane_row = lax.broadcasted_iota(I32, (1, HD), 1)
    slots = jnp.zeros((1, HD), I32)
    for n in range(SLOTS):
        slots = jnp.where(lane_row == span[0, n], n, slots)
    slot_v[...] = slots
    slot_copy = pltpu.make_async_copy(slot_v, slot_of, local.at[9])
    slot_copy.start()
    mine = (span[0, 2 * me], span[0, 2 * me + 1])
    for s in range(2):
        own_rows = SPAN // 4
        row = lax.broadcasted_iota(I32, (own_rows, HD), 0)
        group = lax.broadcasted_iota(I32, (own_rows, HD), 1) >> 5
        at = pl.ds(BACK * SPAN, SPAN)
        rope_tables(mine[s] * SPAN + group * own_rows + row, lens, freq, cos.at[s, at], sin.at[s, at])
        row = lax.broadcasted_iota(I32, (SPAN, HD), 0)
        group = lax.broadcasted_iota(I32, (SPAN, HD), 1) >> 5
        pos = (mine[s] - BACK + (row >> 4)) * SPAN + group * PIECE + (row & 15)
        at = pl.ds(0, BACK * SPAN)
        rope_tables(pos, lens, freq, cos.at[s, at], sin.at[s, at])
    slot_copy.wait()
    settle(held[0].at[pl.ds(0, 2 * (N_CTX - 1))], send1.at[0])
    spread(1)

    def fill(slot):
        at = span[0, slot]
        for w in range(BACK):
            take[slot * BACK + w] = slot_of[0, jnp.maximum(at - BACK + w, 0)]
            later = at + 1 + w
            source = slot_of[0, jnp.minimum(later, SLOTS - 1)] * BACK + (BACK - 1 - w)
            give[slot * BACK + w] = jnp.where(later < SLOTS, source, N_CTX * REACH)

    loop(0, SLOTS, fill)
    for s in range(2):
        lane8 = lax.broadcasted_iota(I32, (8, HD), 1)
        qpos = mine[s] * SPAN + jnp.where(lane8 >= SPAN, lane8 - SPAN, lane8)
        qbegin = begin_of(qpos, lens)
        n = lax.broadcasted_iota(I32, (KEYS, HD), 0)
        r, w, t = n >> 6, (n >> 4) & 3, n & 15
        earlier = (mine[s] - BACK + w) * SPAN + r * PIECE + t
        kpos = jnp.where(n < BACK * SPAN, earlier, mine[s] * SPAN + (n - BACK * SPAN))
        allowed = (kpos <= qpos[0:1]) & (kpos >= qbegin[0:1])
        bias[s] = jnp.where(allowed, 0.0, MASKED)
    fetches[7].wait()

    def rotate(h):
        for s in range(2):
            rows = slice(s * SPAN, (s + 1) * SPAN)
            v = q[rows, lanes(h * HD, HD)].astype(F32)
            v = v * cos[s, BACK * SPAN :] + swap_halves(v) * sin[s, BACK * SPAN :]
            qrot[rows, lanes(h * HD, HD)] = v.astype(BF16)

    loop(0, KVH * G, rotate)
    empty = jnp.zeros((REACH, PIECE, HD), BF16)

    def clear(dz, dx):
        device = lax.rem(z + dz, N_Z) * N_X + lax.rem(x + dx, N_X)
        for side in landed:
            side[pl.ds(REACH * device, REACH)] = empty

    loop(0, 12, lambda k: clear(3 + k // N_X, lax.rem(k, N_X)))
    loop(0, 2, lambda k: clear(2, 2 * k + 1))
    loop(0, 2, lambda k: clear(6, 2 * k))
    for side in landed:
        side[N_CTX * REACH] = jnp.zeros((PIECE, HD), BF16)

    def choose(kind, s, k):
        device = reader(k)
        for w in range(BACK):
            chosen[kind, s, k, w] = held[kind][take[device * REACH + s * BACK + w]]

    def copy2(kind, s, k):
        return remote(
            chosen.at[kind, s, k], win.at[kind, s, piece_here], send2, recv2.at[s, lax.rem(k, N_X)], (dp, reader(k))
        )

    def hand_out(kind, s):
        def serve(k):
            n = k - N_X
            k = jnp.where(n < 0, k * N_X, lax.rem(n, N_ROW) * N_X + N_X - 1 - n // N_ROW)
            choose(kind, s, k)
            copy2(kind, s, k).start()

        loop(1, N_PIECE, serve)
        choose(kind, s, 0)
        win[kind, s, piece_here] = chosen[kind, s, 0]

    settle(held[0].at[pl.ds(0, 2 * (N_CTX - 1))], recv1.at[0])
    hand_out(0, 0)
    settle(held[1].at[pl.ds(0, 2 * (N_CTX - 1))], recv1.at[1])
    hand_out(1, 0)
    hand_out(0, 1)
    hand_out(1, 1)
    fetches[8].wait()

    def copy3(kind, s, k):
        return remote(
            part.at[kind, s, piece_of(holder(k))],
            landed[kind].at[pl.ds(REACH * me + BACK * s, BACK)],
            send3,
            recv3.at[kind],
            (dp, holder(k)),
        )

    def hand_over(kind, s, n, grad):
        j = lax.rem(x + n, KVH)
        earlier = grad[: BACK * SPAN].astype(BF16).reshape(N_ROW, BACK, PIECE, HD)
        for r in range(N_ROW):
            part[kind, s, r * KVH + j] = earlier[r]
        own[kind, s * SPAN : (s + 1) * SPAN, lanes(j * HD, HD)] = grad[BACK * SPAN :]

        def send(dz):
            at = dz * N_X + lax.rem(N_X - n, N_X)

            @pl.when(at > 0)
            def _():
                copy3(kind, s, at).start()

        loop(0, N_ROW, send)

    def stacked(ref, s, j):
        rows = slice(s * SPAN, (s + 1) * SPAN)
        return jnp.concatenate([ref[rows, lanes((j * G + g) * HD, HD)] for g in range(G)], axis=0)

    for s in range(2):

        def attend(n, s=s):
            j = lax.rem(x + n, KVH)

            def window(kind):
                parts = [win[kind, s, r * KVH + j].reshape(BACK * PIECE, HD) for r in range(N_ROW)]
                parts += [pack[kind, r * KVH + j, s] for r in range(N_ROW)]
                return jnp.concatenate(parts, axis=0)

            k, v = window(0).astype(F32), window(1)
            k = (k * cos[s] + swap_halves(k) * sin[s]).astype(BF16)
            qs, dos = stacked(qrot, s, j), stacked(do, s, j)
            mask = jnp.concatenate([bias[s]] * (G * SPAN // HD), axis=1)
            scores = lax.dot_general(k, qs, NT, preferred_element_type=F32)
            scores = scores * (SCALE * float(np.log2(np.e))) + mask
            weight = jnp.exp2(scores - jnp.max(scores, axis=0, keepdims=True))
            probs = weight * (1.0 / jnp.sum(weight, axis=0, keepdims=True))
            dprobs = lax.dot_general(v, dos, NT, preferred_element_type=F32)
            delta = jnp.sum(probs * dprobs, axis=0, keepdims=True)
            dscores = (probs * (dprobs - delta)).astype(BF16)
            low = probs.astype(BF16)
            hand_over(1, s, n, jnp.dot(low, dos, preferred_element_type=F32))
            kept_k[s, j] = k
            kept_ds[s, j] = dscores

        def key_part(n, s=s):
            j = lax.rem(x + n, KVH)
            dk = jnp.dot(kept_ds[s, j], stacked(qrot, s, j), preferred_element_type=F32)
            hand_over(0, s, n, dk * SCALE)

        def attend_next(n, s=s):
            settle(win.at[:, s, pl.ds(0, N_ROW)], recv2.at[s, N_X - n])
            attend(n)

        settle(win.at[:, s, pl.ds(0, N_ROW - 1)], recv2.at[s, 0])
        attend(0)
        loop(1, KVH, attend_next)
        loop(0, KVH, key_part)
        for kind in range(2):
            landed[kind][pl.ds(REACH * me + BACK * s, BACK)] = part[kind, s, piece_here]

    def query_grads(j):
        for s in range(2):
            rows = slice(s * SPAN, (s + 1) * SPAN)
            across_keys = lax.dot_general(kept_k[s, j], kept_ds[s, j], TN, preferred_element_type=F32)
            upright = across_keys.T * SCALE
            for g in range(G):
                u = upright[g * SPAN : (g + 1) * SPAN]
                u = u * cos[s, BACK * SPAN :] - swap_halves(u) * sin[s, BACK * SPAN :]
                dq[rows, lanes((j * G + g) * HD, HD)] = u.astype(BF16)

    loop(0, KVH, query_grads)
    dq_copy = pltpu.make_async_copy(dq, dq_h, local.at[10])
    dq_copy.start()

    def copy4(kind, src, owner, peer):
        return remote(
            total.at[kind, src], back.at[kind, owner], send4.at[kind], recv4.at[kind], (dp, peer)
        )

    def sum_up(kind, device):
        for s in range(2):
            at = (2 * device + s) * BACK
            acc = landed[kind][give[at]].astype(F32)
            for w in range(1, BACK):
                acc += landed[kind][give[at + w]].astype(F32)
            total[kind, device, s] = acc.astype(BF16)

    for kind in (1, 0):
        settle(landed[kind].at[pl.ds(0, REACH * (N_PIECE - 1))], recv3.at[kind])
        if kind == 0:
            settle(total.at[1, pl.ds(0, N_CTX - 1)], send4.at[1])

        def give_back(k, kind=kind):
            sum_up(kind, far_peer(k))
            copy4(kind, far_peer(k), me, far_peer(k)).start()

        loop(1, N_CTX, give_back)
        sum_up(kind, me)
        back[kind, me] = total[kind, me]

    def copy6(c, k):
        mine = grads.at[c, core, y]
        return remote(mine, mine, send6, recv6.at[c], (y_peer(k), me))

    def copy7(c):
        return remote(grads.at[c, core], grads.at[c, core], send7, recv7.at[c], (sib, me))

    def assemble(c):
        kind = c * HEADS // KVH
        for n in range(HEADS):
            j = (c * HEADS + n) % KVH
            for r in range(N_ROW):
                for s in range(2):
                    rows = slice(s * SPAN + r * PIECE, s * SPAN + (r + 1) * PIECE)
                    piece = r * KVH + j
                    g = back[kind, piece, s].astype(F32) + back[kind, N_PIECE + piece, s].astype(F32)
                    g += own[kind, rows, j * HD : (j + 1) * HD]
                    if kind == 0:
                        at = slice(BACK * SPAN + r * PIECE, BACK * SPAN + (r + 1) * PIECE)
                        g = g * cos[s, at] - swap_halves(g) * sin[s, at]
                    grads[c, core, y, rows, n * HD : (n + 1) * HD] = g.astype(BF16)
        loop(1, LINE, lambda k: copy6(c, far_step(k)).start())

    def forward(c):
        settle(grads.at[c, 0, pl.ds(0, LINE - 1)], recv6.at[c])
        copy7(c).start()

    def copy8(c, k):
        peer = x_peer(k)
        return remote(wsend.at[c, peer], wland.at[c, x], send8, recv8.at[c], (dp, z * N_X + peer))

    def copy9(c, peer):
        return remote(zsend.at[c, peer], zland.at[c, z], send9, recv9.at[c], (dp, peer * N_X + x))

    def multiply(c):
        settle(grads.at[c, 0], recv7.at[c])
        w = jnp.dot(xt[...], grads[c].reshape(N_DP * ROWS, W_COL), preferred_element_type=F32)
        wsend[c] = w.astype(BF16).reshape(LINE, W_X, W_COL)
        loop(1, LINE, lambda k: copy8(c, far_step(k)).start())
        wland[c, x] = wsend[c, x]

    def sum_line(c):
        settle(wland.at[c, pl.ds(0, LINE - 1)], recv8.at[c])
        acc = wland[c, 0].astype(F32)
        for n in range(1, LINE):
            acc += wland[c, n].astype(F32)
        pad = jnp.zeros((PIECE - W_DEV, W_COL), F32)
        for n in range(N_Z):
            block = jnp.concatenate([acc[n * W_DEV : (n + 1) * W_DEV], pad], axis=0)
            zsend[c, n] = block.astype(BF16)
        loop(1, N_Z, lambda k: copy9(c, z_peer(far_z(k))).start())
        zland[c, z] = zsend[c, z]

    def sum_z(c):
        settle(zland.at[c, pl.ds(0, N_Z - 1)], recv9.at[c])
        acc = zland[c, 0].astype(F32)
        for n in range(1, N_Z):
            acc += zland[c, n].astype(F32)
        out_ref[:, c * W_COL : (c + 1) * W_COL] = acc[:W_DEV]

    settle(xt.at[:, pl.ds(0, (N_DP - 1) * ROWS)], recv5)
    settle(back.at[1, pl.ds(0, N_CTX - 1)], recv4.at[1])
    values, keyed = range(CHUNKS // 2, CHUNKS), range(CHUNKS // 2)
    for c in values:
        assemble(c)
    settle(back.at[0, pl.ds(0, N_CTX - 1)], recv4.at[0])
    for c in keyed:
        assemble(c)
    for part_of in (values, keyed):
        for c in part_of:
            forward(c)
        for c in part_of:
            multiply(c)
    for c in (*values, *keyed):
        sum_line(c)
    for c in (*values, *keyed):
        sum_z(c)

    settle(held[1].at[pl.ds(0, 2 * (N_CTX - 1))], send1.at[1])
    settle(xt.at[:, pl.ds(0, (N_DP - 1) * ROWS)], send5)
    settle(chosen.at[:, :, pl.ds(0, N_PIECE - 1)], send2)
    settle(part.at[:, :, pl.ds(0, N_PIECE - 1)], send3)
    settle(total.at[0, pl.ds(0, N_CTX - 1)], send4.at[0])
    settle(grads.at[:, 0, pl.ds(0, LINE - 1)], send6)
    settle(grads.at[:, 0], send7)
    settle(wsend.at[:, pl.ds(0, LINE - 1)], send8)
    settle(zsend.at[:, pl.ds(0, N_Z - 1)], send9)
    dq_copy.wait()


def per_device(queries, keys, values, grad_out, inputs, span_map, doc_lengths):
    vmem, smem, dma = pltpu.VMEM, pltpu.SMEM, pltpu.SemaphoreType.DMA
    hbm = pl.BlockSpec(memory_space=pl.ANY)
    wide = KVH * G * HD
    tile = (PIECE, HD)
    return pl.pallas_call(
        kernel,
        out_shape=[
            jax.ShapeDtypeStruct((ROWS, wide), BF16),
            jax.ShapeDtypeStruct((W_DEV, 2 * KVC), F32),
        ],
        in_specs=[hbm] * 9,
        out_specs=[hbm, pl.BlockSpec(memory_space=pltpu.VMEM)],
        scratch_shapes=[
            smem((1, SLOTS), I32),
            smem((1, NDOC), I32),
            smem((1, HD), I32),
            smem((SLOTS * BACK,), I32),
            smem((SLOTS * BACK,), I32),
            vmem((1, HD), I32),
            vmem((1, HD), F32),
            vmem((W_DP, W_DP), BF16),
            vmem((ROWS, wide), BF16),
            vmem((ROWS, KVC), BF16),
            vmem((ROWS, KVC), BF16),
            vmem((ROWS, wide), BF16),
            vmem((ROWS, DW), BF16),
            vmem((2, KEYS, HD), F32),
            vmem((2, KEYS, HD), F32),
            vmem((2, KEYS, HD), F32),
            vmem((ROWS, wide), BF16),
            vmem((ROWS, wide), BF16),
            vmem((2, N_PIECE, 2) + tile, BF16),
            vmem((SLOTS,) + tile, BF16),
            vmem((SLOTS,) + tile, BF16),
            vmem((2, 2, N_PIECE, BACK) + tile, BF16),
            vmem((2, 2, N_PIECE, BACK) + tile, BF16),
            vmem((2, 2, N_PIECE, BACK) + tile, BF16),
            vmem((2, ROWS, KVC), F32),
            vmem((2, KVH, KEYS, HD), BF16),
            vmem((2, KVH, KEYS, G * SPAN), BF16),
            vmem((N_CTX * REACH + 1,) + tile, BF16),
            vmem((N_CTX * REACH + 1,) + tile, BF16),
            vmem((2, N_CTX, 2) + tile, BF16),
            vmem((2, N_CTX, 2) + tile, BF16),
            vmem((N_DP, W_DP, ROWS), BF16),
            vmem((W_DP, N_DP * ROWS), BF16),
            vmem((CHUNKS, 2, LINE, ROWS, W_COL), BF16),
            vmem((CHUNKS, N_X, W_X, W_COL), BF16),
            vmem((CHUNKS, N_X, W_X, W_COL), BF16),
            vmem((CHUNKS, N_Z, PIECE, W_COL), BF16),
            vmem((CHUNKS, N_Z, PIECE, W_COL), BF16),
            dma((11,)),
            dma((2,)), dma((2,)),
            dma, dma((2, N_X)),
            dma, dma((2,)),
            dma((2,)), dma((2,)),
            dma, dma,
            dma, dma((CHUNKS,)),
            dma, dma((CHUNKS,)),
            dma, dma((CHUNKS,)),
            dma, dma((CHUNKS,)),
        ],
        compiler_params=pltpu.CompilerParams(
            collective_id=0, has_side_effects=True, vmem_limit_bytes=VMEM_LIMIT
        ),
        name="packed_backward",
    )(
        span_map, doc_lengths, jnp.asarray(rope_lanes()), jnp.asarray(feature_order(), BF16),
        queries, keys, values, grad_out, inputs,
    )

def solution(mesh):
    rows = P(("dp", "ctx"), None)
    return jax.shard_map(
        per_device,
        mesh=mesh,
        in_specs=(rows, rows, rows, rows, rows, P("dp", None), P("dp", None)),
        out_specs=(rows, rows),
        check_vma=False,
    )
```
